32 devices in a mesh: dp: 8 (over y, x, core), fsdp: 4 (over z).
Axes of the slice: x: 2, y: 2, z: 4, core: 2. Of those that a mesh axis runs over, the one named last changes fastest.
Arguments:
- block_in: bfloat16 [64, 320, 1024], P(('dp', 'fsdp')), may hold values from -6 to 6
- keep_mask: int32 [64, 256], P(('dp', 'fsdp')), may hold values from 0 to 1, as said below
- out_cotangent: bfloat16 [64, 320, 1024], P(('dp', 'fsdp')), may hold values from -6 to 6
- norm1_gain: float32 [1024], P(('dp', 'fsdp')), may hold values from 0.1 to 1.9
- norm1_bias: float32 [1024], P(('dp', 'fsdp')), may hold values from -3 to 3
- qkv_weight: float32 [1024, 3072], P(('dp', 'fsdp')), may hold values from -0.1875 to 0.1875
- qv_bias: float32 [2048], P(('dp', 'fsdp')), may hold values from -3 to 3
- out_weight: float32 [1024, 1024], P(('dp', 'fsdp')), may hold values from -0.75 to 0.75
- out_bias: float32 [1024], P(('dp', 'fsdp')), may hold values from -3 to 3
- norm2_gain: float32 [1024], P(('dp', 'fsdp')), may hold values from 0.1 to 1.9
- norm2_bias: float32 [1024], P(('dp', 'fsdp')), may hold values from -3 to 3
- fc1_weight: float32 [1024, 4096], P(('dp', 'fsdp')), may hold values from -0.1875 to 0.1875
- fc1_bias: float32 [4096], P(('dp', 'fsdp')), may hold values from -3 to 3
- fc2_weight: float32 [4096, 1024], P(('dp', 'fsdp')), may hold values from -0.09375 to 0.09375
- fc2_bias: float32 [1024], P(('dp', 'fsdp')), may hold values from -3 to 3
Outputs:
- block_out: float32 [64, 320, 1024], P(('dp', 'fsdp'))
- input_grad: float32 [64, 320, 1024], P(('dp', 'fsdp'))
- norm1_gain_grad: float32 [1024], P(('dp', 'fsdp'))
- norm1_bias_grad: float32 [1024], P(('dp', 'fsdp'))
- qkv_weight_grad: float32 [1024, 3072], P(('dp', 'fsdp'))
- qv_bias_grad: float32 [2048], P(('dp', 'fsdp'))
- out_weight_grad: float32 [1024, 1024], P(('dp', 'fsdp'))
- out_bias_grad: float32 [1024], P(('dp', 'fsdp'))
- norm2_gain_grad: float32 [1024], P(('dp', 'fsdp'))
- norm2_bias_grad: float32 [1024], P(('dp', 'fsdp'))
- fc1_weight_grad: float32 [1024, 4096], P(('dp', 'fsdp'))
- fc1_bias_grad: float32 [4096], P(('dp', 'fsdp'))
- fc2_weight_grad: float32 [4096, 1024], P(('dp', 'fsdp'))
- fc2_bias_grad: float32 [1024], P(('dp', 'fsdp'))
The draws below stay inside these ranges and needn't reach their ends.
Inputs may be any that keep to these rules, and one draw needn't show every extreme that they name: `keep_mask`: each sequence keeps its image tokens at a rate of its own between 60 and 100 percent.
All inputs are finite; a program needn't handle non-finite values.
Results may differ from the reference program's by a relative error of at most 0.012.
The reference program's roundings to bfloat16 on the way count: a program that leaves them out, or rounds other values in their place, can miss the bound.
Values may be sent and summed in bfloat16 or wider, within the bound.
No kernel may reach another device: no remote copies, remote signals or barrier semaphores. Data moves between devices by JAX's collectives and lax.ppermute only.
A program may use at most 256 MiB of HBM per device.

```python
import math
import jax
import jax.numpy as jnp
from jax import lax

D = 1024
H = 16
HD = 64
FF = 4096
BUF = 64
IMG = 256
L = 320
SEQS = 64


def draw_keep_mask(key, part):
    key = jax.random.fold_in(key, 11)
    rate_key, pick_key = jax.random.split(key)
    rates = jax.random.randint(rate_key, (SEQS, 1), 60, 101)
    picks = jax.random.randint(pick_key, (SEQS, IMG), 0, 100)
    return (picks < rates).astype(jnp.int32)


def steps_of(stream_key, shape, cuts, smallest, top_value):
    def one(axis_at, shards_of):
        draws = jax.random.uniform(jax.random.fold_in(jax.random.fold_in(stream_key, 6), axis_at), (shards_of,), jnp.float32, smallest / len(cuts), top_value / len(cuts))
        return jnp.repeat(jnp.exp(draws), shape[axis_at] // shards_of).reshape((-1,) + (1,) * (len(shape) - axis_at - 1))

    factor_of = one(*cuts[0])
    for cut in cuts[1:]:
        factor_of = factor_of * one(*cut)
    return factor_of


def bell_draw(key, shape, width, reach, shards=(), held_as=jnp.bfloat16):
    factor_of = steps_of(key, shape, shards, -0.22, 0.18) if shards else 1.0
    drawn = jax.random.normal(key, shape, jnp.float32) * width * factor_of
    return jnp.minimum(jnp.maximum(drawn, -reach), reach).astype(held_as)


def setup_inputs(seed: int = 0) -> dict:
    arg_keys = jax.random.split(jax.random.key(seed), 16)
    return {
        "block_in": bell_draw(arg_keys[0], (SEQS, L, D), 1.0, 6.0, ((0, 32),)),
        "keep_mask": draw_keep_mask(jax.random.fold_in(arg_keys[15], 71), 0),
        "out_cotangent": bell_draw(arg_keys[2], (SEQS, L, D), 1.0, 6.0, ((0, 32),)),
        "norm1_gain": jnp.clip(1.0 + 0.18 * jax.random.normal(arg_keys[3], (D,), jnp.float32), 0.1, 1.9),
        "norm1_bias": bell_draw(arg_keys[4], (D,), 0.5, 3.0, ((0, 32),), jnp.float32),
        "qkv_weight": bell_draw(arg_keys[5], (D, 3 * D), D ** -0.5, 0.1875, ((0, 32),), jnp.float32),
        "qv_bias": bell_draw(arg_keys[6], (2 * D,), 0.5, 3.0, ((0, 32),), jnp.float32),
        "out_weight": bell_draw(arg_keys[7], (D, D), (D // 16) ** -0.5, 0.75, ((0, 32),), jnp.float32),
        "out_bias": bell_draw(arg_keys[8], (D,), 0.5, 3.0, ((0, 32),), jnp.float32),
        "norm2_gain": jnp.clip(1.0 + 0.18 * jax.random.normal(arg_keys[9], (D,), jnp.float32), 0.1, 1.9),
        "norm2_bias": bell_draw(arg_keys[10], (D,), 0.5, 3.0, ((0, 32),), jnp.float32),
        "fc1_weight": bell_draw(arg_keys[11], (D, FF), D ** -0.5, 0.1875, ((0, 32),), jnp.float32),
        "fc1_bias": bell_draw(arg_keys[12], (FF,), 0.5, 3.0, ((0, 32),), jnp.float32),
        "fc2_weight": bell_draw(arg_keys[13], (FF, D), FF ** -0.5, 0.09375, ((0, 32),), jnp.float32),
        "fc2_bias": bell_draw(arg_keys[14], (D,), 0.5, 3.0, ((0, 32),), jnp.float32),
    }


@jax.custom_vjp
def low(v):
    return lax.optimization_barrier(v.astype(jnp.bfloat16)).astype(jnp.float32)

@jax.custom_vjp
def low_back(v):
    return v

def low_keep(v):
    return (low(v), None)

def low_pass(kept, grad):
    return (grad,)

def back_keep(v):
    return (v, None)

def back_low(kept, grad):
    return (low(grad),)
low.defvjp(low_keep, low_pass)
low_back.defvjp(back_keep, back_low)
EPSILON = 1e-05
HIGHEST = lax.Precision.HIGHEST

def layer_norm(values, norm_gain, norm_bias):
    average = lax.optimization_barrier(jnp.mean(values, -1, keepdims=True))
    centered = values - average
    inverse = lax.rsqrt(lax.optimization_barrier(jnp.mean(centered * centered, -1, keepdims=True)) + EPSILON)
    return centered * inverse * norm_gain + norm_bias

def gelu_exact(values):
    return 0.5 * values * (1.0 + jax.scipy.special.erf(values * 0.7071067811865476))

def forward(params, inputs, keep_full):
    gain_one, bias_one, qkv_mat, qv_shift, out_mat, out_shift, gain_two, bias_two, up_mat, up_shift, down_mat, down_shift = [low(item) for item in params]
    groups = inputs.shape[0]
    length = inputs.shape[1]
    scale = 1.0 / math.sqrt(HD)
    normed_one = low(layer_norm(inputs, gain_one, bias_one))
    project = jnp.einsum('gld,de->gle', normed_one, qkv_mat, precision=HIGHEST)
    queries = low_back(low(project[..., :D] + qv_shift[:D])).reshape(groups, length, H, HD)
    keys_all = low_back(low(project[..., D:2 * D])).reshape(groups, length, H, HD)
    values_all = low_back(low(project[..., 2 * D:] + qv_shift[D:])).reshape(groups, length, H, HD)
    logits = jnp.einsum('gqhe,gkhe->ghqk', queries, keys_all, precision=HIGHEST) * scale
    visible = keep_full[:, None, None, :] > 0
    logits = jnp.where(visible, low_back(logits), -1000000000.0)
    top_score = lax.optimization_barrier(jnp.max(logits, -1, keepdims=True))
    expo = jnp.exp(logits - top_score)
    probs = expo / lax.optimization_barrier(jnp.sum(expo, -1, keepdims=True))
    mixed = jnp.einsum('ghqk,gkhe->gqhe', low(probs), values_all, precision=HIGHEST).reshape(groups, length, D)
    mixed = low_back(low(mixed))
    branch = low_back(jnp.einsum('gld,de->gle', mixed, out_mat, precision=HIGHEST) + out_shift)
    middle = inputs + branch
    normed_two = low(layer_norm(middle, gain_two, bias_two))
    hidden_pre = low_back(jnp.einsum('gld,df->glf', normed_two, up_mat, precision=HIGHEST) + up_shift)
    hidden = low(gelu_exact(hidden_pre))
    feed = low_back(jnp.einsum('glf,fd->gld', hidden, down_mat, precision=HIGHEST) + down_shift)
    return keep_full.astype(jnp.float32)[..., None] * (middle + feed)

def reference(block_in, keep_mask, out_cotangent, norm1_gain, norm1_bias, qkv_weight, qv_bias, out_weight, out_bias, norm2_gain, norm2_bias, fc1_weight, fc1_bias, fc2_weight, fc2_bias):
    params = (norm1_gain, norm1_bias, qkv_weight, qv_bias, out_weight, out_bias, norm2_gain, norm2_bias, fc1_weight, fc1_bias, fc2_weight, fc2_bias)
    seq_count = block_in.shape[0]
    per_group = 8
    group_count = seq_count // per_group
    keep_full = jnp.concatenate([jnp.ones((seq_count, BUF), jnp.int32), keep_mask.astype(jnp.int32)], axis=1)
    inputs = block_in.astype(jnp.float32).reshape(group_count, per_group, L, D)
    cotan = out_cotangent.astype(jnp.float32).reshape(group_count, per_group, L, D)
    keep_groups = keep_full.reshape(group_count, per_group, L)

    def one_group(totals, pieces):
        block_x, block_keep, block_cot = pieces
        outputs, pullback = jax.vjp(lambda weights, values: forward(weights, values, block_keep), params, block_x)
        grad_params, grad_inputs = pullback(block_cot)
        return (tuple((left + right for left, right in zip(totals, grad_params))), (outputs, grad_inputs))
    starting = tuple((jnp.zeros(item.shape, jnp.float32) for item in params))
    totals, (outputs, grad_inputs) = lax.scan(one_group, starting, (inputs, keep_groups, cotan))
    return (outputs.reshape(seq_count, L, D), grad_inputs.reshape(seq_count, L, D), totals[0], totals[1], totals[2], totals[3], totals[4], totals[5], totals[6], totals[7], totals[8], totals[9], totals[10], totals[11])
```

```python
import functools
import math

import jax
import jax.numpy as jnp
from jax import lax
from jax.experimental import pallas as pl
from jax.experimental.pallas import tpu as pltpu
from jax.sharding import PartitionSpec as P

HD = 64
EPSILON = 1e-05
AXES = ("dp", "fsdp")
bf16 = jnp.bfloat16
f32 = jnp.float32
NN = (((1,), (0,)), ((), ()))
NT = (((1,), (1,)), ((), ()))
TN = (((0,), (0,)), ((), ()))


def dot(left, right, dims=NN):
    return lax.dot_general(left, right, dims, preferred_element_type=f32)


def attention_forward_kernel(seqs, length, keep_ref, q_ref, k_ref, v_ref, o_ref):
    scale = 1.0 / math.sqrt(HD)
    for s in range(seqs):
        rows = slice(s * length, (s + 1) * length)
        visible = keep_ref[s] > 0
        mixed = []
        for h in range(128 // HD):
            cols = slice(h * HD, (h + 1) * HD)
            logits = dot(k_ref[rows, cols], q_ref[rows, cols] * scale, NT)
            logits = jnp.where(visible, logits, -1e9)
            raised = jnp.exp(logits - jnp.max(logits, 0, keepdims=True))
            probs = raised * (1.0 / jnp.sum(raised, 0, keepdims=True))
            mixed.append(dot(probs.astype(bf16), v_ref[rows, cols], TN))
        o_ref[rows, :] = jnp.concatenate(mixed, 1).astype(bf16)


def attention_backward_kernel(
    seqs, length, keep_ref, q_ref, k_ref, v_ref, do_ref, dq_ref, dk_ref, dv_ref, sq_ref, sv_ref
):
    scale = 1.0 / math.sqrt(HD)
    sum_q = jnp.zeros((1, 128), f32)
    sum_v = jnp.zeros((1, 128), f32)
    for s in range(seqs):
        rows = slice(s * length, (s + 1) * length)
        visible = keep_ref[s] > 0
        dqs, dks, dvs = [], [], []
        for h in range(128 // HD):
            cols = slice(h * HD, (h + 1) * HD)
            queries = q_ref[rows, cols] * scale
            keys = k_ref[rows, cols]
            grad_mixed = do_ref[rows, cols]
            logits = dot(keys, queries, NT)
            grad_probs = dot(v_ref[rows, cols], grad_mixed, NT)
            logits = jnp.where(visible, logits, -1e9)
            raised = jnp.exp(logits - jnp.max(logits, 0, keepdims=True))
            probs = raised * (1.0 / jnp.sum(raised, 0, keepdims=True))
            dvs.append(dot(probs.astype(bf16), grad_mixed))
            row_terms = jnp.sum(grad_probs * probs, 0, keepdims=True)
            grad_logits = (probs * (grad_probs - row_terms)).astype(bf16)
            dks.append(dot(grad_logits, queries))
            dqs.append(dot(grad_logits, keys, TN) * scale)
        dq = jnp.concatenate(dqs, 1).astype(bf16)
        dv = jnp.concatenate(dvs, 1).astype(bf16)
        dq_ref[rows, :] = dq
        dk_ref[rows, :] = jnp.concatenate(dks, 1).astype(bf16)
        dv_ref[rows, :] = dv
        sum_q += jnp.sum(dq.astype(f32), 0, keepdims=True)
        sum_v += jnp.sum(dv.astype(f32), 0, keepdims=True)
    sq_ref[...] = sum_q
    sv_ref[...] = sum_v


def attention_forward(keep, q, k, v):
    seqs, length = keep.shape[:2]
    rows, width = q.shape
    block = pl.BlockSpec((rows, 128), lambda i: (0, i))
    return pl.pallas_call(
        functools.partial(attention_forward_kernel, seqs, length),
        grid=(width // 128,),
        in_specs=[pl.BlockSpec((seqs, length, 1), lambda i: (0, 0, 0))] + [block] * 3,
        out_specs=block,
        out_shape=jax.ShapeDtypeStruct((rows, width), bf16),
        compiler_params=pltpu.CompilerParams(vmem_limit_bytes=40 << 20),
        cost_estimate=pl.CostEstimate(
            flops=16 * rows * length * width, bytes_accessed=8 * rows * width, transcendentals=0
        ),
    )(keep, q, k, v)


def attention_backward(keep, q, k, v, grad_mixed):
    seqs, length = keep.shape[:2]
    rows, width = q.shape
    block = pl.BlockSpec((rows, 128), lambda i: (0, i))
    vector = pl.BlockSpec((1, 128), lambda i: (0, i))
    low = jax.ShapeDtypeStruct((rows, width), bf16)
    sums = jax.ShapeDtypeStruct((1, width), f32)
    return pl.pallas_call(
        functools.partial(attention_backward_kernel, seqs, length),
        grid=(width // 128,),
        in_specs=[pl.BlockSpec((seqs, length, 1), lambda i: (0, 0, 0))] + [block] * 4,
        out_specs=[block] * 3 + [vector] * 2,
        out_shape=[low] * 3 + [sums] * 2,
        compiler_params=pltpu.CompilerParams(vmem_limit_bytes=40 << 20),
        cost_estimate=pl.CostEstimate(
            flops=24 * rows * length * width, bytes_accessed=14 * rows * width, transcendentals=0
        ),
    )(keep, q, k, v, grad_mixed)


def norm_forward(values, norm_gain, norm_bias):
    average = jnp.mean(values, -1, keepdims=True)
    centered = values - average
    inverse = lax.rsqrt(jnp.mean(centered * centered, -1, keepdims=True) + EPSILON)
    normed = centered * inverse
    return (normed * norm_gain + norm_bias, normed, inverse)


def norm_backward(grad_norm, normed, inverse, norm_gain):
    scaled = grad_norm * norm_gain
    return inverse * (
        scaled
        - jnp.mean(scaled, -1, keepdims=True)
        - normed * jnp.mean(scaled * normed, -1, keepdims=True)
    )


class Exchange:
    def __init__(self, dp_size):
        self.size = dp_size
        bits = [1 << i for i in range(dp_size.bit_length() - 1)]
        self.paths = (bits[:1] + bits[1:][::-1], bits)
        self.me = lax.axis_index("dp")

    def swap(self, value, bit):
        return lax.ppermute(value, "dp", [(i, i ^ bit) for i in range(self.size)])

    def order(self, path):
        count = len(path)
        return [
            sum(bit for at, bit in enumerate(path) if place >> (count - 1 - at) & 1)
            for place in range(self.size)
        ]

    def relative(self, value, path):
        width = value.shape[1] // self.size
        rows = value.shape[0]
        return jnp.concatenate(
            [
                lax.dynamic_slice(value, (0, (self.me ^ r) * width), (rows, width))
                for r in self.order(path)
            ],
            1,
        )

    def weight_grad(self, left, right):
        half = right.shape[1] // 2
        parts = []
        for path, right_part in zip(self.paths, (right[:, :half], right[:, half:])):
            ordered = self.relative(left, path)
            arrived = []

            def rows_of(first, last):
                total = dot(ordered[:, first:last], right_part, TN)
                for piece in arrived:
                    total = total + piece[first:last].astype(f32)
                return total.astype(bf16)

            rest = left.shape[1]
            for bit in path:
                sent = rows_of(rest // 2, rest)
                arrived.append(self.swap(sent, bit))
                rest //= 2
            parts.append(rows_of(0, rest))
        own = lax.psum_scatter(
            jnp.concatenate(parts, 1), "fsdp", scatter_dimension=0, tiled=True
        )
        return own.astype(f32)


def local(dp_size, device_count, block_in, keep_mask, out_cotangent, *params):
    (g1, b1, qkv_weight, qv_bias, out_weight, out_bias, g2, b2, up_weight, up_bias, down_weight, down_bias) = params
    seqs, length, width = block_in.shape
    rows = seqs * length
    exchange = Exchange(dp_size)

    vectors = (g1, b1, qv_bias, out_bias, g2, b2, up_bias, down_bias)
    sizes = [v.shape[0] for v in vectors]
    cuts = [sum(sizes[:i]) for i in range(1, len(sizes))]
    packed = lax.all_gather(jnp.concatenate([v.astype(bf16) for v in vectors]), AXES, axis=0, tiled=False)
    g1, b1, qv_bias, out_bias, g2, b2, up_bias, down_bias = (
        part.reshape(-1).astype(f32) for part in jnp.split(packed, cuts, axis=1)
    )
    qkv_mat, out_mat, up_mat, down_mat = (
        lax.all_gather(w.astype(bf16), AXES, axis=0, tiled=True)
        for w in (qkv_weight, out_weight, up_weight, down_weight)
    )

    keep = jnp.concatenate(
        [jnp.ones((seqs, length - keep_mask.shape[1]), jnp.int32), keep_mask], axis=1
    )
    keep_rows = keep.reshape(rows, 1).astype(f32)
    keep_column = keep.reshape(seqs, length, 1)
    inputs = block_in.astype(f32).reshape(rows, width)
    grad_out = out_cotangent.astype(f32).reshape(rows, width) * keep_rows
    grad_feed = grad_out.astype(bf16)
    down_bias_grad = jnp.sum(grad_feed.astype(f32), 0)

    normed_one, plain_one, inverse_one = norm_forward(inputs, g1, b1)
    act_one = normed_one.astype(bf16)
    queries = (dot(act_one, qkv_mat[:, :width]) + qv_bias[:width]).astype(bf16)
    keys = dot(act_one, qkv_mat[:, width : 2 * width]).astype(bf16)
    values = (dot(act_one, qkv_mat[:, 2 * width :]) + qv_bias[width:]).astype(bf16)
    mixed = attention_forward(keep_column, queries, keys, values)
    middle = inputs + dot(mixed, out_mat) + out_bias
    normed_two, plain_two, inverse_two = norm_forward(middle, g2, b2)
    act_two = normed_two.astype(bf16)
    pre = dot(act_two, up_mat) + up_bias
    cumul = 0.5 * (1.0 + lax.erf(pre * 0.7071067811865476))
    hidden = (pre * cumul).astype(bf16)
    slope = cumul + pre * jnp.exp(-0.5 * pre * pre) * 0.3989422804014327
    hidden, slope = lax.optimization_barrier((hidden, slope))

    down_grad = exchange.weight_grad(hidden, grad_feed)
    grad_pre = (dot(grad_feed, down_mat, NT) * slope).astype(bf16)
    up_bias_grad = jnp.sum(grad_pre.astype(f32), 0)
    up_grad = exchange.weight_grad(act_two, grad_pre)
    grad_act_two = dot(grad_pre, up_mat, NT)
    gain_two_grad = jnp.sum(grad_act_two * plain_two, 0)
    bias_two_grad = jnp.sum(grad_act_two, 0)
    grad_middle = grad_out + norm_backward(grad_act_two, plain_two, inverse_two, g2)
    grad_branch = grad_middle.astype(bf16)
    out_bias_grad = jnp.sum(grad_branch.astype(f32), 0)
    out_grad = exchange.weight_grad(mixed, grad_branch)
    grad_mixed = dot(grad_branch, out_mat, NT).astype(bf16)
    dq, dk, dv, sum_q, sum_v = attention_backward(keep_column, queries, keys, values, grad_mixed)
    grad_project = jnp.concatenate([dq, dk, dv], 1)
    qkv_grad = exchange.weight_grad(act_one, grad_project)
    grad_act_one = dot(grad_project, qkv_mat, NT)
    gain_one_grad = jnp.sum(grad_act_one * plain_one, 0)
    bias_one_grad = jnp.sum(grad_act_one, 0)
    input_grad = grad_middle + norm_backward(grad_act_one, plain_one, inverse_one, g1)

    feed = dot(hidden, down_mat) + down_bias
    block_out = keep_rows * (middle + feed)

    grads = (
        gain_one_grad,
        bias_one_grad,
        jnp.concatenate([sum_q.reshape(-1), sum_v.reshape(-1)]),
        out_bias_grad,
        gain_two_grad,
        bias_two_grad,
        up_bias_grad,
        down_bias_grad,
    )
    packed_grads = jnp.concatenate([g.reshape(device_count, -1) for g in grads], 1)
    summed = lax.psum_scatter(packed_grads, AXES, scatter_dimension=0, tiled=False)
    v = jnp.split(summed, cuts)
    return (
        block_out.reshape(seqs, length, width),
        input_grad.reshape(seqs, length, width),
        v[0],
        v[1],
        qkv_grad,
        v[2],
        out_grad,
        v[3],
        v[4],
        v[5],
        up_grad,
        v[6],
        down_grad,
        v[7],
    )


def solution(mesh):
    dp_size = mesh.shape["dp"]
    row = P(AXES, None)
    vec = P(AXES)
    cube = P(AXES, None, None)
    return jax.shard_map(
        functools.partial(local, dp_size, dp_size * mesh.shape["fsdp"]),
        mesh=mesh,
        in_specs=(cube, row, cube, vec, vec, row, vec, row, vec, vec, vec, row, vec, row, vec),
        out_specs=(cube, cube, vec, vec, row, vec, row, vec, vec, vec, row, vec, row, vec),
        check_vma=False,
    )
```

```python
import functools
import math

import jax
import jax.numpy as jnp
from jax import lax
from jax.experimental import pallas as pl
from jax.experimental.pallas import tpu as pltpu
from jax.sharding import PartitionSpec as P

HD = 64
EPSILON = 1e-05
AXES = ("dp", "fsdp")
bf16 = jnp.bfloat16
f32 = jnp.float32
NN = (((1,), (0,)), ((), ()))
NT = (((1,), (1,)), ((), ()))
TN = (((0,), (0,)), ((), ()))


def dot(left, right, dims=NN):
    return lax.dot_general(left, right, dims, preferred_element_type=f32)


def attention_forward_kernel(seqs, length, keep_ref, q_ref, k_ref, v_ref, o_ref):
    scale = 1.0 / math.sqrt(HD)
    for s in range(seqs):
        rows = slice(s * length, (s + 1) * length)
        visible = keep_ref[s] > 0
        mixed = []
        for h in range(128 // HD):
            cols = slice(h * HD, (h + 1) * HD)
            logits = dot(k_ref[rows, cols], q_ref[rows, cols] * scale, NT)
            logits = jnp.where(visible, logits, -1e9)
            raised = jnp.exp(logits - jnp.max(logits, 0, keepdims=True))
            probs = raised * (1.0 / jnp.sum(raised, 0, keepdims=True))
            mixed.append(dot(probs.astype(bf16), v_ref[rows, cols], TN))
        o_ref[rows, :] = jnp.concatenate(mixed, 1).astype(bf16)


def attention_backward_kernel(
    seqs, length, keep_ref, q_ref, k_ref, v_ref, do_ref, above_ref, dp_ref, sq_ref, sv_ref
):
    scale = 1.0 / math.sqrt(HD)
    sum_q = jnp.zeros((1, 128), f32)
    sum_v = jnp.zeros((1, 128), f32)
    for s in range(seqs):
        rows = slice(s * length, (s + 1) * length)
        visible = keep_ref[s] > 0
        dqs, dks, dvs = [], [], []
        for h in range(128 // HD):
            cols = slice(h * HD, (h + 1) * HD)
            queries = q_ref[rows, cols] * scale
            keys = k_ref[rows, cols]
            grad_mixed = do_ref[rows, cols]
            logits = dot(keys, queries, NT)
            grad_probs = dot(v_ref[rows, cols], grad_mixed, NT)
            logits = jnp.where(visible, logits, -1e9)
            raised = jnp.exp(logits - jnp.max(logits, 0, keepdims=True))
            probs = raised * (1.0 / jnp.sum(raised, 0, keepdims=True))
            dvs.append(dot(probs.astype(bf16), grad_mixed))
            row_terms = jnp.sum(grad_probs * probs, 0, keepdims=True)
            grad_logits = (probs * (grad_probs - row_terms)).astype(bf16)
            dks.append(dot(grad_logits, queries))
            dqs.append(dot(grad_logits, keys, TN) * scale)
        dq = jnp.concatenate(dqs, 1).astype(bf16)
        dv = jnp.concatenate(dvs, 1).astype(bf16)
        dp_ref[0, rows, :] = dq
        dp_ref[1, rows, :] = jnp.concatenate(dks, 1).astype(bf16)
        dp_ref[2, rows, :] = dv
        sum_q += jnp.sum(dq.astype(f32), 0, keepdims=True)
        sum_v += jnp.sum(dv.astype(f32), 0, keepdims=True)
    dp_ref[3] = above_ref[...]
    sq_ref[...] = sum_q
    sv_ref[...] = sum_v


def attention_forward(keep, project, part):
    seqs, length = keep.shape[:2]
    rows, width = project.shape[0], project.shape[1] // 6
    steps = width // 128
    block = pl.BlockSpec((rows, 128), lambda i: (0, i))
    return pl.pallas_call(
        functools.partial(attention_forward_kernel, seqs, length),
        grid=(steps,),
        in_specs=[pl.BlockSpec((seqs, length, 1), lambda i: (0, 0, 0))]
        + [
            pl.BlockSpec((rows, 128), lambda i, at=at: (0, i + (2 * at + part) * steps))
            for at in range(3)
        ],
        out_specs=block,
        out_shape=jax.ShapeDtypeStruct((rows, width), bf16),
        compiler_params=pltpu.CompilerParams(vmem_limit_bytes=16 << 20),
        cost_estimate=pl.CostEstimate(flops=int(8.5 * COST), bytes_accessed=1, transcendentals=0),
    )(keep, project, project, project)


def attention_backward(keep, project, grad_mixed, above):
    seqs, length = keep.shape[:2]
    rows, width = project.shape[0], project.shape[1] // 3
    steps = width // 128
    block = pl.BlockSpec((rows, 128), lambda i: (0, i))
    vector = pl.BlockSpec((1, 128), lambda i: (0, i))
    sums = jax.ShapeDtypeStruct((1, width), f32)
    return pl.pallas_call(
        functools.partial(attention_backward_kernel, seqs, length),
        grid=(steps,),
        in_specs=[pl.BlockSpec((seqs, length, 1), lambda i: (0, 0, 0))]
        + [pl.BlockSpec((rows, 128), lambda i, at=at: (0, i + at * steps)) for at in range(3)]
        + [block] * 2,
        out_specs=[pl.BlockSpec((4, rows, 128), lambda i: (0, 0, i)), vector, vector],
        out_shape=[jax.ShapeDtypeStruct((4, rows, width), bf16), sums, sums],
        compiler_params=pltpu.CompilerParams(vmem_limit_bytes=16 << 20),
        cost_estimate=pl.CostEstimate(flops=int(22 * COST), bytes_accessed=1, transcendentals=0),
    )(keep, project, project, project, grad_mixed, above)


def norm_forward(values, norm_gain, norm_bias):
    average = jnp.mean(values, -1, keepdims=True)
    centered = values - average
    inverse = lax.rsqrt(jnp.mean(centered * centered, -1, keepdims=True) + EPSILON)
    normed = centered * inverse
    return (normed * norm_gain + norm_bias, normed, inverse)


def norm_backward(grad_norm, normed, inverse, norm_gain):
    scaled = grad_norm * norm_gain
    return inverse * (
        scaled
        - jnp.mean(scaled, -1, keepdims=True)
        - normed * jnp.mean(scaled * normed, -1, keepdims=True)
    )


def gathered(device_count, block_in, keep_mask, out_cotangent, *params):
    (g1, b1, qkv_weight, qv_bias, out_weight, out_bias, g2, b2, up_weight, up_bias, down_weight, down_bias) = params
    seqs, length, width = block_in.shape
    rows = seqs * length
    vectors = (g1, b1, qv_bias, out_bias, g2, b2, up_bias, down_bias)
    sizes = [v.shape[0] for v in vectors]
    cuts = [sum(sizes[:i]) for i in range(1, len(sizes))]
    packed = lax.all_gather(jnp.concatenate(vectors).astype(bf16), AXES, axis=0, tiled=False)
    g1, b1, qv_bias, out_bias, g2, b2, up_bias, down_bias = (
        part.reshape(-1).astype(f32) for part in jnp.split(packed, cuts, axis=1)
    )
    qkv_mat, out_mat, up_mat, down_mat = (
        lax.all_gather(w.astype(bf16), AXES, axis=0, tiled=True)
        for w in (qkv_weight, out_weight, up_weight, down_weight)
    )
    keep = jnp.concatenate(
        [jnp.ones((seqs, length - keep_mask.shape[1]), jnp.int32), keep_mask], axis=1
    )
    keep_rows = keep.reshape(rows, 1).astype(f32)
    keep_column = keep.reshape(seqs, length, 1)
    inputs = block_in.astype(f32).reshape(rows, width)
    grad_out = out_cotangent.astype(f32).reshape(rows, width) * keep_rows
    grad_feed = grad_out.astype(bf16)

    normed_one, plain_one, inverse_one = norm_forward(inputs, g1, b1)
    act_one = normed_one.astype(bf16)
    zeros = jnp.zeros((width,), f32)
    shift = jnp.concatenate([qv_bias[:width], zeros, qv_bias[width:]])
    project = (dot(act_one, qkv_mat) + shift).astype(bf16)

    mixed = jnp.concatenate([attention_forward(keep_column, project, part) for part in range(2)], 1)
    middle = inputs + dot(mixed, out_mat) + out_bias
    normed_two, plain_two, inverse_two = norm_forward(middle, g2, b2)
    act_two = normed_two.astype(bf16)
    pre = dot(act_two, up_mat) + up_bias
    cumul = 0.5 * (1.0 + lax.erf(pre * 0.7071067811865476))
    hidden = (pre * cumul).astype(bf16)
    slope = cumul + pre * jnp.exp(-0.5 * pre * pre) * 0.3989422804014327
    feed = dot(hidden, down_mat) + down_bias
    block_out = keep_rows * (middle + feed)

    grad_pre = (dot(grad_feed, down_mat, NT) * slope).astype(bf16)
    grad_act_two = dot(grad_pre, up_mat, NT)
    grad_middle = grad_out + norm_backward(grad_act_two, plain_two, inverse_two, g2)
    grad_branch = grad_middle.astype(bf16)
    grad_mixed = dot(grad_branch, out_mat, NT).astype(bf16)
    grad_parts, sum_q, sum_v = attention_backward(keep_column, project, grad_mixed, grad_branch)
    grad_project = jnp.concatenate([grad_parts[i] for i in range(3)], 1)
    grad_act_one = dot(grad_project, qkv_mat, NT)
    input_grad = grad_middle + norm_backward(grad_act_one, plain_one, inverse_one, g1)
    grads = (
        jnp.sum(grad_act_one * plain_one, 0),
        jnp.sum(grad_act_one, 0),
        jnp.concatenate([sum_q[0], sum_v[0]]),
        jnp.sum(grad_branch.astype(f32), 0),
        jnp.sum(grad_act_two * plain_two, 0),
        jnp.sum(grad_act_two, 0),
        jnp.sum(grad_pre.astype(f32), 0),
        jnp.sum(grad_feed.astype(f32), 0),
    )
    shares = jnp.concatenate([g.reshape(device_count, -1) for g in grads], 1)
    v = jnp.split(lax.psum_scatter(shares, AXES, scatter_dimension=0, tiled=False), cuts)

    def to_owner(left, right):
        total = dot(left, right, TN).astype(bf16)
        return lax.psum_scatter(total, AXES, scatter_dimension=0, tiled=True).astype(f32)

    return (
        block_out.reshape(seqs, length, width),
        input_grad.reshape(seqs, length, width),
        v[0],
        v[1],
        to_owner(act_one, grad_project),
        v[2],
        to_owner(mixed, grad_branch),
        v[3],
        v[4],
        v[5],
        to_owner(act_two, grad_pre),
        v[6],
        to_owner(hidden, grad_feed),
        v[7],
    )


CORE, XBIT, YBIT = 1, 2, 4
BLOCKS = [c * CORE + y * YBIT + x * XBIT for c in range(2) for y in range(2) for x in range(2)]
COST = 1e12


def positions(me, line, count):
    true = [me ^ r for r in BLOCKS]
    place = [
        sum(jnp.where((me ^ d) == r, at, 0) for at, r in enumerate(BLOCKS)) for d in range(8)
    ]
    ahead = [(line + by) % count for by in range(count)]
    return jnp.stack(true + place + ahead).astype(jnp.int32)


def call(kernel, grid, where, ins, outs, scratch=(), micros=3):
    held = 6 << 20
    specs = []
    for array, block, index in ins:
        once = tuple(block) == tuple(array.shape)
        size = math.prod(n or 1 for n in block) * array.dtype.itemsize
        held += size if once else 2 * size
        specs.append(pl.BlockSpec(block, index, pipeline_mode=pl.Buffered(1) if once else None))
    for _, dtype, block, _ in outs:
        held += 2 * math.prod(block) * jnp.dtype(dtype).itemsize
    for buffer in scratch:
        held += math.prod(buffer.shape) * jnp.dtype(buffer.dtype).itemsize
    return pl.pallas_call(
        kernel,
        grid_spec=pltpu.PrefetchScalarGridSpec(
            num_scalar_prefetch=1,
            grid=grid,
            in_specs=specs,
            out_specs=[pl.BlockSpec(block, index) for _, _, block, index in outs],
            scratch_shapes=list(scratch),
        ),
        out_shape=[jax.ShapeDtypeStruct(shape, dtype) for shape, dtype, _, _ in outs],
        compiler_params=pltpu.CompilerParams(vmem_limit_bytes=held),
        cost_estimate=pl.CostEstimate(flops=int(micros * COST), bytes_accessed=1, transcendentals=0),
    )(where, *[array for array, _, _ in ins])


def whole(array):
    return (array, array.shape, lambda *_: (0,) * array.ndim)


def whole_out(shape, dtype):
    return (shape, dtype, shape, lambda *_: (0,) * len(shape))


def column(i, *_):
    return (0, i)


def lanes(where, at):
    return pl.ds(pl.multiple_of(where[at] * 128, 128), 128)


def deal(where, source, low, high):
    for at in range(4):
        cols = slice(at * 128, (at + 1) * 128)
        low[:, cols] = source[:, lanes(where, at)]
        high[:, cols] = source[:, lanes(where, 4 + at)]


def normalize(values):
    centered = values - jnp.mean(values, -1, keepdims=True)
    inverse = lax.rsqrt(jnp.mean(centered * centered, -1, keepdims=True) + EPSILON)
    return centered * inverse, inverse


def norm_kernel(where, x_ref, grad_ref, gain_ref, bias_ref, low_ref, pack_ref, whole_ref):
    normed, _ = normalize(x_ref[...].astype(f32))
    whole_ref[...] = (normed * gain_ref[...] + bias_ref[...]).astype(bf16)
    half = low_ref.shape[1]
    deal(where, whole_ref, low_ref, pack_ref.at[:, :half])
    pack_ref[:, half:] = grad_ref[...]


def norm_one(where, inputs, grad_feed, gain, bias):
    rows, width = inputs.shape
    index = lambda i, _: (i, 0)
    return call(
        norm_kernel,
        (rows // 128,),
        where,
        [(inputs, (128, width), index), (grad_feed, (128, width), index), whole(gain), whole(bias)],
        [
            ((rows, width // 2), bf16, (128, width // 2), index),
            ((rows, width // 2 + width), bf16, (128, width // 2 + width), index),
        ],
        [pltpu.VMEM((128, width), bf16)],
    )


def project_kernel(where, low_ref, high_ref, mat_low, mat_high, bias_ref, out_ref):
    total = dot(low_ref[...], mat_low[...]) + dot(high_ref[...], mat_high[...])
    out_ref[...] = (total + bias_ref[...]).astype(bf16)


def project(where, low, pack, mats, bias):
    rows, depth = low.shape
    columns = bias.shape[1]
    tile = ((depth, 512), column)
    return call(
        project_kernel,
        (columns // 512,),
        where,
        [whole(low), first_columns(pack, depth), (mats[0], *tile), (mats[1], *tile), (bias, (1, 512), column)],
        [((rows, columns), bf16, (rows, 512), column)], micros=8)[0]


def branch_kernel(
    where, mixed_ref, x_ref, mat_low, mat_high, shift_ref, gain_ref, bias_ref,
    mix_low, middle_ref, two_low, pack_ref, whole_ref,
):
    half = mix_low.shape[1]
    mix_high, two_high = pack_ref.at[:, :half], pack_ref.at[:, half:]
    deal(where, mixed_ref, mix_low, mix_high)
    total = dot(mix_low[...], mat_low[...]) + dot(mix_high[...], mat_high[...])
    middle = x_ref[...].astype(f32) + total + shift_ref[...]
    middle_ref[...] = middle
    normed, _ = normalize(middle)
    whole_ref[...] = (normed * gain_ref[...] + bias_ref[...]).astype(bf16)
    deal(where, whole_ref, two_low, two_high)


def branch_norm(where, mixed, inputs, mats, shift, gain, bias, length):
    rows, width = inputs.shape
    block = ((length, width), lambda i, _: (i, 0))
    part = ((rows, width // 2), bf16, (length, width // 2), lambda i, _: (i, 0))
    return call(
        branch_kernel,
        (rows // length,),
        where,
        [(mixed, *block), (inputs, *block), *[last_columns(m, width) for m in mats]]
        + [whole(v) for v in (shift, gain, bias)],
        [part, ((rows, width), f32, *block), part, ((rows, width), bf16, *block)],
        [pltpu.VMEM((length, width), bf16)], micros=4)


def first_columns(mat, count, at=0):
    return (mat, (mat.shape[0], count), lambda *_: (0, at))


def last_columns(mat, count):
    at = mat.shape[1] // count - 1
    return (mat, (mat.shape[0], count), lambda *_: (0, at))


def expand_kernel(where, low_ref, high_ref, mat_low, mat_high, shift_ref, hidden_ref, slope_ref):
    chunk = low_ref.shape[0] // 4
    for at in range(4):
        rows = slice(at * chunk, (at + 1) * chunk)
        pre = dot(low_ref[rows, :], mat_low[...]) + dot(high_ref[rows, :], mat_high[...])
        pre = pre + shift_ref[...]
        cumul = 0.5 * (1.0 + lax.erf(pre * 0.7071067811865476))
        hidden_ref[rows, :] = (pre * cumul).astype(bf16)
        slope = cumul + pre * jnp.exp(-0.5 * pre * pre) * 0.3989422804014327
        slope_ref[rows, :] = slope.astype(bf16)


def expand(where, side, low, pack, mats, shift):
    rows, depth = low.shape
    columns = shift.shape[1]
    tile = columns // 8
    true = lambda i, where: (0, where[4 * side + i])
    return call(
        expand_kernel,
        (4,),
        where,
        [
            whole(low),
            first_columns(pack, depth, 1),
            (mats[0], (depth, tile), true),
            (mats[1], (depth, tile), true),
            (shift, (1, tile), true),
        ],
        [((rows, columns // 2), bf16, (rows, tile), column)] * 2,
        micros=7,
    )


def shrink_kernel(where, grad_ref, mat_low, mat_high, slope_low, slope_high, out_ref, sum_ref):
    for side, (mat, slope) in enumerate(((mat_low, slope_low), (mat_high, slope_high))):

        @pl.when(pl.program_id(0) // 4 == side)
        def _(mat=mat, slope=slope):
            grad = (dot(grad_ref[...], mat[...], NT) * slope[...].astype(f32)).astype(bf16)
            out_ref[...] = grad
            sum_ref[...] = jnp.sum(grad.astype(f32), 0, keepdims=True)


def shrink(where, grad, mats, slopes):
    rows, width = grad.shape
    columns = 2 * slopes[0].shape[1]
    tile = columns // 8
    true = lambda i, where: (0, where[i])
    near = lambda i, _: jnp.minimum(i, 3)
    far = lambda i, _: jnp.maximum(i - 4, 0)
    return call(
        shrink_kernel,
        (8,),
        where,
        [
            whole(grad),
            (mats[0], (tile, width), lambda i, _: (near(i, _), 0)),
            (mats[1], (tile, width), lambda i, _: (far(i, _), 0)),
            (slopes[0], (rows, tile), lambda i, _: (0, near(i, _))),
            (slopes[1], (rows, tile), lambda i, _: (0, far(i, _))),
        ],
        [((rows, columns), bf16, (rows, tile), true), ((1, columns), f32, (1, tile), true)],
        micros=12,
    )


def back_product(grad, mat):
    if len(grad.shape) == 2:
        return dot(grad[...], mat[...], NT)
    cols = grad.shape[2]
    return sum(dot(grad[i], mat[:, i * cols : (i + 1) * cols], NT) for i in range(3))


def back_kernel(low, where, grad_ref, mat_low, mat_high, values_ref, above_ref, gain_ref, out_ref, *rest):
    (*low_refs, gain_sum, bias_sum, total) = rest
    step = pl.program_id(0)

    def put(mat):
        part = back_product(grad_ref, mat)
        for side in range(2):
            total[:, lanes(where, 2 * step + side)] = part[:, side * 128 : (side + 1) * 128]

    @pl.when(step < 2)
    def _():
        put(mat_low)

    @pl.when(step >= 2)
    def _():
        put(mat_high)

    @pl.when(step == 3)
    def _():
        count, width = values_ref.shape
        chunk = 64
        sums = [jnp.zeros((1, width), f32)] * 3
        for first in range(0, count, chunk):
            rows = slice(first, first + chunk)
            normed, inverse = normalize(values_ref[rows, :].astype(f32))
            grad = total[rows, :]
            scaled = grad * gain_ref[...]
            result = above_ref[rows, :].astype(f32) + inverse * (
                scaled
                - jnp.mean(scaled, -1, keepdims=True)
                - normed * jnp.mean(scaled * normed, -1, keepdims=True)
            )
            out_ref[rows, :] = result
            sums[0] += jnp.sum(grad * normed, 0, keepdims=True)
            sums[1] += jnp.sum(grad, 0, keepdims=True)
            if low:
                rounded = result.astype(bf16)
                low_refs[0][rows, :] = rounded
                sums[2] += jnp.sum(rounded.astype(f32), 0, keepdims=True)
        gain_sum[...] = sums[0]
        bias_sum[...] = sums[1]
        if low:
            low_refs[1][...] = sums[2]


def back(where, grad, mats, values, above, gain, low):
    rows, width = values.shape
    columns = grad.shape[1] if grad.ndim == 2 else 3 * width
    outs = [whole_out((rows, width), f32)]
    if low:
        outs += [whole_out((rows, width), bf16), whole_out((1, width), f32)]
    outs += [whole_out((1, width), f32)] * 2
    return call(
        functools.partial(back_kernel, low),
        (4,),
        where,
        [
            whole(grad) if grad.ndim == 2 else (grad, (3, rows, width), lambda *_: (0, 0, 0)),
            (mats[0], (256, columns), lambda i, _: (jnp.minimum(i, 1), 0)),
            (mats[1], (256, columns), lambda i, _: (jnp.maximum(i - 2, 0), 0)),
            whole(values),
            whole(above),
            whole(gain),
        ],
        outs,
        [pltpu.VMEM((rows, width), f32)], micros=13)


def mixed_grad_kernel(where, grad_ref, low, high, out_ref):
    for at in range(4):
        mat = (low, high)[at // 2]
        part = dot(grad_ref[...], mat[at % 2 * 256 : at % 2 * 256 + 256, :], NT).astype(bf16)
        for side in range(2):
            out_ref[:, lanes(where, 2 * at + side)] = part[:, side * 128 : (side + 1) * 128]


def mixed_grad(where, grad, mats):
    return call(
        mixed_grad_kernel,
        (1,),
        where,
        [whole(grad), *[last_columns(m, grad.shape[1]) for m in mats]],
        [whole_out(grad.shape, bf16)], micros=3)[0]


def feed_kernel(where, low_ref, high_ref, mat_low, mat_high, middle_ref, shift_ref, keep_ref, out_ref):
    total = dot(low_ref[...], mat_low[...]) + dot(high_ref[...], mat_high[...])
    out_ref[...] = keep_ref[...] * (total + middle_ref[...] + shift_ref[...])


def feed(where, low, high, mats, middle, shift, keep):
    rows, width = middle.shape
    mat = ((mats[0].shape[0], 256), column)
    return call(
        feed_kernel,
        (width // 256,),
        where,
        [
            whole(low),
            whole(high),
            (mats[0], *mat),
            (mats[1], *mat),
            (middle, (rows, 256), column),
            (shift, (1, 256), column),
            whole(keep),
        ],
        [((rows, width), f32, (rows, 256), column)], micros=10)[0]


def product_kernel(counts, where, *refs):
    n = len(counts)
    lefts, rights, outs, turned = refs[: 2 * n], refs[2 * n : 4 * n], refs[4 * n : -2 * n], refs[-2 * n :]
    keep_a, send_a, keep_b, send_b = outs
    step = pl.program_id(0)
    middle = sum(counts) // 2

    @pl.when(step == 0)
    def _():
        for left, turn in zip(lefts, turned):
            turn[...] = left[...].T

    def put(pair, targets):
        own, other = turned[2 * pair : 2 * pair + 2]
        right, right_other = rights[2 * pair : 2 * pair + 2]
        count = own.shape[0] // 4
        total = (dot(own[...], right[...]) + dot(other[...], right_other[...])).astype(bf16)
        for target, blocks in targets:
            for at, block in enumerate(blocks):
                target[at * count : (at + 1) * count, :] = total[block * count : (block + 1) * count, :]

    first = 0
    for pair, count in enumerate(counts):
        here = (step >= first) & (step < first + count)

        @pl.when(here & (step < middle))
        def _(pair=pair):
            put(pair, ((keep_a, (0, 1)), (send_a, (2, 3))))

        @pl.when(here & (step >= middle))
        def _(pair=pair):
            put(pair, ((keep_b, (0, 2)), (send_b, (1, 3))))

        first += count


def add_kernel(where, a0, a1, b0, b1, keep_a, send_a, keep_b, send_b):
    half = a0.shape[0] // 2
    for kept, piece, targets in ((a0, a1, (keep_a, send_a)), (b0, b1, (keep_b, send_b))):
        for part, target in enumerate(targets):
            rows = slice(part * half, (part + 1) * half)
            total = kept[rows, :].astype(f32) + piece[rows, :].astype(f32)
            target[...] = total.astype(bf16)


def flat_kernel(where, a0, a1, b0, b1, out):
    columns = a0.shape[1]
    for side, (kept, piece) in enumerate(((a0, a1), (b0, b1))):
        total = kept[...].astype(f32) + piece[...].astype(f32)
        out[:, side * columns : (side + 1) * columns] = total.astype(bf16)


def finish_kernel(where, a0, a1, b0, b1, *refs):
    own, *others, total = refs
    columns = a0.shape[1]
    for side, (kept, piece) in enumerate(((a0, a1), (b0, b1))):
        total[:, side * columns : (side + 1) * columns] = kept[...].astype(f32) + piece[...].astype(f32)
    count = own.shape[0]
    for at, out in enumerate((own, *others)):
        rows = pl.ds(pl.multiple_of(where[16 + at] * count, count), count)
        out[...] = total[rows, :].astype(out.dtype)


class Sum:
    def __init__(self, swap, along, order, where, lefts, rights, tile, counts, flat=False):
        self.swap, self.along, self.order, self.where = swap, along, order, where
        self.lefts = [left for pair in lefts for left in pair]
        self.rights = [right for pair in rights for right in pair]
        self.tile, self.counts, self.flat = tile, counts, flat
        self.sent = 0

    def product(self, *arrays):
        n = len(self.counts)
        lefts, rights = arrays[: 2 * n], arrays[2 * n :]
        depth = lefts[0].shape[0]
        count = self.lefts[0][0].shape[1]
        specs = [first_columns(left, count, at) for left, (_, at) in zip(lefts, self.lefts)]
        first = 0
        for pair, steps in enumerate(self.counts):
            for right, (_, base) in list(zip(rights, self.rights))[2 * pair : 2 * pair + 2]:
                at = lambda i, first=first, steps=steps, base=base: base + jnp.clip(i - first, 0, steps - 1)
                if right.ndim == 2:
                    specs.append((right, (depth, self.tile), lambda i, _, at=at: (0, at(i))))
                else:
                    per = right.shape[2] // self.tile
                    specs.append(
                        (right, (None, depth, self.tile), lambda i, _, at=at: (at(i) // per, 0, at(i) % per))
                    )
            first += steps
        near = lambda i, _: (0, jnp.minimum(i, first // 2 - 1))
        far = lambda i, _: (0, jnp.maximum(i - first // 2, 0))
        shape = (count // 2, self.tile * first // 2)
        block = (count // 2, self.tile)
        return call(
            functools.partial(product_kernel, self.counts),
            (first,),
            self.where,
            specs,
            [(shape, bf16, block, near)] * 2 + [(shape, bf16, block, far)] * 2,
            [pltpu.VMEM((count, depth), bf16)] * (2 * n),
            micros=12,
        )

    def add(self, *pieces):
        rows, columns = pieces[0].shape
        tile = columns // 2
        block = ((rows, tile), column)
        half = ((rows // 2, columns), bf16, (rows // 2, tile), column)
        return call(
            add_kernel, (columns // tile,), self.where, [(v, *block) for v in pieces], [half] * 4, micros=12)

    def finish(self, *pieces):
        rows, columns = pieces[0].shape
        if self.flat:
            out = whole_out((rows, 2 * columns), bf16)
            return call(flat_kernel, (1,), self.where, [whole(v) for v in pieces], [out])
        owners = self.where.shape[0] - 16
        share = (rows // owners, 2 * columns)
        return call(
            finish_kernel,
            (1,),
            self.where,
            [whole(v) for v in pieces],
            [whole_out(share, f32)] + [whole_out(share, bf16)] * (owners - 1),
            [pltpu.VMEM((rows, 2 * columns), f32)],
        )

    def work(self):
        if self.sent == 2:
            self.own, *self.ready = self.order(
                self.finish, self.kept[0], self.arrived[0], self.kept[1], self.arrived[1]
            )
            return
        if self.sent == 0:
            factors = [array for array, _ in (*self.lefts, *self.rights)]
            keep_a, send_a, keep_b, send_b = self.order(self.product, *factors)
        else:
            keep_a, send_a, keep_b, send_b = self.order(
                self.add, self.kept[0], self.arrived[0], self.kept[1], self.arrived[1]
            )
        self.kept = keep_a, keep_b
        self.ready = send_a, send_b

    def send(self):
        if self.sent == 2 and self.flat:
            self.share = lax.psum_scatter(
                self.order.tie(self.own)[0], "fsdp", scatter_dimension=0, tiled=True
            )
            return
        ready = self.order.tie(*self.ready)
        if self.sent == 2:
            self.shares = [self.along(piece, by) for by, piece in enumerate(ready, 1)]
        else:
            bits = (XBIT, YBIT) if self.sent else (YBIT, XBIT)
            self.arrived = self.swap(ready[0], bits[0]), self.swap(ready[1], bits[1])
        self.sent += 1

    def total(self):
        if self.flat:
            return self.order(lambda share: share.astype(f32), self.share)
        return self.order(
            lambda own, *others: sum((piece.astype(f32) for piece in others), own), self.own, *self.shares
        )


class Order:
    def __init__(self):
        self.last = ()

    def __call__(self, function, *values):
        result = function(*self.tie(*values))
        self.last = (result[0] if isinstance(result, (tuple, list)) else result,)
        return result

    def tie(self, *values):
        return lax.optimization_barrier((*values, *self.last))[: len(values)]


def assemble_kernel(where, *refs):
    count = refs[0].shape[0]
    for at, piece in enumerate(refs[:-1]):
        rows = pl.ds(pl.multiple_of(where[at] * count, count), count)
        refs[-1][rows, :] = piece[...]


def assemble(places, *pieces):
    rows, columns = pieces[0].shape
    out = whole_out((rows * len(pieces), columns), bf16)
    return call(assemble_kernel, (1,), places, [whole(p) for p in pieces], [out])[0]


def join_kernel(where, own, near, far, left, right, out):
    count = own.shape[0]
    for at, piece in enumerate((own, near, far)):
        out[at * count : (at + 1) * count, :] = piece[...]
    for side, piece in enumerate((left, right)):

        @pl.when(pl.program_id(0) == side)
        def _(piece=piece):
            out[3 * count :, :] = piece[...]


def join(where, own, near, far, left, right):
    rows, columns = own.shape
    block = (rows, columns // 2)
    return call(
        join_kernel,
        (2,),
        where,
        [(v, block, column) for v in (own, near, far)] + [whole(left), whole(right)],
        [((4 * rows, columns), bf16, (4 * rows, columns // 2), column)], micros=4)[0]


def turn_kernel(where, near, far, left, right):
    left[...] = near[...]
    right[...] = far[...]


def turn(where, near, far):
    rows, columns = near.shape
    half = (rows, columns // 2)
    return call(
        turn_kernel,
        (1,),
        where,
        [(near, half, lambda *_: (0, 0)), (far, half, lambda *_: (0, 1))],
        [whole_out(half, bf16)] * 2,
    )


def pack_kernel(where, *refs):
    out = refs[-1]
    owners = out.shape[0]
    first = 0
    for vector in refs[:-1]:
        share = vector.shape[1] // owners
        for owner in range(owners):
            out[owner : owner + 1, first : first + share] = vector[:, owner * share : (owner + 1) * share]
        first += share


def pack(where, vectors, owners):
    columns = sum(v.shape[1] for v in vectors) // owners
    return call(
        pack_kernel, (1,), where, [whole(v) for v in vectors], [whole_out((owners, columns), f32)]
    )[0]


def unpack_kernel(where, low, high, *refs):
    outs, true = refs[:-1], refs[-1]
    for side, part in enumerate((low, high)):
        turned = part[...].astype(f32).T
        for at in range(4):
            true[:, lanes(where, 4 * side + at)] = turned[:, at * 128 : (at + 1) * 128]
    share = 32
    first = 0
    for vector in outs:
        columns = vector.shape[1] // true.shape[1]
        if columns == 1:
            vector[...] = true[first : first + 1, :]
        else:
            for owner in range(true.shape[1] // share):
                for at in range(columns):
                    start = (owner * columns + at) * share
                    vector[:, start : start + share] = true[
                        first + at : first + at + 1, owner * share : (owner + 1) * share
                    ]
        first += columns


def unpack(where, mats, sizes):
    block = mats[0].shape[1] // 128 - 2
    outs = [whole_out((1, size), f32) for size in sizes]
    rows = mats[0].shape[0]
    return call(
        unpack_kernel,
        (1,),
        where,
        [(mat, (rows, 128), lambda *_: (0, block)) for mat in mats],
        outs,
        [pltpu.VMEM((128, 2 * rows), f32)],
    )


def exchanged(fsdp_size, block_in, keep_mask, out_cotangent, *params):
    (g1, b1, qkv_weight, qv_bias, out_weight, out_bias, g2, b2, up_weight, up_bias, down_weight, down_bias) = params
    seqs, length, width = block_in.shape
    rows = seqs * length
    half = width // 2
    order = Order()
    me, line = lax.axis_index("dp"), lax.axis_index("fsdp")
    where = positions(me, line, fsdp_size)

    def swap(value, bit):
        return lax.ppermute(value, "dp", [(i, i ^ bit) for i in range(8)])

    def along(value, by):
        return lax.ppermute(value, "fsdp", [(i, (i + by) % fsdp_size) for i in range(fsdp_size)])

    class Gather:
        def start(self, block):
            self.own = order.tie(block)[0]
            self.near, self.far = swap(self.own, XBIT), swap(self.own, YBIT)

        def turn(self, *others):
            self.ready = order(lambda near, far, *_: turn(where, near, far), self.near, self.far, *others)

        def turned(self):
            left, right = order.tie(*self.ready)
            self.left, self.right = swap(left, YBIT), swap(right, XBIT)

        def join(self):
            self.low = order(
                functools.partial(join, where), self.own, self.near, self.far, self.left, self.right
            )

        def joined(self):
            low = order.tie(self.low)[0]
            self.mats = low, swap(low, CORE)

    def around(shard):
        return [shard] + [along(shard, by) for by in range(1, fsdp_size)]

    vectors = (g1, b1, qv_bias, out_bias, g2, b2, up_bias, down_bias)
    device_count = 8 * fsdp_size
    sizes = [v.shape[0] * device_count for v in vectors]
    cuts = [sum(v.shape[0] for v in vectors[:i]) for i in range(1, len(vectors))]
    share = qkv_weight.shape[0]
    beside = jnp.concatenate(vectors).reshape(-1, share).T
    beside = jnp.pad(beside, ((0, 0), (0, 256 - beside.shape[1])))
    qkv_low = jnp.concatenate([qkv_weight, beside], 1).astype(bf16)
    behind = jnp.stack([(line - by) % fsdp_size for by in range(fsdp_size)]).astype(jnp.int32)
    qkv_pieces = around(qkv_low)
    up_low = jnp.concatenate([up_weight, out_weight], 1).astype(bf16)
    down_block = lax.all_gather(down_weight.astype(bf16), "fsdp", axis=0, tiled=True)

    keep = jnp.concatenate(
        [jnp.ones((seqs, length - keep_mask.shape[1]), jnp.int32), keep_mask], axis=1
    )
    keep_rows = keep.reshape(rows, 1).astype(f32)
    keep_column = keep.reshape(seqs, length, 1)
    inputs = block_in.reshape(rows, width)
    grad_feed = jnp.where(keep_rows > 0, out_cotangent.reshape(rows, width), jnp.zeros((), bf16))
    down_bias_grad = jnp.sum(grad_feed.astype(f32), 0)

    qkv, up, down = Gather(), Gather(), Gather()
    block = order(functools.partial(assemble, behind), *qkv_pieces)
    qkv.start(block)
    up_pieces = around(order.tie(up_low)[0])
    qkv.turn()
    qkv.turned()
    up_block = order(functools.partial(assemble, behind), *up_pieces)
    qkv.join()
    qkv.joined()
    up.start(up_block)
    g1, b1, qv_bias, out_bias, g2, b2, up_bias, down_bias = order(
        lambda *m: unpack(where, m, sizes), *qkv.mats
    )
    one_low, one_pack = order(functools.partial(norm_one, where), inputs, grad_feed, g1, b1)
    shift = jnp.concatenate([qv_bias[:, :width], jnp.zeros((1, width), f32), qv_bias[:, width:]], 1)
    projected = order(
        lambda lo, hi, s, *m: project(where, lo, hi, m, s), one_low, one_pack, shift, *qkv.mats
    )
    mixed_left = order(lambda p: attention_forward(keep_column, p, 0), projected)
    up.turn(down_block)
    up.turned()
    one_other = swap(order.tie(one_pack)[0], CORE)
    mixed_right = order(lambda p: attention_forward(keep_column, p, 1), projected)
    up.join()
    up.joined()
    down.start(down_block)
    mixed = jnp.concatenate([mixed_left, mixed_right], 1)
    mix_low, middle, two_low, two_pack = order(
        lambda m, o, *mats: branch_norm(where, m, inputs, mats, o, g2, b2, length),
        mixed, out_bias, *up.mats,
    )
    hidden_high, slope_high = order(
        lambda lo, hi, s, *m: expand(where, 1, lo, hi, m, s), two_low, two_pack, up_bias, *up.mats
    )
    hidden_low, slope_low = order(
        lambda lo, hi, s, *m: expand(where, 0, lo, hi, m, s), two_low, two_pack, up_bias, *up.mats
    )
    down.turn()
    down.turned()
    hidden_other = swap(order.tie(hidden_high)[0], CORE)
    two_other = swap(order.tie(two_pack)[0], CORE)
    down_sum = Sum(
        swap, along, order, where,
        [((hidden_low, 0), (hidden_other, 0))], [((grad_feed, 0), (one_other, half // 256))],
        256, [width // 256], True,
    )
    down_sum.work()
    down.join()
    down.joined()
    down_sum.send()
    grad_pre, up_bias_grad = order(
        lambda g, s0, s1, *m: shrink(where, g, m, (s0, s1)),
        grad_feed, slope_low, slope_high, *down.mats,
    )
    down_sum.work()
    down_sum.send()
    pre_other = swap(order.tie(grad_pre)[0], CORE)
    grad_middle, grad_branch, out_bias_grad, gain_two_grad, bias_two_grad = order(
        lambda g, mid, above, *m: back(where, g, m, mid, above, g2, True),
        grad_pre, middle, grad_feed, *up.mats,
    )
    up_sum = Sum(
        swap, along, order, where,
        [((two_low, 0), (two_other, 1))], [((grad_pre, 0), (pre_other, 0))],
        512, [grad_pre.shape[1] // 512],
    )
    up_sum.work()
    down_sum.work()
    up_sum.send()
    grad_mixed = order(lambda g, *m: mixed_grad(where, g, m), grad_branch, *up.mats)
    grad_projected, sum_q, sum_v = order(
        lambda p, g, b: attention_backward(keep_column, p, g, b), projected, grad_mixed, grad_branch
    )
    up_sum.work()
    up_sum.send()
    projected_other = swap(order.tie(grad_projected)[0], CORE)
    down_sum.send()
    input_grad, gain_one_grad, bias_one_grad = order(
        lambda g, x, above, *m: back(where, g, m, x, above, g1, False),
        grad_projected, inputs, grad_middle, *qkv.mats,
    )
    grads = (
        gain_one_grad,
        bias_one_grad,
        jnp.concatenate([sum_q, sum_v], 1),
        out_bias_grad,
        gain_two_grad,
        bias_two_grad,
        up_bias_grad,
        down_bias_grad,
    )
    shares = order(lambda *g: pack(where, g, device_count), *[g.reshape(1, -1) for g in grads])
    mid_sum = Sum(
        swap, along, order, where,
        [((one_low, 0), (one_other, 0)), ((mix_low, 0), (two_other, 0))],
        [((grad_projected, 0), (projected_other, 0)), ((grad_projected, 6), (projected_other, 6))],
        512, [3 * width // 512, width // 512],
    )
    mid_sum.work()
    down_grad = down_sum.total()
    up_sum.work()
    mid_sum.send()
    up_sum.send()
    upper = me % 2 == 1
    shares = shares.reshape(4, 2, fsdp_size, -1)
    low, high = shares[:, 0], shares[:, 1]
    core_share = swap(order.tie(jnp.where(upper, low, high))[0], CORE)
    shares = jnp.where(upper, high, low)
    block_out = order(
        lambda lo, hi, mid, s, *m: feed(where, lo, hi, m, mid, s, keep_rows),
        hidden_low, hidden_high, middle, down_bias, *down.mats,
    )
    mid_sum.work()
    mid_sum.send()
    shares = order.tie(shares + core_share)[0]

    def part_of(bits):
        return lax.dynamic_index_in_dim(shares, (me ^ bits) // 2, 0, keepdims=False)

    plane_shares = [swap(part_of(bits), bits) for bits in (XBIT, YBIT, XBIT + YBIT)]
    up_grad = up_sum.total()
    mid_sum.work()
    mid_sum.send()
    shares = order.tie(sum(plane_shares, part_of(0)))[0]

    def row_of(by):
        return lax.dynamic_slice(shares, ((line + by) % fsdp_size, 0), (1, shares.shape[1]))

    line_shares = [along(row_of(by), by) for by in range(1, fsdp_size)]
    mid_grad = mid_sum.total()
    mine = sum(line_shares, row_of(0))
    qkv_grad, out_grad = mid_grad[:, : 3 * width], mid_grad[:, 3 * width :]
    v = jnp.split(mine[0], cuts)
    return (
        block_out.reshape(seqs, length, width),
        input_grad.reshape(seqs, length, width),
        v[0],
        v[1],
        qkv_grad,
        v[2],
        out_grad,
        v[3],
        v[4],
        v[5],
        up_grad,
        v[6],
        down_grad,
        v[7],
    )


def solution(mesh):
    dp_size, fsdp_size = mesh.shape["dp"], mesh.shape["fsdp"]
    if dp_size == 8:
        local = functools.partial(exchanged, fsdp_size)
    else:
        local = functools.partial(gathered, dp_size * fsdp_size)
    row = P(AXES, None)
    vec = P(AXES)
    cube = P(AXES, None, None)
    return jax.shard_map(
        local,
        mesh=mesh,
        in_specs=(cube, row, cube, vec, vec, row, vec, row, vec, vec, vec, row, vec, row, vec),
        out_specs=(cube, cube, vec, vec, row, vec, row, vec, vec, vec, row, vec, row, vec),
        check_vma=False,
    )
```

```python
import functools
import math

import jax
import jax.numpy as jnp
from jax import lax
from jax.experimental import pallas as pl
from jax.experimental.pallas import tpu as pltpu
from jax.sharding import PartitionSpec as P

HD = 64
EPSILON = 1e-05
AXES = ("dp", "fsdp")
bf16 = jnp.bfloat16
f32 = jnp.float32
NN = (((1,), (0,)), ((), ()))
NT = (((1,), (1,)), ((), ()))
TN = (((0,), (0,)), ((), ()))


def dot(left, right, dims=NN):
    return lax.dot_general(left, right, dims, preferred_element_type=f32)


def attention_forward_kernel(seqs, length, keep_ref, q_ref, k_ref, v_ref, o_ref):
    scale = 1.0 / math.sqrt(HD)
    for s in range(seqs):
        rows = slice(s * length, (s + 1) * length)
        visible = keep_ref[s] > 0
        mixed = []
        for h in range(128 // HD):
            cols = slice(h * HD, (h + 1) * HD)
            logits = dot(k_ref[rows, cols], q_ref[rows, cols] * scale, NT)
            logits = jnp.where(visible, logits, -1e9)
            raised = jnp.exp(logits - jnp.max(logits, 0, keepdims=True))
            probs = raised * (1.0 / jnp.sum(raised, 0, keepdims=True))
            mixed.append(dot(probs.astype(bf16), v_ref[rows, cols], TN))
        o_ref[rows, :] = jnp.concatenate(mixed, 1).astype(bf16)


def attention_backward_kernel(
    seqs, length, keep_ref, q_ref, k_ref, v_ref, do_ref, dp_ref, sq_ref, sv_ref
):
    scale = 1.0 / math.sqrt(HD)
    sum_q = jnp.zeros((1, 128), f32)
    sum_v = jnp.zeros((1, 128), f32)
    for s in range(seqs):
        rows = slice(s * length, (s + 1) * length)
        visible = keep_ref[s] > 0
        dqs, dks, dvs = [], [], []
        for h in range(128 // HD):
            cols = slice(h * HD, (h + 1) * HD)
            queries = q_ref[rows, cols] * scale
            keys = k_ref[rows, cols]
            grad_mixed = do_ref[rows, cols]
            logits = dot(keys, queries, NT)
            grad_probs = dot(v_ref[rows, cols], grad_mixed, NT)
            logits = jnp.where(visible, logits, -1e9)
            raised = jnp.exp(logits - jnp.max(logits, 0, keepdims=True))
            probs = raised * (1.0 / jnp.sum(raised, 0, keepdims=True))
            dvs.append(dot(probs.astype(bf16), grad_mixed))
            row_terms = jnp.sum(grad_probs * probs, 0, keepdims=True)
            grad_logits = (probs * (grad_probs - row_terms)).astype(bf16)
            dks.append(dot(grad_logits, queries))
            dqs.append(dot(grad_logits, keys, TN) * scale)
        dq = jnp.concatenate(dqs, 1).astype(bf16)
        dv = jnp.concatenate(dvs, 1).astype(bf16)
        dp_ref[0, rows, :] = dq
        dp_ref[1, rows, :] = jnp.concatenate(dks, 1).astype(bf16)
        dp_ref[2, rows, :] = dv
        sum_q += jnp.sum(dq.astype(f32), 0, keepdims=True)
        sum_v += jnp.sum(dv.astype(f32), 0, keepdims=True)
    sq_ref[...] = sum_q
    sv_ref[...] = sum_v


def attention_forward(keep, project, part):
    seqs, length = keep.shape[:2]
    rows, width = project.shape[0], project.shape[1] // 6
    steps = width // 128
    block = pl.BlockSpec((rows, 128), lambda i: (0, i))
    return pl.pallas_call(
        functools.partial(attention_forward_kernel, seqs, length),
        grid=(steps,),
        in_specs=[pl.BlockSpec((seqs, length, 1), lambda i: (0, 0, 0))]
        + [
            pl.BlockSpec((rows, 128), lambda i, at=at: (0, i + (2 * at + part) * steps))
            for at in range(3)
        ],
        out_specs=block,
        out_shape=jax.ShapeDtypeStruct((rows, width), bf16),
        compiler_params=pltpu.CompilerParams(vmem_limit_bytes=16 << 20),
        cost_estimate=pl.CostEstimate(flops=int(8.5 * COST), bytes_accessed=1, transcendentals=0),
    )(keep, project, project, project)


def attention_backward(keep, project, grad_mixed):
    seqs, length = keep.shape[:2]
    rows, width = project.shape[0], project.shape[1] // 3
    steps = width // 128
    block = pl.BlockSpec((rows, 128), lambda i: (0, i))
    vector = pl.BlockSpec((1, 128), lambda i: (0, i))
    sums = jax.ShapeDtypeStruct((1, width), f32)
    return pl.pallas_call(
        functools.partial(attention_backward_kernel, seqs, length),
        grid=(steps,),
        in_specs=[pl.BlockSpec((seqs, length, 1), lambda i: (0, 0, 0))]
        + [pl.BlockSpec((rows, 128), lambda i, at=at: (0, i + at * steps)) for at in range(3)]
        + [block],
        out_specs=[pl.BlockSpec((3, rows, 128), lambda i: (0, 0, i)), vector, vector],
        out_shape=[pltpu.HBM((3, rows, width), bf16), sums, sums],
        compiler_params=pltpu.CompilerParams(vmem_limit_bytes=16 << 20),
        cost_estimate=pl.CostEstimate(flops=int(22 * COST), bytes_accessed=1, transcendentals=0),
    )(keep, project, project, project, grad_mixed)


def norm_forward(values, norm_gain, norm_bias):
    average = jnp.mean(values, -1, keepdims=True)
    centered = values - average
    inverse = lax.rsqrt(jnp.mean(centered * centered, -1, keepdims=True) + EPSILON)
    normed = centered * inverse
    return (normed * norm_gain + norm_bias, normed, inverse)


def norm_backward(grad_norm, normed, inverse, norm_gain):
    scaled = grad_norm * norm_gain
    return inverse * (
        scaled
        - jnp.mean(scaled, -1, keepdims=True)
        - normed * jnp.mean(scaled * normed, -1, keepdims=True)
    )


def gathered(device_count, block_in, keep_mask, out_cotangent, *params):
    (g1, b1, qkv_weight, qv_bias, out_weight, out_bias, g2, b2, up_weight, up_bias, down_weight, down_bias) = params
    seqs, length, width = block_in.shape
    rows = seqs * length
    vectors = (g1, b1, qv_bias, out_bias, g2, b2, up_bias, down_bias)
    sizes = [v.shape[0] for v in vectors]
    cuts = [sum(sizes[:i]) for i in range(1, len(sizes))]
    packed = lax.all_gather(jnp.concatenate(vectors).astype(bf16), AXES, axis=0, tiled=False)
    g1, b1, qv_bias, out_bias, g2, b2, up_bias, down_bias = (
        part.reshape(-1).astype(f32) for part in jnp.split(packed, cuts, axis=1)
    )
    qkv_mat, out_mat, up_mat, down_mat = (
        lax.all_gather(w.astype(bf16), AXES, axis=0, tiled=True)
        for w in (qkv_weight, out_weight, up_weight, down_weight)
    )
    keep = jnp.concatenate(
        [jnp.ones((seqs, length - keep_mask.shape[1]), jnp.int32), keep_mask], axis=1
    )
    keep_rows = keep.reshape(rows, 1).astype(f32)
    keep_column = keep.reshape(seqs, length, 1)
    inputs = block_in.astype(f32).reshape(rows, width)
    grad_out = out_cotangent.astype(f32).reshape(rows, width) * keep_rows
    grad_feed = grad_out.astype(bf16)

    normed_one, plain_one, inverse_one = norm_forward(inputs, g1, b1)
    act_one = normed_one.astype(bf16)
    zeros = jnp.zeros((width,), f32)
    shift = jnp.concatenate([qv_bias[:width], zeros, qv_bias[width:]])
    project = (dot(act_one, qkv_mat) + shift).astype(bf16)

    mixed = jnp.concatenate([attention_forward(keep_column, project, part) for part in range(2)], 1)
    middle = inputs + dot(mixed, out_mat) + out_bias
    normed_two, plain_two, inverse_two = norm_forward(middle, g2, b2)
    act_two = normed_two.astype(bf16)
    pre = dot(act_two, up_mat) + up_bias
    cumul = 0.5 * (1.0 + lax.erf(pre * 0.7071067811865476))
    hidden = (pre * cumul).astype(bf16)
    slope = cumul + pre * jnp.exp(-0.5 * pre * pre) * 0.3989422804014327
    feed = dot(hidden, down_mat) + down_bias
    block_out = keep_rows * (middle + feed)

    grad_pre = (dot(grad_feed, down_mat, NT) * slope).astype(bf16)
    grad_act_two = dot(grad_pre, up_mat, NT)
    grad_middle = grad_out + norm_backward(grad_act_two, plain_two, inverse_two, g2)
    grad_branch = grad_middle.astype(bf16)
    grad_mixed = dot(grad_branch, out_mat, NT).astype(bf16)
    grad_parts, sum_q, sum_v = attention_backward(keep_column, project, grad_mixed)
    grad_project = jnp.concatenate([grad_parts[i] for i in range(3)], 1)
    grad_act_one = dot(grad_project, qkv_mat, NT)
    input_grad = grad_middle + norm_backward(grad_act_one, plain_one, inverse_one, g1)
    grads = (
        jnp.sum(grad_act_one * plain_one, 0),
        jnp.sum(grad_act_one, 0),
        jnp.concatenate([sum_q[0], sum_v[0]]),
        jnp.sum(grad_branch.astype(f32), 0),
        jnp.sum(grad_act_two * plain_two, 0),
        jnp.sum(grad_act_two, 0),
        jnp.sum(grad_pre.astype(f32), 0),
        jnp.sum(grad_feed.astype(f32), 0),
    )
    shares = jnp.concatenate([g.reshape(device_count, -1) for g in grads], 1)
    v = jnp.split(lax.psum_scatter(shares, AXES, scatter_dimension=0, tiled=False), cuts)

    def to_owner(left, right):
        total = dot(left, right, TN).astype(bf16)
        return lax.psum_scatter(total, AXES, scatter_dimension=0, tiled=True).astype(f32)

    return (
        block_out.reshape(seqs, length, width),
        input_grad.reshape(seqs, length, width),
        v[0],
        v[1],
        to_owner(act_one, grad_project),
        v[2],
        to_owner(mixed, grad_branch),
        v[3],
        v[4],
        v[5],
        to_owner(act_two, grad_pre),
        v[6],
        to_owner(hidden, grad_feed),
        v[7],
    )


CORE, XBIT, YBIT = 1, 2, 4
BLOCKS = [c * CORE + y * YBIT + x * XBIT for c in range(2) for y in range(2) for x in range(2)]
COST = 1e12


def positions(me, line, count):
    true = [me ^ r for r in BLOCKS]
    place = [
        sum(jnp.where((me ^ d) == r, at, 0) for at, r in enumerate(BLOCKS)) for d in range(8)
    ]
    ahead = [(line + by) % count for by in range(count)]
    return jnp.stack(true + place + ahead).astype(jnp.int32)


def call(kernel, grid, where, ins, outs, scratch=(), micros=3, sent=()):
    held = 6 << 20
    specs = []
    for array, block, index in ins:
        once = tuple(block) == tuple(array.shape)
        size = math.prod(n or 1 for n in block) * array.dtype.itemsize
        held += size if once else 2 * size
        specs.append(pl.BlockSpec(block, index, pipeline_mode=pl.Buffered(1) if once else None))
    for _, dtype, block, _ in outs:
        held += 2 * math.prod(block) * jnp.dtype(dtype).itemsize
    for buffer in scratch:
        held += math.prod(buffer.shape) * jnp.dtype(buffer.dtype).itemsize
    return pl.pallas_call(
        kernel,
        grid_spec=pltpu.PrefetchScalarGridSpec(
            num_scalar_prefetch=1,
            grid=grid,
            in_specs=specs,
            out_specs=[pl.BlockSpec(block, index) for _, _, block, index in outs],
            scratch_shapes=list(scratch),
        ),
        out_shape=[
            pltpu.HBM(shape, dtype) if at in sent else jax.ShapeDtypeStruct(shape, dtype)
            for at, (shape, dtype, _, _) in enumerate(outs)
        ],
        compiler_params=pltpu.CompilerParams(vmem_limit_bytes=held),
        cost_estimate=pl.CostEstimate(flops=int(micros * COST), bytes_accessed=1, transcendentals=0),
    )(where, *[array for array, _, _ in ins])


def whole(array):
    return (array, array.shape, lambda *_: (0,) * array.ndim)


def whole_out(shape, dtype):
    return (shape, dtype, shape, lambda *_: (0,) * len(shape))


def column(i, *_):
    return (0, i)


def lanes(where, at):
    return pl.ds(pl.multiple_of(where[at] * 128, 128), 128)


def deal(where, source, low, high):
    for at in range(4):
        cols = slice(at * 128, (at + 1) * 128)
        low[:, cols] = source[:, lanes(where, at)]
        high[:, cols] = source[:, lanes(where, 4 + at)]


def normalize(values):
    centered = values - jnp.mean(values, -1, keepdims=True)
    inverse = lax.rsqrt(jnp.mean(centered * centered, -1, keepdims=True) + EPSILON)
    return centered * inverse, inverse


def norm_kernel(where, x_ref, grad_ref, gain_ref, bias_ref, low_ref, pack_ref, whole_ref):
    normed, _ = normalize(x_ref[...].astype(f32))
    whole_ref[...] = (normed * gain_ref[...] + bias_ref[...]).astype(bf16)
    half = low_ref.shape[1]
    deal(where, whole_ref, low_ref, pack_ref.at[:, :half])
    pack_ref[:, half:] = grad_ref[...]


def norm_one(where, inputs, grad_feed, gain, bias):
    rows, width = inputs.shape
    index = lambda i, _: (i, 0)
    return call(
        norm_kernel,
        (rows // 128,),
        where,
        [(inputs, (128, width), index), (grad_feed, (128, width), index), whole(gain), whole(bias)],
        [
            ((rows, width // 2), bf16, (128, width // 2), index),
            ((rows, width // 2 + width), bf16, (128, width // 2 + width), index),
        ],
        [pltpu.VMEM((128, width), bf16)],
    )


def project_kernel(where, low_ref, high_ref, mat_low, mat_high, bias_ref, out_ref):
    total = dot(low_ref[...], mat_low[...]) + dot(high_ref[...], mat_high[...])
    out_ref[...] = (total + bias_ref[...]).astype(bf16)


def project(where, low, pack, mats, bias):
    rows, depth = low.shape
    columns = bias.shape[1]
    tile = ((depth, 512), column)
    return call(
        project_kernel,
        (columns // 512,),
        where,
        [whole(low), first_columns(pack, depth), (mats[0], *tile), (mats[1], *tile), (bias, (1, 512), column)],
        [((rows, columns), bf16, (rows, 512), column)], micros=8)[0]


def branch_kernel(
    where, mixed_ref, x_ref, mat_low, mat_high, shift_ref, gain_ref, bias_ref,
    mix_low, middle_ref, two_low, pack_ref, whole_ref,
):
    half = mix_low.shape[1]
    mix_high, two_high = pack_ref.at[:, :half], pack_ref.at[:, half:]
    deal(where, mixed_ref, mix_low, mix_high)
    total = dot(mix_low[...], mat_low[...]) + dot(mix_high[...], mat_high[...])
    middle = x_ref[...].astype(f32) + total + shift_ref[...]
    middle_ref[...] = middle
    normed, _ = normalize(middle)
    whole_ref[...] = (normed * gain_ref[...] + bias_ref[...]).astype(bf16)
    deal(where, whole_ref, two_low, two_high)


def branch_norm(where, mixed, inputs, mats, shift, gain, bias, length):
    rows, width = inputs.shape
    block = ((length, width), lambda i, _: (i, 0))
    part = ((rows, width // 2), bf16, (length, width // 2), lambda i, _: (i, 0))
    return call(
        branch_kernel,
        (rows // length,),
        where,
        [(mixed, *block), (inputs, *block), *[last_columns(m, width) for m in mats]]
        + [whole(v) for v in (shift, gain, bias)],
        [part, ((rows, width), f32, *block), part, ((rows, width), bf16, *block)],
        [pltpu.VMEM((length, width), bf16)], micros=4)


def first_columns(mat, count, at=0):
    return (mat, (mat.shape[0], count), lambda *_: (0, at))


def last_columns(mat, count):
    at = mat.shape[1] // count - 1
    return (mat, (mat.shape[0], count), lambda *_: (0, at))


def expand_kernel(where, low_ref, high_ref, mat_low, mat_high, shift_ref, hidden_ref, slope_ref):
    chunk = low_ref.shape[0] // 4
    for at in range(4):
        rows = slice(at * chunk, (at + 1) * chunk)
        pre = dot(low_ref[rows, :], mat_low[...]) + dot(high_ref[rows, :], mat_high[...])
        pre = pre + shift_ref[...]
        cumul = 0.5 * (1.0 + lax.erf(pre * 0.7071067811865476))
        hidden_ref[rows, :] = (pre * cumul).astype(bf16)
        slope = cumul + pre * jnp.exp(-0.5 * pre * pre) * 0.3989422804014327
        slope_ref[rows, :] = slope.astype(bf16)


def expand(where, side, low, pack, mats, shift):
    rows, depth = low.shape
    columns = shift.shape[1]
    tile = columns // 8
    true = lambda i, where: (0, where[4 * side + i])
    return call(
        expand_kernel,
        (4,),
        where,
        [
            whole(low),
            first_columns(pack, depth, 1),
            (mats[0], (depth, tile), true),
            (mats[1], (depth, tile), true),
            (shift, (1, tile), true),
        ],
        [((rows, columns // 2), bf16, (rows, tile), column)] * 2,
        micros=7,
    )


def shrink_kernel(where, grad_ref, mat_low, mat_high, slope_low, slope_high, out_ref, sum_ref):
    for side, (mat, slope) in enumerate(((mat_low, slope_low), (mat_high, slope_high))):

        @pl.when(pl.program_id(0) // 4 == side)
        def _(mat=mat, slope=slope):
            grad = (dot(grad_ref[...], mat[...], NT) * slope[...].astype(f32)).astype(bf16)
            out_ref[...] = grad
            sum_ref[...] = jnp.sum(grad.astype(f32), 0, keepdims=True)


def shrink(where, grad, mats, slopes):
    rows, width = grad.shape
    columns = 2 * slopes[0].shape[1]
    tile = columns // 8
    true = lambda i, where: (0, where[i])
    near = lambda i, _: jnp.minimum(i, 3)
    far = lambda i, _: jnp.maximum(i - 4, 0)
    return call(
        shrink_kernel,
        (8,),
        where,
        [
            whole(grad),
            (mats[0], (tile, width), lambda i, _: (near(i, _), 0)),
            (mats[1], (tile, width), lambda i, _: (far(i, _), 0)),
            (slopes[0], (rows, tile), lambda i, _: (0, near(i, _))),
            (slopes[1], (rows, tile), lambda i, _: (0, far(i, _))),
        ],
        [((rows, columns), bf16, (rows, tile), true), ((1, columns), f32, (1, tile), true)],
        micros=12,
    )


def back_product(grad, mat):
    if len(grad.shape) == 2:
        return dot(grad[...], mat[...], NT)
    cols = grad.shape[2]
    return sum(dot(grad[i], mat[:, i * cols : (i + 1) * cols], NT) for i in range(3))


def back_kernel(low, where, grad_ref, mat_low, mat_high, values_ref, above_ref, gain_ref, *rest):
    if low:
        out_ref, low_ref, low_sum, gain_sum, bias_sum, total = rest
    else:
        *vectors, out_ref, packed, total = rest
    step = pl.program_id(0)

    def put(mat):
        part = back_product(grad_ref, mat)
        for side in range(2):
            total[:, lanes(where, 2 * step + side)] = part[:, side * 128 : (side + 1) * 128]

    @pl.when(step < 2)
    def _():
        put(mat_low)

    @pl.when(step >= 2)
    def _():
        put(mat_high)

    @pl.when(step == 3)
    def _():
        count, width = values_ref.shape
        chunk = 64
        sums = [jnp.zeros((1, width), f32)] * 3
        for first in range(0, count, chunk):
            rows = slice(first, first + chunk)
            normed, inverse = normalize(values_ref[rows, :].astype(f32))
            grad = total[rows, :]
            scaled = grad * gain_ref[...]
            result = above_ref[rows, :].astype(f32) + inverse * (
                scaled
                - jnp.mean(scaled, -1, keepdims=True)
                - normed * jnp.mean(scaled * normed, -1, keepdims=True)
            )
            out_ref[rows, :] = result
            sums[0] += jnp.sum(grad * normed, 0, keepdims=True)
            sums[1] += jnp.sum(grad, 0, keepdims=True)
            if low:
                rounded = result.astype(bf16)
                low_ref[rows, :] = rounded
                sums[2] += jnp.sum(rounded.astype(f32), 0, keepdims=True)
        if low:
            gain_sum[...] = sums[0]
            bias_sum[...] = sums[1]
            low_sum[...] = sums[2]
        else:
            owners = packed.shape[0]
            at = 0
            for vector in (*sums[:2], *[ref[...] for ref in vectors]):
                share = vector.shape[1] // owners
                for owner in range(owners):
                    packed[owner : owner + 1, at : at + share] = vector[
                        :, owner * share : (owner + 1) * share
                    ]
                at += share


def back(where, grad, mats, values, above, gain, vectors=(), owners=0):
    low = not vectors
    rows, width = values.shape
    columns = grad.shape[1] if grad.ndim == 2 else 3 * width
    outs = [whole_out((rows, width), f32)]
    if low:
        outs += [whole_out((rows, width), bf16)] + [whole_out((1, width), f32)] * 3
    else:
        columns_packed = (2 * width + sum(v.shape[1] for v in vectors)) // owners
        outs += [whole_out((owners, columns_packed), f32)]
    return call(
        functools.partial(back_kernel, low),
        (4,),
        where,
        [
            whole(grad) if grad.ndim == 2 else (grad, (3, rows, width), lambda *_: (0, 0, 0)),
            (mats[0], (256, columns), lambda i, _: (jnp.minimum(i, 1), 0)),
            (mats[1], (256, columns), lambda i, _: (jnp.maximum(i - 2, 0), 0)),
            whole(values),
            whole(above),
            whole(gain),
            *[whole(v) for v in vectors],
        ],
        outs,
        [pltpu.VMEM((rows, width), f32)], micros=13)


def mixed_grad_kernel(where, grad_ref, low, high, out_ref):
    for at in range(4):
        mat = (low, high)[at // 2]
        part = dot(grad_ref[...], mat[at % 2 * 256 : at % 2 * 256 + 256, :], NT).astype(bf16)
        for side in range(2):
            out_ref[:, lanes(where, 2 * at + side)] = part[:, side * 128 : (side + 1) * 128]


def mixed_grad(where, grad, mats):
    return call(
        mixed_grad_kernel,
        (1,),
        where,
        [whole(grad), *[last_columns(m, grad.shape[1]) for m in mats]],
        [whole_out(grad.shape, bf16)], micros=3)[0]


def feed_kernel(where, low_ref, high_ref, mat_low, mat_high, middle_ref, shift_ref, keep_ref, out_ref):
    total = dot(low_ref[...], mat_low[...]) + dot(high_ref[...], mat_high[...])
    out_ref[...] = keep_ref[...] * (total + middle_ref[...] + shift_ref[...])


def feed(where, low, high, mats, middle, shift, keep):
    rows, width = middle.shape
    mat = ((mats[0].shape[0], 256), column)
    return call(
        feed_kernel,
        (width // 256,),
        where,
        [
            whole(low),
            whole(high),
            (mats[0], *mat),
            (mats[1], *mat),
            (middle, (rows, 256), column),
            (shift, (1, 256), column),
            whole(keep),
        ],
        [((rows, width), f32, (rows, 256), column)], micros=10)[0]


def product_kernel(counts, where, *refs):
    n = len(counts)
    lefts, rights, outs, turned = refs[: 2 * n], refs[2 * n : 4 * n], refs[4 * n : -2 * n], refs[-2 * n :]
    keep_a, send_a, keep_b, send_b = outs
    step = pl.program_id(0)
    middle = sum(counts) // 2

    @pl.when(step == 0)
    def _():
        for left, turn in zip(lefts, turned):
            turn[...] = left[...].T

    def put(pair, targets):
        own, other = turned[2 * pair : 2 * pair + 2]
        right, right_other = rights[2 * pair : 2 * pair + 2]
        count = own.shape[0] // 4
        total = (dot(own[...], right[...]) + dot(other[...], right_other[...])).astype(bf16)
        for target, blocks in targets:
            for at, block in enumerate(blocks):
                target[at * count : (at + 1) * count, :] = total[block * count : (block + 1) * count, :]

    first = 0
    for pair, count in enumerate(counts):
        here = (step >= first) & (step < first + count)

        @pl.when(here & (step < middle))
        def _(pair=pair):
            put(pair, ((keep_a, (0, 1)), (send_a, (2, 3))))

        @pl.when(here & (step >= middle))
        def _(pair=pair):
            put(pair, ((keep_b, (0, 2)), (send_b, (1, 3))))

        first += count


def add_kernel(where, a0, a1, b0, b1, keep_a, send_a, keep_b, send_b):
    half = a0.shape[0] // 2
    for kept, piece, targets in ((a0, a1, (keep_a, send_a)), (b0, b1, (keep_b, send_b))):
        for part, target in enumerate(targets):
            rows = slice(part * half, (part + 1) * half)
            total = kept[rows, :].astype(f32) + piece[rows, :].astype(f32)
            target[...] = total.astype(bf16)


def flat_kernel(where, a0, a1, b0, b1, out):
    columns = a0.shape[1]
    for side, (kept, piece) in enumerate(((a0, a1), (b0, b1))):
        total = kept[...].astype(f32) + piece[...].astype(f32)
        out[:, side * columns : (side + 1) * columns] = total.astype(bf16)


def finish_kernel(where, a0, a1, b0, b1, *refs):
    own, *others, total = refs
    columns = a0.shape[1]
    for side, (kept, piece) in enumerate(((a0, a1), (b0, b1))):
        total[:, side * columns : (side + 1) * columns] = kept[...].astype(f32) + piece[...].astype(f32)
    count = own.shape[0]
    for at, out in enumerate((own, *others)):
        rows = pl.ds(pl.multiple_of(where[16 + at] * count, count), count)
        out[...] = total[rows, :].astype(out.dtype)


class Sum:
    def __init__(self, swap, along, order, where, lefts, rights, tile, counts, flat=False):
        self.swap, self.along, self.order, self.where = swap, along, order, where
        self.lefts = [left for pair in lefts for left in pair]
        self.rights = [right for pair in rights for right in pair]
        self.tile, self.counts, self.flat = tile, counts, flat
        self.sent = 0
        self.shares = []

    def product(self, *arrays):
        n = len(self.counts)
        lefts, rights = arrays[: 2 * n], arrays[2 * n :]
        depth = lefts[0].shape[0]
        count = self.lefts[0][0].shape[1]
        specs = [first_columns(left, count, at) for left, (_, at) in zip(lefts, self.lefts)]
        first = 0
        for pair, steps in enumerate(self.counts):
            for right, (_, base) in list(zip(rights, self.rights))[2 * pair : 2 * pair + 2]:
                at = lambda i, first=first, steps=steps, base=base: base + jnp.clip(i - first, 0, steps - 1)
                if right.ndim == 2:
                    specs.append((right, (depth, self.tile), lambda i, _, at=at: (0, at(i))))
                else:
                    per = right.shape[2] // self.tile
                    specs.append(
                        (right, (None, depth, self.tile), lambda i, _, at=at: (at(i) // per, 0, at(i) % per))
                    )
            first += steps
        near = lambda i, _: (0, jnp.minimum(i, first // 2 - 1))
        far = lambda i, _: (0, jnp.maximum(i - first // 2, 0))
        shape = (count // 2, self.tile * first // 2)
        block = (count // 2, self.tile)
        return call(
            functools.partial(product_kernel, self.counts),
            (first,),
            self.where,
            specs,
            [(shape, bf16, block, near)] * 2 + [(shape, bf16, block, far)] * 2,
            [pltpu.VMEM((count, depth), bf16)] * (2 * n),
            micros=12,
            sent=(0, 1, 2, 3),
        )

    def add(self, *pieces):
        rows, columns = pieces[0].shape
        tile = columns // 2
        block = ((rows, tile), column)
        half = ((rows // 2, columns), bf16, (rows // 2, tile), column)
        return call(
            add_kernel, (columns // tile,), self.where, [(v, *block) for v in pieces], [half] * 4, micros=12)

    def finish(self, *pieces):
        rows, columns = pieces[0].shape
        if self.flat:
            out = whole_out((rows, 2 * columns), bf16)
            return call(flat_kernel, (1,), self.where, [whole(v) for v in pieces], [out])
        owners = self.where.shape[0] - 16
        share = (rows // owners, 2 * columns)
        return call(
            finish_kernel,
            (1,),
            self.where,
            [whole(v) for v in pieces],
            [whole_out(share, f32)] + [whole_out(share, bf16)] * (owners - 1),
            [pltpu.VMEM((rows, 2 * columns), f32)],
        )

    def work(self):
        if self.sent == 2:
            self.own, *self.ready = self.order(
                self.finish, self.kept[0], self.arrived[0], self.kept[1], self.arrived[1]
            )
            return
        if self.sent == 0:
            factors = [array for array, _ in (*self.lefts, *self.rights)]
            keep_a, send_a, keep_b, send_b = self.order(self.product, *factors)
        else:
            keep_a, send_a, keep_b, send_b = self.order(
                self.add, self.kept[0], self.arrived[0], self.kept[1], self.arrived[1]
            )
        self.kept = keep_a, keep_b
        self.ready = send_a, send_b

    def send(self, shares=()):
        if self.sent < 2:
            ready = self.order.tie(*self.ready)
            bits = (XBIT, YBIT) if self.sent else (YBIT, XBIT)
            self.arrived = self.swap(ready[0], bits[0]), self.swap(ready[1], bits[1])
            self.sent += 1
        elif self.flat:
            self.share = lax.psum_scatter(
                self.order.tie(self.own)[0], "fsdp", scatter_dimension=0, tiled=True
            )
        else:
            for by, piece in zip(shares, self.order.tie(*[self.ready[by - 1] for by in shares])):
                self.shares.append(self.along(piece, by))

    def meet(self):
        if self.flat:
            (self.share,) = self.order.tie(self.share)
            self.order.last = (self.share,)
        else:
            self.shares = list(self.order.tie(*self.shares))
            self.order.last = (self.shares[0],)

    def total(self):
        if self.flat:
            return self.order(lambda share: share.astype(f32), self.share)
        return self.order(
            lambda own, *others: sum((piece.astype(f32) for piece in others), own), self.own, *self.shares
        )


class Order:
    def __init__(self):
        self.last = ()

    def __call__(self, function, *values):
        result = function(*self.tie(*values))
        self.last = (result[0] if isinstance(result, (tuple, list)) else result,)
        return result

    def tie(self, *values):
        return lax.optimization_barrier((*values, *self.last))[: len(values)]


def assemble_kernel(where, *refs):
    pieces, targets = [], []
    for ref in refs:
        (pieces if ref.shape[0] == refs[0].shape[0] else targets).append(ref)
    count = pieces[0].shape[0]
    columns = targets[0].shape[1]
    for at, piece in enumerate(pieces):
        rows = pl.ds(pl.multiple_of(where[at] * count, count), count)
        for side, target in enumerate(targets):
            target[rows, :] = piece[:, side * columns : (side + 1) * columns]


def assemble(count, places, *pieces):
    rows, columns = pieces[0].shape
    out = whole_out((rows * len(pieces), columns // count), bf16)
    return call(assemble_kernel, (1,), places, [whole(p) for p in pieces], [out] * count)


def join_kernel(where, *refs):
    out = refs[-1]
    count = refs[0].shape[0]
    for side in range(2):

        @pl.when(pl.program_id(0) == side)
        def _(side=side):
            for at, piece in enumerate(refs[4 * side : 4 * side + 4]):
                out[at * count : (at + 1) * count, :] = piece[...]


def join(where, *pieces):
    rows, columns = pieces[3].shape
    ins = [first_columns(p, columns, at // 4 if p.shape[1] > columns else 0) for at, p in enumerate(pieces)]
    return call(
        join_kernel,
        (2,),
        where,
        ins,
        [((4 * rows, 2 * columns), bf16, (4 * rows, columns), column)],
        micros=4,
    )[0]


def split_kernel(where, near, far, left, right):
    left[...] = near[...]
    right[...] = far[...]


def split(where, near, far):
    rows, columns = near.shape[0], near.shape[1] // 2
    return call(
        split_kernel,
        (1,),
        where,
        [first_columns(near, columns, 0), first_columns(far, columns, 1)],
        [whole_out((rows, columns), bf16)] * 2,
    )


def unpack_kernel(where, low, high, *refs):
    outs, true = refs[:-1], refs[-1]
    for side, part in enumerate((low, high)):
        turned = part[...].astype(f32).T
        for at in range(4):
            true[:, lanes(where, 4 * side + at)] = turned[:, at * 128 : (at + 1) * 128]
    share = 32
    first = 0
    for vector in outs:
        columns = vector.shape[1] // true.shape[1]
        if columns == 1:
            vector[...] = true[first : first + 1, :]
        else:
            for owner in range(true.shape[1] // share):
                for at in range(columns):
                    start = (owner * columns + at) * share
                    vector[:, start : start + share] = true[
                        first + at : first + at + 1, owner * share : (owner + 1) * share
                    ]
        first += columns


def unpack(where, mats, sizes):
    block = mats[0].shape[1] // 128 - 2
    outs = [whole_out((1, size), f32) for size in sizes]
    rows = mats[0].shape[0]
    return call(
        unpack_kernel,
        (1,),
        where,
        [(mat, (rows, 128), lambda *_: (0, block)) for mat in mats],
        outs,
        [pltpu.VMEM((128, 2 * rows), f32)],
    )


def exchanged(fsdp_size, block_in, keep_mask, out_cotangent, *params):
    (g1, b1, qkv_weight, qv_bias, out_weight, out_bias, g2, b2, up_weight, up_bias, down_weight, down_bias) = params
    seqs, length, width = block_in.shape
    rows = seqs * length
    half = width // 2
    order = Order()
    me, line = lax.axis_index("dp"), lax.axis_index("fsdp")
    where = positions(me, line, fsdp_size)

    def swap(value, bit):
        return lax.ppermute(value, "dp", [(i, i ^ bit) for i in range(8)])

    def along(value, by):
        return lax.ppermute(value, "fsdp", [(i, (i + by) % fsdp_size) for i in range(fsdp_size)])

    class Gather:
        def start(self, left, right):
            left, right = self.own = order.tie(left, right)
            self.near = swap(left, XBIT), swap(right, XBIT)
            self.far = swap(left, YBIT), swap(right, YBIT)

        def turn(self, *others):
            *pieces, = order.tie(*self.near, *self.far, *others)
            self.near, self.far = tuple(pieces[:2]), tuple(pieces[2:4])
            left, right = self.near[0], self.far[1]
            order.last = (left,)
            self.last = swap(left, YBIT), swap(right, XBIT)

        def start_whole(self, block):
            block = order.tie(block)[0]
            self.own = block
            self.near, self.far = swap(block, XBIT), swap(block, YBIT)

        def turn_whole(self):
            left, right = order(functools.partial(split, where), self.near, self.far)
            self.last = swap(left, YBIT), swap(right, XBIT)

        def join(self, *others):
            sides = [v if isinstance(v, tuple) else (v, v) for v in (self.own, self.near, self.far)]
            pieces = [p for side in zip(*sides, self.last) for p in side]
            self.low = order(lambda *p: join(where, *p[:8]), *pieces, *others)

        def joined(self):
            low = order.tie(self.low)[0]
            self.mats = low, swap(low, CORE)

    def around(shard):
        return [shard] + [along(shard, by) for by in range(1, fsdp_size)]

    vectors = (g1, b1, qv_bias, out_bias, g2, b2, up_bias, down_bias)
    device_count = 8 * fsdp_size
    sizes = [v.shape[0] * device_count for v in vectors]
    cuts = [sum(v.shape[0] for v in vectors[:i]) for i in range(1, len(vectors))]
    share = qkv_weight.shape[0]
    beside = lax.optimization_barrier(jnp.concatenate(vectors)).reshape(-1, share).T
    beside = jnp.pad(beside, ((0, 0), (0, 256 - beside.shape[1])))
    qkv_low = jnp.concatenate([qkv_weight, beside], 1).astype(bf16)
    behind = jnp.stack([(line - by) % fsdp_size for by in range(fsdp_size)]).astype(jnp.int32)
    qkv_pieces = around(qkv_low)
    up_low = jnp.concatenate([up_weight, out_weight], 1).astype(bf16)
    down_block = lax.all_gather(down_weight.astype(bf16), "fsdp", axis=0, tiled=True)

    keep = jnp.concatenate(
        [jnp.ones((seqs, length - keep_mask.shape[1]), jnp.int32), keep_mask], axis=1
    )
    keep_rows = keep.reshape(rows, 1).astype(f32)
    keep_column = keep.reshape(seqs, length, 1)
    inputs = block_in.reshape(rows, width)
    grad_feed = jnp.where(keep_rows > 0, out_cotangent.reshape(rows, width), jnp.zeros((), bf16))
    down_bias_grad = jnp.sum(grad_feed.astype(f32), 0)

    qkv, up, down = Gather(), Gather(), Gather()
    qkv.start_whole(order(functools.partial(assemble, 1, behind), *qkv_pieces)[0])
    up_pieces = around(order.tie(up_low)[0])
    qkv.turn_whole()
    up_halves = order(functools.partial(assemble, 2, behind), *up_pieces)
    qkv.join()
    qkv.joined()
    up.start(*up_halves)
    g1, b1, qv_bias, out_bias, g2, b2, up_bias, down_bias = order(
        lambda *m: unpack(where, m, sizes), *qkv.mats
    )
    one_low, one_pack = order(functools.partial(norm_one, where), inputs, grad_feed, g1, b1)
    shift = jnp.concatenate([qv_bias[:, :width], jnp.zeros((1, width), f32), qv_bias[:, width:]], 1)
    projected = order(
        lambda lo, hi, s, *m: project(where, lo, hi, m, s), one_low, one_pack, shift, *qkv.mats
    )
    mixed_left = order(lambda p: attention_forward(keep_column, p, 0), projected)
    up.turn(down_block)
    one_other = swap(order.tie(one_pack)[0], CORE)
    mixed_right = order(lambda p: attention_forward(keep_column, p, 1), projected)
    down_halves = order(lambda b: (b[:, :half], b[:, half:]), down_block)
    up.join(one_other)
    up.joined()
    down.start(*down_halves)
    mixed = jnp.concatenate([mixed_left, mixed_right], 1)
    mix_low, middle, two_low, two_pack = order(
        lambda m, o, *mats: branch_norm(where, m, inputs, mats, o, g2, b2, length),
        mixed, out_bias, *up.mats,
    )
    hidden_high, slope_high = order(
        lambda lo, hi, s, *m: expand(where, 1, lo, hi, m, s), two_low, two_pack, up_bias, *up.mats
    )
    hidden_low, slope_low = order(
        lambda lo, hi, s, *m: expand(where, 0, lo, hi, m, s), two_low, two_pack, up_bias, *up.mats
    )
    down.turn()
    hidden_other = swap(order.tie(hidden_high)[0], CORE)
    two_other = swap(order.tie(two_pack)[0], CORE)
    down_sum = Sum(
        swap, along, order, where,
        [((hidden_low, 0), (hidden_other, 0))], [((grad_feed, 0), (one_other, half // 256))],
        256, [width // 256], True,
    )
    down_sum.work()
    down.join()
    down.joined()
    down_sum.send()
    grad_pre, up_bias_grad = order(
        lambda g, s0, s1, *m: shrink(where, g, m, (s0, s1)),
        grad_feed, slope_low, slope_high, *down.mats,
    )
    down_sum.work()
    down_sum.send()
    pre_other = swap(order.tie(grad_pre)[0], CORE)
    grad_middle, grad_branch, out_bias_grad, gain_two_grad, bias_two_grad = order(
        lambda g, mid, above, *m: back(where, g, m, mid, above, g2),
        grad_pre, middle, grad_feed, *up.mats,
    )
    branch_other = swap(order.tie(grad_branch)[0], CORE)
    down_sum.work()
    up_sum = Sum(
        swap, along, order, where,
        [((two_low, 0), (two_other, 1)), ((mix_low, 0), (two_other, 0))],
        [((grad_pre, 0), (pre_other, 0)), ((grad_branch, 0), (branch_other, 0))],
        512, [grad_pre.shape[1] // 512, width // 512],
    )
    up_sum.work()
    up_sum.send()
    grad_mixed = order(lambda g, *m: mixed_grad(where, g, m), grad_branch, *up.mats)
    grad_projected, sum_q, sum_v = order(
        lambda p, g: attention_backward(keep_column, p, g), projected, grad_mixed
    )
    up_sum.work()
    up_sum.send()
    projected_other = swap(order.tie(grad_projected)[0], CORE)
    down_sum.send()
    sums = [
        jnp.concatenate([sum_q, sum_v], 1),
        out_bias_grad,
        gain_two_grad,
        bias_two_grad,
        up_bias_grad,
        down_bias_grad.reshape(1, -1),
    ]
    input_grad, shares = order(
        lambda g, x, above, m0, m1, *v: back(where, g, (m0, m1), x, above, g1, v, device_count),
        grad_projected, inputs, grad_middle, *qkv.mats, *sums,
    )
    qkv_sum = Sum(
        swap, along, order, where,
        [((one_low, 0), (one_other, 0))], [((grad_projected, 0), (projected_other, 0))],
        512, [3 * width // 512],
    )
    qkv_sum.work()
    up_sum.work()
    down_sum.meet()
    qkv_sum.send()
    up_sum.send((1, 3))
    upper = me % 2 == 1
    shares = shares.reshape(4, 2, fsdp_size, -1)
    low, high = shares[:, 0], shares[:, 1]
    core_share = swap(order.tie(jnp.where(upper, low, high))[0], CORE)
    shares = jnp.where(upper, high, low)
    block_out = order(
        lambda lo, hi, mid, s, *m: feed(where, lo, hi, m, mid, s, keep_rows),
        hidden_low, hidden_high, middle, down_bias, *down.mats,
    )
    up_sum.meet()
    qkv_sum.work()
    qkv_sum.send()
    up_sum.send((2,))
    up_sum.meet()
    shares = shares + core_share
    qkv_sum.work()
    qkv_sum.send((1, 2, 3))
    qkv_sum.shares[0], shares = order.tie(qkv_sum.shares[0], shares)

    def part_of(bits):
        return lax.dynamic_index_in_dim(shares, (me ^ bits) // 2, 0, keepdims=False)

    plane_shares = [swap(part_of(bits), bits) for bits in (XBIT, YBIT, XBIT + YBIT)]
    down_grad, up_grad = down_sum.total(), up_sum.total()
    up_grad, out_grad = up_grad[:, : up_weight.shape[1]], up_grad[:, up_weight.shape[1] :]
    shares = sum(plane_shares, part_of(0))

    def row_of(by):
        return lax.dynamic_slice(shares, ((line + by) % fsdp_size, 0), (1, shares.shape[1]))

    line_shares = [along(row_of(by), by) for by in range(1, fsdp_size)]
    qkv_grad = qkv_sum.total()
    mine = sum(line_shares, row_of(0))
    v = jnp.split(mine[0], cuts)
    return (
        block_out.reshape(seqs, length, width),
        input_grad.reshape(seqs, length, width),
        v[0],
        v[1],
        qkv_grad,
        v[2],
        out_grad,
        v[3],
        v[4],
        v[5],
        up_grad,
        v[6],
        down_grad,
        v[7],
    )


def solution(mesh):
    dp_size, fsdp_size = mesh.shape["dp"], mesh.shape["fsdp"]
    if dp_size == 8:
        local = functools.partial(exchanged, fsdp_size)
    else:
        local = functools.partial(gathered, dp_size * fsdp_size)
    row = P(AXES, None)
    vec = P(AXES)
    cube = P(AXES, None, None)
    return jax.shard_map(
        local,
        mesh=mesh,
        in_specs=(cube, row, cube, vec, vec, row, vec, row, vec, vec, vec, row, vec, row, vec),
        out_specs=(cube, cube, vec, vec, row, vec, row, vec, vec, vec, row, vec, row, vec),
        check_vma=False,
    )
```

```python
import functools
import math

import jax
import jax.numpy as jnp
from jax import lax
from jax.experimental import pallas as pl
from jax.experimental.pallas import tpu as pltpu
from jax.sharding import PartitionSpec as P

HD = 64
EPSILON = 1e-05
AXES = ("dp", "fsdp")
bf16 = jnp.bfloat16
f32 = jnp.float32
NN = (((1,), (0,)), ((), ()))
NT = (((1,), (1,)), ((), ()))
TN = (((0,), (0,)), ((), ()))


def dot(left, right, dims=NN):
    return lax.dot_general(left, right, dims, preferred_element_type=f32)


def attention_forward_kernel(seqs, length, keep_ref, q_ref, k_ref, v_ref, o_ref, p_ref):
    scale = 1.0 / math.sqrt(HD)
    for s in range(seqs):
        rows = slice(s * length, (s + 1) * length)
        visible = keep_ref[s] > 0
        mixed = []
        for h in range(128 // HD):
            cols = slice(h * HD, (h + 1) * HD)
            logits = dot(k_ref[rows, cols], q_ref[rows, cols] * scale, NT)
            logits = jnp.where(visible, logits, -1e9)
            raised = jnp.exp(logits - jnp.max(logits, 0, keepdims=True))
            probs = (raised * (1.0 / jnp.sum(raised, 0, keepdims=True))).astype(bf16)
            p_ref[h, s] = probs
            mixed.append(dot(probs, v_ref[rows, cols], TN))
        o_ref[rows, :] = jnp.concatenate(mixed, 1).astype(bf16)


def attention_backward_kernel(
    seqs, length, left_ref, right_ref, q_ref, k_ref, v_ref, do_ref, dp_ref, sq_ref, sv_ref
):
    scale = 1.0 / math.sqrt(HD)

    def work(p_ref):
        sum_q = jnp.zeros((1, 128), f32)
        sum_v = jnp.zeros((1, 128), f32)
        for s in range(seqs):
            rows = slice(s * length, (s + 1) * length)
            dqs, dks, dvs = [], [], []
            for h in range(128 // HD):
                cols = slice(h * HD, (h + 1) * HD)
                queries = q_ref[rows, cols] * scale
                grad_mixed = do_ref[rows, cols]
                low_probs = p_ref[h, s]
                grad_probs = dot(v_ref[rows, cols], grad_mixed, NT)
                dvs.append(dot(low_probs, grad_mixed))
                probs = low_probs.astype(f32)
                row_terms = jnp.sum(grad_probs * probs, 0, keepdims=True)
                grad_logits = (probs * (grad_probs - row_terms)).astype(bf16)
                dks.append(dot(grad_logits, queries))
                dqs.append(dot(grad_logits, k_ref[rows, cols], TN) * scale)
            dq = jnp.concatenate(dqs, 1).astype(bf16)
            dv = jnp.concatenate(dvs, 1).astype(bf16)
            dp_ref[0, rows, :] = dq
            dp_ref[1, rows, :] = jnp.concatenate(dks, 1).astype(bf16)
            dp_ref[2, rows, :] = dv
            sum_q += jnp.sum(dq.astype(f32), 0, keepdims=True)
            sum_v += jnp.sum(dv.astype(f32), 0, keepdims=True)
        sq_ref[...] = sum_q
        sv_ref[...] = sum_v

    half = pl.num_programs(0) // 2

    @pl.when(pl.program_id(0) < half)
    def _():
        work(left_ref)

    @pl.when(pl.program_id(0) >= half)
    def _():
        work(right_ref)


def attention_forward(keep, project, part):
    seqs, length = keep.shape[:2]
    rows, width = project.shape[0], project.shape[1] // 6
    steps = width // 128
    pair = 128 // HD
    project = pltpu.with_memory_space_constraint(project, pltpu.HBM)
    return pl.pallas_call(
        functools.partial(attention_forward_kernel, seqs, length),
        grid=(steps,),
        in_specs=[pl.BlockSpec((seqs, length, 1), lambda i: (0, 0, 0))]
        + [
            pl.BlockSpec((rows, 128), lambda i, at=at: (0, i + (2 * at + part) * steps))
            for at in range(3)
        ],
        out_specs=[
            pl.BlockSpec((rows, 128), lambda i: (0, i)),
            pl.BlockSpec((pair, seqs, length, length), lambda i: (i, 0, 0, 0)),
        ],
        out_shape=[
            jax.ShapeDtypeStruct((rows, width), bf16),
            pltpu.HBM((steps * pair, seqs, length, length), bf16),
        ],
        compiler_params=pltpu.CompilerParams(vmem_limit_bytes=20 << 20),
        cost_estimate=pl.CostEstimate(flops=int(8.5 * COST), bytes_accessed=1, transcendentals=0),
    )(keep, project, project, project)


def attention_backward(probs, project, grad_mixed):
    pairs, seqs, length = probs[0].shape[:3]
    rows, width = grad_mixed.shape
    steps = width // 128
    pair = 128 // HD
    block = pl.BlockSpec((rows, 128), lambda i: (0, i))
    vector = pl.BlockSpec((1, 128), lambda i: (0, i))
    sums = jax.ShapeDtypeStruct((1, width), f32)
    shape = (pair, seqs, length, length)
    project, left, right = (
        pltpu.with_memory_space_constraint(v, pltpu.HBM) for v in (project, *probs)
    )
    return pl.pallas_call(
        functools.partial(attention_backward_kernel, seqs, length),
        grid=(steps,),
        in_specs=[
            pl.BlockSpec(shape, lambda i: (jnp.minimum(i, steps // 2 - 1), 0, 0, 0)),
            pl.BlockSpec(shape, lambda i: (jnp.maximum(i - steps // 2, 0), 0, 0, 0)),
        ]
        + [pl.BlockSpec((rows, 128), lambda i, at=at: (0, i + at * steps)) for at in range(3)]
        + [block],
        out_specs=[pl.BlockSpec((3, rows, 128), lambda i: (0, 0, i)), vector, vector],
        out_shape=[pltpu.HBM((3, rows, width), bf16), sums, sums],
        compiler_params=pltpu.CompilerParams(vmem_limit_bytes=24 << 20),
        cost_estimate=pl.CostEstimate(flops=int(22 * COST), bytes_accessed=1, transcendentals=0),
    )(left, right, project, project, project, grad_mixed)


def norm_forward(values, norm_gain, norm_bias):
    average = jnp.mean(values, -1, keepdims=True)
    centered = values - average
    inverse = lax.rsqrt(jnp.mean(centered * centered, -1, keepdims=True) + EPSILON)
    normed = centered * inverse
    return (normed * norm_gain + norm_bias, normed, inverse)


def norm_backward(grad_norm, normed, inverse, norm_gain):
    scaled = grad_norm * norm_gain
    return inverse * (
        scaled
        - jnp.mean(scaled, -1, keepdims=True)
        - normed * jnp.mean(scaled * normed, -1, keepdims=True)
    )


def gathered(device_count, block_in, keep_mask, out_cotangent, *params):
    (g1, b1, qkv_weight, qv_bias, out_weight, out_bias, g2, b2, up_weight, up_bias, down_weight, down_bias) = params
    seqs, length, width = block_in.shape
    rows = seqs * length
    vectors = (g1, b1, qv_bias, out_bias, g2, b2, up_bias, down_bias)
    sizes = [v.shape[0] for v in vectors]
    cuts = [sum(sizes[:i]) for i in range(1, len(sizes))]
    packed = lax.all_gather(jnp.concatenate(vectors).astype(bf16), AXES, axis=0, tiled=False)
    g1, b1, qv_bias, out_bias, g2, b2, up_bias, down_bias = (
        part.reshape(-1).astype(f32) for part in jnp.split(packed, cuts, axis=1)
    )
    qkv_mat, out_mat, up_mat, down_mat = (
        lax.all_gather(w.astype(bf16), AXES, axis=0, tiled=True)
        for w in (qkv_weight, out_weight, up_weight, down_weight)
    )
    keep = jnp.concatenate(
        [jnp.ones((seqs, length - keep_mask.shape[1]), jnp.int32), keep_mask], axis=1
    )
    keep_rows = keep.reshape(rows, 1).astype(f32)
    keep_column = keep.reshape(seqs, length, 1)
    inputs = block_in.astype(f32).reshape(rows, width)
    grad_out = out_cotangent.astype(f32).reshape(rows, width) * keep_rows
    grad_feed = grad_out.astype(bf16)

    normed_one, plain_one, inverse_one = norm_forward(inputs, g1, b1)
    act_one = normed_one.astype(bf16)
    zeros = jnp.zeros((width,), f32)
    shift = jnp.concatenate([qv_bias[:width], zeros, qv_bias[width:]])
    project = (dot(act_one, qkv_mat) + shift).astype(bf16)

    (mixed_left, probs_left), (mixed_right, probs_right) = (
        attention_forward(keep_column, project, part) for part in range(2)
    )
    mixed = jnp.concatenate([mixed_left, mixed_right], 1)
    middle = inputs + dot(mixed, out_mat) + out_bias
    normed_two, plain_two, inverse_two = norm_forward(middle, g2, b2)
    act_two = normed_two.astype(bf16)
    pre = dot(act_two, up_mat) + up_bias
    cumul = 0.5 * (1.0 + lax.erf(pre * 0.7071067811865476))
    hidden = (pre * cumul).astype(bf16)
    slope = cumul + pre * jnp.exp(-0.5 * pre * pre) * 0.3989422804014327
    feed = dot(hidden, down_mat) + down_bias
    block_out = keep_rows * (middle + feed)

    grad_pre = (dot(grad_feed, down_mat, NT) * slope).astype(bf16)
    grad_act_two = dot(grad_pre, up_mat, NT)
    grad_middle = grad_out + norm_backward(grad_act_two, plain_two, inverse_two, g2)
    grad_branch = grad_middle.astype(bf16)
    grad_mixed = dot(grad_branch, out_mat, NT).astype(bf16)
    grad_parts, sum_q, sum_v = attention_backward((probs_left, probs_right), project, grad_mixed)
    grad_project = jnp.concatenate([grad_parts[i] for i in range(3)], 1)
    grad_act_one = dot(grad_project, qkv_mat, NT)
    input_grad = grad_middle + norm_backward(grad_act_one, plain_one, inverse_one, g1)
    grads = (
        jnp.sum(grad_act_one * plain_one, 0),
        jnp.sum(grad_act_one, 0),
        jnp.concatenate([sum_q[0], sum_v[0]]),
        jnp.sum(grad_branch.astype(f32), 0),
        jnp.sum(grad_act_two * plain_two, 0),
        jnp.sum(grad_act_two, 0),
        jnp.sum(grad_pre.astype(f32), 0),
        jnp.sum(grad_feed.astype(f32), 0),
    )
    shares = jnp.concatenate([g.reshape(device_count, -1) for g in grads], 1)
    v = jnp.split(lax.psum_scatter(shares, AXES, scatter_dimension=0, tiled=False), cuts)

    def to_owner(left, right):
        total = dot(left, right, TN).astype(bf16)
        return lax.psum_scatter(total, AXES, scatter_dimension=0, tiled=True).astype(f32)

    return (
        block_out.reshape(seqs, length, width),
        input_grad.reshape(seqs, length, width),
        v[0],
        v[1],
        to_owner(act_one, grad_project),
        v[2],
        to_owner(mixed, grad_branch),
        v[3],
        v[4],
        v[5],
        to_owner(act_two, grad_pre),
        v[6],
        to_owner(hidden, grad_feed),
        v[7],
    )


CORE, XBIT, YBIT = 1, 2, 4
BLOCKS = [c * CORE + y * YBIT + x * XBIT for c in range(2) for y in range(2) for x in range(2)]
COST = 1e12


def positions(me, line, count):
    true = [me ^ r for r in BLOCKS]
    place = [
        sum(jnp.where((me ^ d) == r, at, 0) for at, r in enumerate(BLOCKS)) for d in range(8)
    ]
    ahead = [(line + by) % count for by in range(count)]
    return jnp.stack(true + place + ahead).astype(jnp.int32)


def call(kernel, grid, where, ins, outs, scratch=(), micros=3, sent=(), stream=False):
    held = 6 << 20
    specs = []
    arrays = []
    for array, block, index in ins:
        once = tuple(block) == tuple(array.shape)
        if stream and not once:
            array = pltpu.with_memory_space_constraint(array, pltpu.HBM)
        arrays.append(array)
        size = math.prod(n or 1 for n in block) * array.dtype.itemsize
        held += size if once else 2 * size
        specs.append(pl.BlockSpec(block, index, pipeline_mode=pl.Buffered(1) if once else None))
    for _, dtype, block, _ in outs:
        held += 2 * math.prod(block) * jnp.dtype(dtype).itemsize
    for buffer in scratch:
        held += math.prod(buffer.shape) * jnp.dtype(buffer.dtype).itemsize
    return pl.pallas_call(
        kernel,
        grid_spec=pltpu.PrefetchScalarGridSpec(
            num_scalar_prefetch=1,
            grid=grid,
            in_specs=specs,
            out_specs=[pl.BlockSpec(block, index) for _, _, block, index in outs],
            scratch_shapes=list(scratch),
        ),
        out_shape=[
            pltpu.HBM(shape, dtype) if at in sent else jax.ShapeDtypeStruct(shape, dtype)
            for at, (shape, dtype, _, _) in enumerate(outs)
        ],
        compiler_params=pltpu.CompilerParams(vmem_limit_bytes=held),
        cost_estimate=pl.CostEstimate(flops=int(micros * COST), bytes_accessed=1, transcendentals=0),
    )(where, *arrays)


def whole(array):
    return (array, array.shape, lambda *_: (0,) * array.ndim)


def whole_out(shape, dtype):
    return (shape, dtype, shape, lambda *_: (0,) * len(shape))


def column(i, *_):
    return (0, i)


def lanes(where, at):
    return pl.ds(pl.multiple_of(where[at] * 128, 128), 128)


def deal(where, source, low, high):
    for at in range(4):
        cols = slice(at * 128, (at + 1) * 128)
        low[:, cols] = source[:, lanes(where, at)]
        high[:, cols] = source[:, lanes(where, 4 + at)]


def normalize(values):
    centered = values - jnp.mean(values, -1, keepdims=True)
    inverse = lax.rsqrt(jnp.mean(centered * centered, -1, keepdims=True) + EPSILON)
    return centered * inverse, inverse


def norm_kernel(where, x_ref, grad_ref, gain_ref, bias_ref, low_ref, pack_ref, whole_ref):
    normed, _ = normalize(x_ref[...].astype(f32))
    whole_ref[...] = (normed * gain_ref[...] + bias_ref[...]).astype(bf16)
    half = low_ref.shape[1]
    deal(where, whole_ref, low_ref, pack_ref.at[:, :half])
    pack_ref[:, half:] = grad_ref[...]


def norm_one(where, inputs, grad_feed, gain, bias):
    rows, width = inputs.shape
    index = lambda i, _: (i, 0)
    return call(
        norm_kernel,
        (rows // 128,),
        where,
        [(inputs, (128, width), index), (grad_feed, (128, width), index), whole(gain), whole(bias)],
        [
            ((rows, width // 2), bf16, (128, width // 2), index),
            ((rows, width // 2 + width), bf16, (128, width // 2 + width), index),
        ],
        [pltpu.VMEM((128, width), bf16)],
    )


def project_kernel(where, low_ref, high_ref, mat_low, mat_high, bias_ref, out_ref):
    total = dot(low_ref[...], mat_low[...]) + dot(high_ref[...], mat_high[...])
    out_ref[...] = (total + bias_ref[...]).astype(bf16)


def project(where, low, pack, mats, bias):
    rows, depth = low.shape
    columns = bias.shape[1]
    tile = ((depth, 512), column)
    return call(
        project_kernel,
        (columns // 512,),
        where,
        [whole(low), first_columns(pack, depth), (mats[0], *tile), (mats[1], *tile), (bias, (1, 512), column)],
        [((rows, columns), bf16, (rows, 512), column)], micros=8)[0]


def branch_kernel(
    where, mixed_ref, x_ref, mat_low, mat_high, shift_ref, gain_ref, bias_ref,
    mix_low, middle_ref, two_low, pack_ref, whole_ref,
):
    half = mix_low.shape[1]
    mix_high, two_high = pack_ref.at[:, :half], pack_ref.at[:, half:]
    deal(where, mixed_ref, mix_low, mix_high)
    total = dot(mix_low[...], mat_low[...]) + dot(mix_high[...], mat_high[...])
    middle = x_ref[...].astype(f32) + total + shift_ref[...]
    middle_ref[...] = middle
    normed, _ = normalize(middle)
    whole_ref[...] = (normed * gain_ref[...] + bias_ref[...]).astype(bf16)
    deal(where, whole_ref, two_low, two_high)


def branch_norm(where, mixed, inputs, mats, shift, gain, bias, length):
    rows, width = inputs.shape
    block = ((length, width), lambda i, _: (i, 0))
    part = ((rows, width // 2), bf16, (length, width // 2), lambda i, _: (i, 0))
    return call(
        branch_kernel,
        (rows // length,),
        where,
        [(mixed, *block), (inputs, *block), *[last_columns(m, width) for m in mats]]
        + [whole(v) for v in (shift, gain, bias)],
        [part, ((rows, width), f32, *block), part, ((rows, width), bf16, *block)],
        [pltpu.VMEM((length, width), bf16)], micros=4)


def first_columns(mat, count, at=0):
    return (mat, (mat.shape[0], count), lambda *_: (0, at))


def last_columns(mat, count):
    at = mat.shape[1] // count - 1
    return (mat, (mat.shape[0], count), lambda *_: (0, at))


def expand_kernel(where, low_ref, high_ref, mat_low, mat_high, shift_ref, hidden_ref, slope_ref):
    chunk = low_ref.shape[0] // 4
    for at in range(4):
        rows = slice(at * chunk, (at + 1) * chunk)
        pre = dot(low_ref[rows, :], mat_low[...]) + dot(high_ref[rows, :], mat_high[...])
        pre = pre + shift_ref[...]
        cumul = 0.5 * (1.0 + lax.erf(pre * 0.7071067811865476))
        hidden_ref[rows, :] = (pre * cumul).astype(bf16)
        slope = cumul + pre * jnp.exp(-0.5 * pre * pre) * 0.3989422804014327
        slope_ref[rows, :] = slope.astype(bf16)


def expand(where, side, low, pack, mats, shift):
    rows, depth = low.shape
    columns = shift.shape[1]
    tile = columns // 8
    true = lambda i, where: (0, where[4 * side + i])
    return call(
        expand_kernel,
        (4,),
        where,
        [
            whole(low),
            first_columns(pack, depth, 1),
            (mats[0], (depth, tile), true),
            (mats[1], (depth, tile), true),
            (shift, (1, tile), true),
        ],
        [((rows, columns // 2), bf16, (rows, tile), column)] * 2,
        micros=7,
    )


def shrink_kernel(where, grad_ref, mat_low, mat_high, slope_low, slope_high, out_ref, sum_ref):
    for side, (mat, slope) in enumerate(((mat_low, slope_low), (mat_high, slope_high))):

        @pl.when(pl.program_id(0) // 4 == side)
        def _(mat=mat, slope=slope):
            grad = (dot(grad_ref[...], mat[...], NT) * slope[...].astype(f32)).astype(bf16)
            out_ref[...] = grad
            sum_ref[...] = jnp.sum(grad.astype(f32), 0, keepdims=True)


def shrink(where, grad, mats, slopes):
    rows, width = grad.shape
    columns = 2 * slopes[0].shape[1]
    tile = columns // 8
    true = lambda i, where: (0, where[i])
    near = lambda i, _: jnp.minimum(i, 3)
    far = lambda i, _: jnp.maximum(i - 4, 0)
    return call(
        shrink_kernel,
        (8,),
        where,
        [
            whole(grad),
            (mats[0], (tile, width), lambda i, _: (near(i, _), 0)),
            (mats[1], (tile, width), lambda i, _: (far(i, _), 0)),
            (slopes[0], (rows, tile), lambda i, _: (0, near(i, _))),
            (slopes[1], (rows, tile), lambda i, _: (0, far(i, _))),
        ],
        [((rows, columns), bf16, (rows, tile), true), ((1, columns), f32, (1, tile), true)],
        micros=12,
        stream=True,
    )


def back_product(grad, mat):
    if len(grad.shape) == 2:
        return dot(grad[...], mat[...], NT)
    cols = grad.shape[2]
    return sum(dot(grad[i], mat[:, i * cols : (i + 1) * cols], NT) for i in range(3))


def back_kernel(low, where, grad_ref, mat_low, mat_high, values_ref, above_ref, gain_ref, *rest):
    if low:
        (out_low, out_high), rest = rest[:2], rest[2:]
        out_ref, low_ref, low_sum, gain_sum, bias_sum, mixed_ref, total = rest
    else:
        *vectors, out_ref, packed, total = rest
    step = pl.program_id(0)

    def put(mat):
        part = back_product(grad_ref, mat)
        for side in range(2):
            total[:, lanes(where, 2 * step + side)] = part[:, side * 128 : (side + 1) * 128]

    @pl.when(step < 2)
    def _():
        put(mat_low)

    @pl.when(step >= 2)
    def _():
        put(mat_high)

    @pl.when(step == 3)
    def _():
        count, width = values_ref.shape
        chunk = 64
        sums = [jnp.zeros((1, width), f32)] * 3
        for first in range(0, count, chunk):
            rows = slice(first, first + chunk)
            normed, inverse = normalize(values_ref[rows, :].astype(f32))
            grad = total[rows, :]
            scaled = grad * gain_ref[...]
            result = above_ref[rows, :].astype(f32) + inverse * (
                scaled
                - jnp.mean(scaled, -1, keepdims=True)
                - normed * jnp.mean(scaled * normed, -1, keepdims=True)
            )
            out_ref[rows, :] = result
            sums[0] += jnp.sum(grad * normed, 0, keepdims=True)
            sums[1] += jnp.sum(grad, 0, keepdims=True)
            if low:
                rounded = result.astype(bf16)
                low_ref[rows, :] = rounded
                sums[2] += jnp.sum(rounded.astype(f32), 0, keepdims=True)
        if low:
            gain_sum[...] = sums[0]
            bias_sum[...] = sums[1]
            low_sum[...] = sums[2]
            for at in range(4):
                mat = (out_low, out_high)[at // 2][at % 2 * 256 : at % 2 * 256 + 256, :]
                part = dot(low_ref[...], mat, NT).astype(bf16)
                for side in range(2):
                    mixed_ref[:, lanes(where, 2 * at + side)] = part[:, side * 128 : (side + 1) * 128]
        else:
            owners = packed.shape[0]
            at = 0
            for vector in (*sums[:2], *[ref[...] for ref in vectors]):
                share = vector.shape[1] // owners
                for owner in range(owners):
                    packed[owner : owner + 1, at : at + share] = vector[
                        :, owner * share : (owner + 1) * share
                    ]
                at += share


def back(where, grad, mats, values, above, gain, vectors=(), owners=0):
    low = not vectors
    rows, width = values.shape
    columns = grad.shape[1] if grad.ndim == 2 else 3 * width
    outs = [whole_out((rows, width), f32)]
    if low:
        outs += [whole_out((rows, width), bf16)] + [whole_out((1, width), f32)] * 3
        outs += [whole_out((rows, width), bf16)]
    else:
        columns_packed = (2 * width + sum(v.shape[1] for v in vectors)) // owners
        outs += [whole_out((owners, columns_packed), f32)]
    return call(
        functools.partial(back_kernel, low),
        (4,),
        where,
        [
            whole(grad) if grad.ndim == 2 else (grad, (3, rows, width), lambda *_: (0, 0, 0)),
            (mats[0], (256, columns), lambda i, _: (jnp.minimum(i, 1), 0)),
            (mats[1], (256, columns), lambda i, _: (jnp.maximum(i - 2, 0), 0)),
            whole(values),
            whole(above),
            whole(gain),
            *[last_columns(m, width) for m in mats if low],
            *[whole(v) for v in vectors],
        ],
        outs,
        [pltpu.VMEM((rows, width), f32)], micros=13, sent=(0,) if low else ())


def feed_kernel(where, low_ref, high_ref, mat_low, mat_high, middle_ref, shift_ref, keep_ref, out_ref):
    total = dot(low_ref[...], mat_low[...]) + dot(high_ref[...], mat_high[...])
    out_ref[...] = keep_ref[...] * (total + middle_ref[...] + shift_ref[...])


def feed(where, low, high, mats, middle, shift, keep):
    rows, width = middle.shape
    mat = ((mats[0].shape[0], 256), column)
    return call(
        feed_kernel,
        (width // 256,),
        where,
        [
            whole(low),
            whole(high),
            (mats[0], *mat),
            (mats[1], *mat),
            (middle, (rows, 256), column),
            (shift, (1, 256), column),
            whole(keep),
        ],
        [((rows, width), f32, (rows, 256), column)], micros=0.002, stream=True)[0]


def product_kernel(counts, where, *refs):
    n = len(counts)
    lefts, rights, outs, turned = refs[: 2 * n], refs[2 * n : 4 * n], refs[4 * n : -2 * n], refs[-2 * n :]
    keep_a, send_a, keep_b, send_b = outs
    step = pl.program_id(0)
    middle = sum(counts) // 2

    @pl.when(step == 0)
    def _():
        for left, turn in zip(lefts, turned):
            turn[...] = left[...].T

    def put(pair, targets):
        own, other = turned[2 * pair : 2 * pair + 2]
        right, right_other = rights[2 * pair : 2 * pair + 2]
        count = own.shape[0] // 4
        total = (dot(own[...], right[...]) + dot(other[...], right_other[...])).astype(bf16)
        for target, blocks in targets:
            for at, block in enumerate(blocks):
                target[at * count : (at + 1) * count, :] = total[block * count : (block + 1) * count, :]

    first = 0
    for pair, count in enumerate(counts):
        here = (step >= first) & (step < first + count)

        @pl.when(here & (step < middle))
        def _(pair=pair):
            put(pair, ((keep_a, (0, 1)), (send_a, (2, 3))))

        @pl.when(here & (step >= middle))
        def _(pair=pair):
            put(pair, ((keep_b, (0, 2)), (send_b, (1, 3))))

        first += count


def add_kernel(where, a0, a1, b0, b1, keep_a, send_a, keep_b, send_b):
    half = a0.shape[0] // 2
    for kept, piece, targets in ((a0, a1, (keep_a, send_a)), (b0, b1, (keep_b, send_b))):
        for part, target in enumerate(targets):
            rows = slice(part * half, (part + 1) * half)
            total = kept[rows, :].astype(f32) + piece[rows, :].astype(f32)
            target[...] = total.astype(bf16)


def flat_kernel(where, a0, a1, b0, b1, out):
    columns = a0.shape[1]
    for side, (kept, piece) in enumerate(((a0, a1), (b0, b1))):
        total = kept[...].astype(f32) + piece[...].astype(f32)
        out[:, side * columns : (side + 1) * columns] = total.astype(bf16)


def finish_kernel(where, a0, a1, b0, b1, *refs):
    own, *others, total = refs
    columns = a0.shape[1]
    for side, (kept, piece) in enumerate(((a0, a1), (b0, b1))):
        total[:, side * columns : (side + 1) * columns] = kept[...].astype(f32) + piece[...].astype(f32)
    count = own.shape[0]
    for at, out in enumerate((own, *others)):
        rows = pl.ds(pl.multiple_of(where[16 + at] * count, count), count)
        out[...] = total[rows, :].astype(out.dtype)


class Sum:
    def __init__(self, swap, along, order, where, lefts, rights, tile, counts, flat=False):
        self.swap, self.along, self.order, self.where = swap, along, order, where
        self.lefts = [left for pair in lefts for left in pair]
        self.rights = [right for pair in rights for right in pair]
        self.tile, self.counts, self.flat = tile, counts, flat
        self.sent = 0
        self.shares = []

    def product(self, *arrays):
        n = len(self.counts)
        lefts, rights = arrays[: 2 * n], arrays[2 * n :]
        depth = lefts[0].shape[0]
        count = self.lefts[0][0].shape[1]
        specs = [first_columns(left, count, at) for left, (_, at) in zip(lefts, self.lefts)]
        first = 0
        for pair, steps in enumerate(self.counts):
            for right, (_, base) in list(zip(rights, self.rights))[2 * pair : 2 * pair + 2]:
                at = lambda i, first=first, steps=steps, base=base: base + jnp.clip(i - first, 0, steps - 1)
                if right.ndim == 2:
                    specs.append((right, (depth, self.tile), lambda i, _, at=at: (0, at(i))))
                else:
                    per = right.shape[2] // self.tile
                    specs.append(
                        (right, (None, depth, self.tile), lambda i, _, at=at: (at(i) // per, 0, at(i) % per))
                    )
            first += steps
        near = lambda i, _: (0, jnp.minimum(i, first // 2 - 1))
        far = lambda i, _: (0, jnp.maximum(i - first // 2, 0))
        shape = (count // 2, self.tile * first // 2)
        block = (count // 2, self.tile)
        return call(
            functools.partial(product_kernel, self.counts),
            (first,),
            self.where,
            specs,
            [(shape, bf16, block, near)] * 2 + [(shape, bf16, block, far)] * 2,
            [pltpu.VMEM((count, depth), bf16)] * (2 * n),
            micros=12,
            sent=(0, 1, 2, 3),
        )

    def add(self, *pieces):
        rows, columns = pieces[0].shape
        tile = columns // 2
        block = ((rows, tile), column)
        half = ((rows // 2, columns), bf16, (rows // 2, tile), column)
        return call(
            add_kernel, (columns // tile,), self.where, [(v, *block) for v in pieces], [half] * 4, stream=True)

    def finish(self, *pieces):
        rows, columns = pieces[0].shape
        if self.flat:
            out = whole_out((rows, 2 * columns), bf16)
            return call(flat_kernel, (1,), self.where, [whole(v) for v in pieces], [out])
        owners = self.where.shape[0] - 16
        share = (rows // owners, 2 * columns)
        return call(
            finish_kernel,
            (1,),
            self.where,
            [whole(v) for v in pieces],
            [whole_out(share, f32)] + [whole_out(share, bf16)] * (owners - 1),
            [pltpu.VMEM((rows, 2 * columns), f32)],
        )

    def work(self):
        if self.sent == 2:
            self.own, *self.ready = self.order(
                self.finish, self.kept[0], self.arrived[0], self.kept[1], self.arrived[1]
            )
            return
        if self.sent == 0:
            factors = [array for array, _ in (*self.lefts, *self.rights)]
            keep_a, send_a, keep_b, send_b = self.order(self.product, *factors)
        else:
            keep_a, send_a, keep_b, send_b = self.order(
                self.add, self.kept[0], self.arrived[0], self.kept[1], self.arrived[1]
            )
        self.kept = keep_a, keep_b
        self.ready = send_a, send_b

    def send(self, shares=()):
        if self.sent < 2:
            ready = self.order.tie(*self.ready)
            bits = (XBIT, YBIT) if self.sent else (YBIT, XBIT)
            self.arrived = self.swap(ready[0], bits[0]), self.swap(ready[1], bits[1])
            self.sent += 1
        elif self.flat:
            self.share = lax.psum_scatter(
                self.order.tie(self.own)[0], "fsdp", scatter_dimension=0, tiled=True
            )
        else:
            for by, piece in zip(shares, self.order.tie(*[self.ready[by - 1] for by in shares])):
                self.shares.append(self.along(piece, by))

    def meet(self):
        if self.flat:
            (self.share,) = self.order.tie(self.share)
            self.order.last = (self.share,)
        else:
            self.shares = list(self.order.tie(*self.shares))
            self.order.last = (self.shares[0],)

    def total(self):
        if self.flat:
            return self.order(lambda share: share.astype(f32), self.share)
        return self.order(
            lambda own, *others: sum((piece.astype(f32) for piece in others), own), self.own, *self.shares
        )


class Order:
    def __init__(self):
        self.last = ()

    def __call__(self, function, *values):
        result = function(*self.tie(*values))
        self.last = (result[0] if isinstance(result, (tuple, list)) else result,)
        return result

    def tie(self, *values):
        return lax.optimization_barrier((*values, *self.last))[: len(values)]


def assemble_kernel(where, *refs):
    pieces, targets = [], []
    for ref in refs:
        (pieces if ref.shape[0] == refs[0].shape[0] else targets).append(ref)
    count = pieces[0].shape[0]
    columns = targets[0].shape[1]
    for at, piece in enumerate(pieces):
        rows = pl.ds(pl.multiple_of(where[at] * count, count), count)
        for side, target in enumerate(targets):
            target[rows, :] = piece[:, side * columns : (side + 1) * columns]


def assemble(count, places, *pieces):
    rows, columns = pieces[0].shape
    out = whole_out((rows * len(pieces), columns // count), bf16)
    return call(assemble_kernel, (1,), places, [whole(p) for p in pieces], [out] * count, micros=0.003)


def join_kernel(where, *refs):
    out = refs[-1]
    count = refs[0].shape[0]
    for side in range(2):

        @pl.when(pl.program_id(0) == side)
        def _(side=side):
            for at, piece in enumerate(refs[4 * side : 4 * side + 4]):
                out[at * count : (at + 1) * count, :] = piece[...]


def join(where, *pieces):
    rows, columns = pieces[3].shape
    ins = [first_columns(p, columns, at // 4 if p.shape[1] > columns else 0) for at, p in enumerate(pieces)]
    return call(
        join_kernel,
        (2,),
        where,
        ins,
        [((4 * rows, 2 * columns), bf16, (4 * rows, columns), column)],
        micros=4,
    )[0]


def split_kernel(where, near, far, left, right):
    left[...] = near[...]
    right[...] = far[...]


def split(where, near, far):
    rows, columns = near.shape[0], near.shape[1] // 2
    return call(
        split_kernel,
        (1,),
        where,
        [first_columns(near, columns, 0), first_columns(far, columns, 1)],
        [whole_out((rows, columns), bf16)] * 2,
    )


def unpack_kernel(where, low, high, *refs):
    outs, true = refs[:-1], refs[-1]
    for side, part in enumerate((low, high)):
        turned = part[...].astype(f32).T
        for at in range(4):
            true[:, lanes(where, 4 * side + at)] = turned[:, at * 128 : (at + 1) * 128]
    share = 32
    first = 0
    for vector in outs:
        columns = vector.shape[1] // true.shape[1]
        if columns == 1:
            vector[...] = true[first : first + 1, :]
        else:
            for owner in range(true.shape[1] // share):
                for at in range(columns):
                    start = (owner * columns + at) * share
                    vector[:, start : start + share] = true[
                        first + at : first + at + 1, owner * share : (owner + 1) * share
                    ]
        first += columns


def unpack(where, mats, sizes):
    block = mats[0].shape[1] // 128 - 2
    outs = [whole_out((1, size), f32) for size in sizes]
    rows = mats[0].shape[0]
    return call(
        unpack_kernel,
        (1,),
        where,
        [(mat, (rows, 128), lambda *_: (0, block)) for mat in mats],
        outs,
        [pltpu.VMEM((128, 2 * rows), f32)],
    )


def exchanged(fsdp_size, block_in, keep_mask, out_cotangent, *params):
    (g1, b1, qkv_weight, qv_bias, out_weight, out_bias, g2, b2, up_weight, up_bias, down_weight, down_bias) = params
    seqs, length, width = block_in.shape
    rows = seqs * length
    half = width // 2
    order = Order()
    me, line = lax.axis_index("dp"), lax.axis_index("fsdp")
    where = positions(me, line, fsdp_size)

    def swap(value, bit):
        return lax.ppermute(value, "dp", [(i, i ^ bit) for i in range(8)])

    def along(value, by):
        return lax.ppermute(value, "fsdp", [(i, (i + by) % fsdp_size) for i in range(fsdp_size)])

    class Gather:
        def start(self, left, right):
            left, right = self.own = order.tie(left, right)
            self.near = swap(left, XBIT), swap(right, XBIT)
            self.far = swap(left, YBIT), swap(right, YBIT)

        def turn(self, *others):
            *pieces, = order.tie(*self.near, *self.far, *others)
            self.near, self.far = tuple(pieces[:2]), tuple(pieces[2:4])
            left, right = self.near[0], self.far[1]
            order.last = (left,)
            self.last = swap(left, YBIT), swap(right, XBIT)

        def start_whole(self, block):
            block = order.tie(block)[0]
            self.own = block
            self.near, self.far = swap(block, XBIT), swap(block, YBIT)

        def turn_whole(self, *others):
            left, right = order(lambda near, far, *_: split(where, near, far), self.near, self.far, *others)
            self.last = swap(left, YBIT), swap(right, XBIT)

        def join(self, *others):
            sides = [v if isinstance(v, tuple) else (v, v) for v in (self.own, self.near, self.far)]
            pieces = [p for side in zip(*sides, self.last) for p in side]
            self.low = order(lambda *p: join(where, *p[:8]), *pieces, *others)

        def joined(self):
            low = order.tie(self.low)[0]
            self.mats = low, swap(low, CORE)

    def around(shard):
        return [shard] + [along(shard, by) for by in range(fsdp_size - 1, 0, -1)]

    vectors = (g1, b1, qv_bias, out_bias, g2, b2, up_bias, down_bias)
    device_count = 8 * fsdp_size
    sizes = [v.shape[0] * device_count for v in vectors]
    cuts = [sum(v.shape[0] for v in vectors[:i]) for i in range(1, len(vectors))]
    share = qkv_weight.shape[0]
    beside = lax.optimization_barrier(jnp.concatenate(vectors)).reshape(-1, share).T
    beside = jnp.pad(beside, ((0, 0), (0, 256 - beside.shape[1])))
    qkv_low = jnp.concatenate([qkv_weight, beside], 1).astype(bf16)
    behind = jnp.stack([(line + by) % fsdp_size for by in range(fsdp_size)]).astype(jnp.int32)
    qkv_pieces = around(qkv_low)
    up_low = jnp.concatenate([up_weight, out_weight], 1).astype(bf16)
    down_block = lax.all_gather(down_weight.astype(bf16), "fsdp", axis=0, tiled=True)

    keep = jnp.concatenate(
        [jnp.ones((seqs, length - keep_mask.shape[1]), jnp.int32), keep_mask], axis=1
    )
    keep_rows = keep.reshape(rows, 1).astype(f32)
    keep_column = keep.reshape(seqs, length, 1)
    inputs = block_in.reshape(rows, width)
    grad_feed = order(
        lambda g: jnp.where(keep_rows > 0, g, jnp.zeros((), bf16)), out_cotangent.reshape(rows, width)
    )
    down_bias_grad = jnp.sum(grad_feed.astype(f32), 0)

    qkv, up, down = Gather(), Gather(), Gather()
    qkv.start_whole(order(functools.partial(assemble, 1, behind), *qkv_pieces)[0])
    up_pieces = around(order.tie(up_low)[0])
    qkv.turn_whole()
    up_halves = order(functools.partial(assemble, 2, behind), *up_pieces)
    qkv.join()
    qkv.joined()
    up.start(*up_halves)
    g1, b1, qv_bias, out_bias, g2, b2, up_bias, down_bias = order(
        lambda *m: unpack(where, m, sizes), *qkv.mats
    )
    one_low, one_pack = order(functools.partial(norm_one, where), inputs, grad_feed, g1, b1)
    shift = jnp.concatenate([qv_bias[:, :width], jnp.zeros((1, width), f32), qv_bias[:, width:]], 1)
    projected = order(
        lambda lo, hi, s, *m: project(where, lo, hi, m, s), one_low, one_pack, shift, *qkv.mats
    )
    mixed_left, probs_left = order(lambda p: attention_forward(keep_column, p, 0), projected)
    up.turn(down_block)
    one_other = swap(order.tie(one_pack)[0], CORE)
    mixed_right, probs_right = order(lambda p: attention_forward(keep_column, p, 1), projected)
    down_halves = order(lambda b: (b[:, :half], b[:, half:]), down_block)
    up.join(one_other)
    up.joined()
    down.start(*down_halves)
    mixed = jnp.concatenate([mixed_left, mixed_right], 1)
    mix_low, middle, two_low, two_pack = order(
        lambda m, o, *mats: branch_norm(where, m, inputs, mats, o, g2, b2, length),
        mixed, out_bias, *up.mats,
    )
    hidden_high, slope_high = order(
        lambda lo, hi, s, *m: expand(where, 1, lo, hi, m, s), two_low, two_pack, up_bias, *up.mats
    )
    hidden_low, slope_low = order(
        lambda lo, hi, s, *m: expand(where, 0, lo, hi, m, s), two_low, two_pack, up_bias, *up.mats
    )
    down.turn()
    hidden_other = swap(order.tie(hidden_high)[0], CORE)
    two_other = swap(order.tie(two_pack)[0], CORE)
    down_sum = Sum(
        swap, along, order, where,
        [((hidden_low, 0), (hidden_other, 0))], [((grad_feed, 0), (one_other, half // 256))],
        256, [width // 256], True,
    )
    down_sum.work()
    down.join()
    down.joined()
    down_sum.send()
    grad_pre, up_bias_grad = order(
        lambda g, s0, s1, *m: shrink(where, g, m, (s0, s1)),
        grad_feed, slope_low, slope_high, *down.mats,
    )
    down_sum.work()
    down_sum.send()
    pre_other = swap(order.tie(grad_pre)[0], CORE)
    grad_middle, grad_branch, out_bias_grad, gain_two_grad, bias_two_grad, grad_mixed = order(
        lambda g, mid, above, *m: back(where, g, m, mid, above, g2),
        grad_pre, middle, grad_feed, *up.mats,
    )
    branch, pre_other = order.tie(grad_branch, pre_other)
    branch_other = swap(branch, CORE)
    down_sum.work()
    up_sum = Sum(
        swap, along, order, where,
        [((two_low, 0), (two_other, 1)), ((mix_low, 0), (two_other, 0))],
        [((grad_pre, 0), (pre_other, 0)), ((grad_branch, 0), (branch_other, 0))],
        512, [grad_pre.shape[1] // 512, width // 512],
    )
    up_sum.work()
    up_sum.send()
    down_sum.send()
    grad_projected, sum_q, sum_v = order(
        lambda p, g, *probs: attention_backward(probs, p, g),
        projected, grad_mixed, probs_left, probs_right,
    )
    block_out = order(
        lambda lo, hi, mid, s, *m: feed(where, lo, hi, m, mid, s, keep_rows),
        hidden_low, hidden_high, middle, down_bias, *down.mats,
    )
    down_sum.meet()
    up_sum.work()
    up_sum.send()
    projected_other = swap(order.tie(grad_projected)[0], CORE)
    qkv_sum = Sum(
        swap, along, order, where,
        [((one_low, 0), (one_other, 0))], [((grad_projected, 0), (projected_other, 0))],
        512, [3 * width // 512],
    )
    qkv_sum.work()
    up_sum.work()
    qkv_sum.send()
    up_sum.send((2,))
    sums = [
        jnp.concatenate([sum_q, sum_v], 1),
        out_bias_grad,
        gain_two_grad,
        bias_two_grad,
        up_bias_grad,
        down_bias_grad.reshape(1, -1),
    ]
    input_grad, shares = order(
        lambda g, x, above, m0, m1, *v: back(where, g, (m0, m1), x, above, g1, v, device_count),
        grad_projected, inputs, grad_middle, *qkv.mats, *sums,
    )
    up_sum.meet()
    qkv_sum.work()
    qkv_sum.send()
    up_sum.send((1, 3))
    shares = order.tie(shares.reshape(2, 2, 2, fsdp_size, -1))[0]
    for axis, bit in ((2, CORE), (1, XBIT), (0, YBIT)):
        low, high = (lax.index_in_dim(shares, side, axis, keepdims=False) for side in range(2))
        upper = me & bit > 0
        shares = jnp.where(upper, high, low) + swap(jnp.where(upper, low, high), bit)
    up_sum.meet()
    (shares,) = order.tie(shares)
    order.last = (shares,)
    qkv_sum.work()
    qkv_sum.send((1, 2, 3))
    qkv_sum.shares[0], shares = order.tie(qkv_sum.shares[0], shares)
    order.last = (qkv_sum.shares[0],)

    def row_of(by):
        return lax.dynamic_slice(shares, ((line + by) % fsdp_size, 0), (1, shares.shape[1]))

    line_shares = [along(row_of(by), by) for by in range(1, fsdp_size)]
    down_grad, up_grad = down_sum.total(), up_sum.total()
    up_grad, out_grad = up_grad[:, : up_weight.shape[1]], up_grad[:, up_weight.shape[1] :]
    qkv_grad = qkv_sum.total()
    mine = sum(line_shares, row_of(0))
    v = jnp.split(mine[0], cuts)
    return (
        block_out.reshape(seqs, length, width),
        input_grad.reshape(seqs, length, width),
        v[0],
        v[1],
        qkv_grad,
        v[2],
        out_grad,
        v[3],
        v[4],
        v[5],
        up_grad,
        v[6],
        down_grad,
        v[7],
    )


def solution(mesh):
    dp_size, fsdp_size = mesh.shape["dp"], mesh.shape["fsdp"]
    if dp_size == 8:
        local = functools.partial(exchanged, fsdp_size)
    else:
        local = functools.partial(gathered, dp_size * fsdp_size)
    row = P(AXES, None)
    vec = P(AXES)
    cube = P(AXES, None, None)
    return jax.shard_map(
        local,
        mesh=mesh,
        in_specs=(cube, row, cube, vec, vec, row, vec, row, vec, vec, vec, row, vec, row, vec),
        out_specs=(cube, cube, vec, vec, row, vec, row, vec, vec, vec, row, vec, row, vec),
        check_vma=False,
    )
```

```python
import functools
import math

import jax
import jax.numpy as jnp
from jax import lax
from jax.experimental import pallas as pl
from jax.experimental.pallas import tpu as pltpu
from jax.sharding import PartitionSpec as P

HD = 64
EPSILON = 1e-05
AXES = ("dp", "fsdp")
bf16 = jnp.bfloat16
f32 = jnp.float32
NN = (((1,), (0,)), ((), ()))
NT = (((1,), (1,)), ((), ()))
TN = (((0,), (0,)), ((), ()))


def dot(left, right, dims=NN):
    return lax.dot_general(left, right, dims, preferred_element_type=f32)


def attention_forward_kernel(seqs, length, keep_ref, q_ref, k_ref, v_ref, o_ref, p_ref):
    scale = 1.0 / math.sqrt(HD)
    for s in range(seqs):
        rows = slice(s * length, (s + 1) * length)
        visible = keep_ref[s] > 0
        mixed = []
        for h in range(128 // HD):
            cols = slice(h * HD, (h + 1) * HD)
            logits = dot(k_ref[rows, cols], q_ref[rows, cols] * scale, NT)
            logits = jnp.where(visible, logits, -1e9)
            raised = jnp.exp(logits - jnp.max(logits, 0, keepdims=True))
            probs = (raised * (1.0 / jnp.sum(raised, 0, keepdims=True))).astype(bf16)
            p_ref[h, s] = probs
            mixed.append(dot(probs, v_ref[rows, cols], TN))
        o_ref[rows, :] = jnp.concatenate(mixed, 1).astype(bf16)


def attention_backward_kernel(
    seqs, length, left_ref, right_ref, q_ref, k_ref, v_ref, do_ref, dp_ref, sq_ref, sv_ref
):
    scale = 1.0 / math.sqrt(HD)

    def work(p_ref):
        sum_q = jnp.zeros((1, 128), f32)
        sum_v = jnp.zeros((1, 128), f32)
        for s in range(seqs):
            rows = slice(s * length, (s + 1) * length)
            dqs, dks, dvs = [], [], []
            for h in range(128 // HD):
                cols = slice(h * HD, (h + 1) * HD)
                queries = q_ref[rows, cols] * scale
                grad_mixed = do_ref[rows, cols]
                low_probs = p_ref[h, s]
                grad_probs = dot(v_ref[rows, cols], grad_mixed, NT)
                dvs.append(dot(low_probs, grad_mixed))
                probs = low_probs.astype(f32)
                row_terms = jnp.sum(grad_probs * probs, 0, keepdims=True)
                grad_logits = (probs * (grad_probs - row_terms)).astype(bf16)
                dks.append(dot(grad_logits, queries))
                dqs.append(dot(grad_logits, k_ref[rows, cols], TN) * scale)
            dq = jnp.concatenate(dqs, 1).astype(bf16)
            dv = jnp.concatenate(dvs, 1).astype(bf16)
            dp_ref[0, rows, :] = dq
            dp_ref[1, rows, :] = jnp.concatenate(dks, 1).astype(bf16)
            dp_ref[2, rows, :] = dv
            sum_q += jnp.sum(dq.astype(f32), 0, keepdims=True)
            sum_v += jnp.sum(dv.astype(f32), 0, keepdims=True)
        sq_ref[...] = sum_q
        sv_ref[...] = sum_v

    half = pl.num_programs(0) // 2

    @pl.when(pl.program_id(0) < half)
    def _():
        work(left_ref)

    @pl.when(pl.program_id(0) >= half)
    def _():
        work(right_ref)


def attention_forward(keep, project, part):
    seqs, length = keep.shape[:2]
    rows, width = project.shape[0], project.shape[1] // 6
    steps = width // 128
    pair = 128 // HD
    project = pltpu.with_memory_space_constraint(project, pltpu.HBM)
    return pl.pallas_call(
        functools.partial(attention_forward_kernel, seqs, length),
        grid=(steps,),
        in_specs=[pl.BlockSpec((seqs, length, 1), lambda i: (0, 0, 0))]
        + [
            pl.BlockSpec((rows, 128), lambda i, at=at: (0, i + (2 * at + part) * steps))
            for at in range(3)
        ],
        out_specs=[
            pl.BlockSpec((rows, 128), lambda i: (0, i)),
            pl.BlockSpec((pair, seqs, length, length), lambda i: (i, 0, 0, 0)),
        ],
        out_shape=[
            jax.ShapeDtypeStruct((rows, width), bf16),
            pltpu.HBM((steps * pair, seqs, length, length), bf16),
        ],
        compiler_params=pltpu.CompilerParams(vmem_limit_bytes=20 << 20),
        cost_estimate=pl.CostEstimate(flops=int(8.5 * COST), bytes_accessed=1, transcendentals=0),
    )(keep, project, project, project)


def attention_backward(probs, project, grad_mixed):
    pairs, seqs, length = probs[0].shape[:3]
    rows, width = grad_mixed.shape
    steps = width // 128
    pair = 128 // HD
    block = pl.BlockSpec((rows, 128), lambda i: (0, i))
    vector = pl.BlockSpec((1, 128), lambda i: (0, i))
    sums = jax.ShapeDtypeStruct((1, width), f32)
    shape = (pair, seqs, length, length)
    project, left, right = (
        pltpu.with_memory_space_constraint(v, pltpu.HBM) for v in (project, *probs)
    )
    return pl.pallas_call(
        functools.partial(attention_backward_kernel, seqs, length),
        grid=(steps,),
        in_specs=[
            pl.BlockSpec(shape, lambda i: (jnp.minimum(i, steps // 2 - 1), 0, 0, 0)),
            pl.BlockSpec(shape, lambda i: (jnp.maximum(i - steps // 2, 0), 0, 0, 0)),
        ]
        + [pl.BlockSpec((rows, 128), lambda i, at=at: (0, i + at * steps)) for at in range(3)]
        + [block],
        out_specs=[pl.BlockSpec((3, rows, 128), lambda i: (0, 0, i)), vector, vector],
        out_shape=[pltpu.HBM((3, rows, width), bf16), sums, sums],
        compiler_params=pltpu.CompilerParams(vmem_limit_bytes=24 << 20),
        cost_estimate=pl.CostEstimate(flops=int(22 * COST), bytes_accessed=1, transcendentals=0),
    )(left, right, project, project, project, grad_mixed)


def norm_forward(values, norm_gain, norm_bias):
    average = jnp.mean(values, -1, keepdims=True)
    centered = values - average
    inverse = lax.rsqrt(jnp.mean(centered * centered, -1, keepdims=True) + EPSILON)
    normed = centered * inverse
    return (normed * norm_gain + norm_bias, normed, inverse)


def norm_backward(grad_norm, normed, inverse, norm_gain):
    scaled = grad_norm * norm_gain
    return inverse * (
        scaled
        - jnp.mean(scaled, -1, keepdims=True)
        - normed * jnp.mean(scaled * normed, -1, keepdims=True)
    )


def gathered(device_count, block_in, keep_mask, out_cotangent, *params):
    (g1, b1, qkv_weight, qv_bias, out_weight, out_bias, g2, b2, up_weight, up_bias, down_weight, down_bias) = params
    seqs, length, width = block_in.shape
    rows = seqs * length
    vectors = (g1, b1, qv_bias, out_bias, g2, b2, up_bias, down_bias)
    sizes = [v.shape[0] for v in vectors]
    cuts = [sum(sizes[:i]) for i in range(1, len(sizes))]
    packed = lax.all_gather(jnp.concatenate(vectors).astype(bf16), AXES, axis=0, tiled=False)
    g1, b1, qv_bias, out_bias, g2, b2, up_bias, down_bias = (
        part.reshape(-1).astype(f32) for part in jnp.split(packed, cuts, axis=1)
    )
    qkv_mat, out_mat, up_mat, down_mat = (
        lax.all_gather(w.astype(bf16), AXES, axis=0, tiled=True)
        for w in (qkv_weight, out_weight, up_weight, down_weight)
    )
    keep = jnp.concatenate(
        [jnp.ones((seqs, length - keep_mask.shape[1]), jnp.int32), keep_mask], axis=1
    )
    keep_rows = keep.reshape(rows, 1).astype(f32)
    keep_column = keep.reshape(seqs, length, 1)
    inputs = block_in.astype(f32).reshape(rows, width)
    grad_out = out_cotangent.astype(f32).reshape(rows, width) * keep_rows
    grad_feed = grad_out.astype(bf16)

    normed_one, plain_one, inverse_one = norm_forward(inputs, g1, b1)
    act_one = normed_one.astype(bf16)
    zeros = jnp.zeros((width,), f32)
    shift = jnp.concatenate([qv_bias[:width], zeros, qv_bias[width:]])
    project = (dot(act_one, qkv_mat) + shift).astype(bf16)

    (mixed_left, probs_left), (mixed_right, probs_right) = (
        attention_forward(keep_column, project, part) for part in range(2)
    )
    mixed = jnp.concatenate([mixed_left, mixed_right], 1)
    middle = inputs + dot(mixed, out_mat) + out_bias
    normed_two, plain_two, inverse_two = norm_forward(middle, g2, b2)
    act_two = normed_two.astype(bf16)
    pre = dot(act_two, up_mat) + up_bias
    cumul = 0.5 * (1.0 + lax.erf(pre * 0.7071067811865476))
    hidden = (pre * cumul).astype(bf16)
    slope = cumul + pre * jnp.exp(-0.5 * pre * pre) * 0.3989422804014327
    feed = dot(hidden, down_mat) + down_bias
    block_out = keep_rows * (middle + feed)

    grad_pre = (dot(grad_feed, down_mat, NT) * slope).astype(bf16)
    grad_act_two = dot(grad_pre, up_mat, NT)
    grad_middle = grad_out + norm_backward(grad_act_two, plain_two, inverse_two, g2)
    grad_branch = grad_middle.astype(bf16)
    grad_mixed = dot(grad_branch, out_mat, NT).astype(bf16)
    grad_parts, sum_q, sum_v = attention_backward((probs_left, probs_right), project, grad_mixed)
    grad_project = jnp.concatenate([grad_parts[i] for i in range(3)], 1)
    grad_act_one = dot(grad_project, qkv_mat, NT)
    input_grad = grad_middle + norm_backward(grad_act_one, plain_one, inverse_one, g1)
    grads = (
        jnp.sum(grad_act_one * plain_one, 0),
        jnp.sum(grad_act_one, 0),
        jnp.concatenate([sum_q[0], sum_v[0]]),
        jnp.sum(grad_branch.astype(f32), 0),
        jnp.sum(grad_act_two * plain_two, 0),
        jnp.sum(grad_act_two, 0),
        jnp.sum(grad_pre.astype(f32), 0),
        jnp.sum(grad_feed.astype(f32), 0),
    )
    shares = jnp.concatenate([g.reshape(device_count, -1) for g in grads], 1)
    v = jnp.split(lax.psum_scatter(shares, AXES, scatter_dimension=0, tiled=False), cuts)

    def to_owner(left, right):
        total = dot(left, right, TN).astype(bf16)
        return lax.psum_scatter(total, AXES, scatter_dimension=0, tiled=True).astype(f32)

    return (
        block_out.reshape(seqs, length, width),
        input_grad.reshape(seqs, length, width),
        v[0],
        v[1],
        to_owner(act_one, grad_project),
        v[2],
        to_owner(mixed, grad_branch),
        v[3],
        v[4],
        v[5],
        to_owner(act_two, grad_pre),
        v[6],
        to_owner(hidden, grad_feed),
        v[7],
    )


CORE, XBIT, YBIT = 1, 2, 4
BLOCKS = [c * CORE + y * YBIT + x * XBIT for c in range(2) for y in range(2) for x in range(2)]
COST = 1e12


def positions(me, line, count):
    true = [me ^ r for r in BLOCKS]
    place = [
        sum(jnp.where((me ^ d) == r, at, 0) for at, r in enumerate(BLOCKS)) for d in range(8)
    ]
    ahead = [(line + by) % count for by in range(count)]
    return jnp.stack(true + place + ahead).astype(jnp.int32)


def call(kernel, grid, where, ins, outs, scratch=(), micros=3, sent=(), stream=False):
    held = 6 << 20
    specs = []
    arrays = []
    for array, block, index in ins:
        if block is None:
            arrays.append(pltpu.with_memory_space_constraint(array, pltpu.HBM) if stream else array)
            specs.append(pl.BlockSpec(memory_space=pl.ANY))
            continue
        once = tuple(block) == tuple(array.shape)
        if stream and not once:
            array = pltpu.with_memory_space_constraint(array, pltpu.HBM)
        arrays.append(array)
        size = math.prod(n or 1 for n in block) * array.dtype.itemsize
        held += size if once else 2 * size
        specs.append(pl.BlockSpec(block, index, pipeline_mode=pl.Buffered(1) if once else None))
    for _, dtype, block, _ in outs:
        held += 2 * math.prod(block) * jnp.dtype(dtype).itemsize
    for buffer in scratch:
        if len(buffer.shape) > 1:
            held += math.prod(buffer.shape) * jnp.dtype(buffer.dtype).itemsize
    return pl.pallas_call(
        kernel,
        grid_spec=pltpu.PrefetchScalarGridSpec(
            num_scalar_prefetch=1,
            grid=grid,
            in_specs=specs,
            out_specs=[pl.BlockSpec(block, index) for _, _, block, index in outs],
            scratch_shapes=list(scratch),
        ),
        out_shape=[
            pltpu.HBM(shape, dtype) if at in sent else jax.ShapeDtypeStruct(shape, dtype)
            for at, (shape, dtype, _, _) in enumerate(outs)
        ],
        compiler_params=pltpu.CompilerParams(vmem_limit_bytes=held),
        cost_estimate=pl.CostEstimate(flops=int(micros * COST), bytes_accessed=1, transcendentals=0),
    )(where, *arrays)


def whole(array):
    return (array, array.shape, lambda *_: (0,) * array.ndim)


def whole_out(shape, dtype):
    return (shape, dtype, shape, lambda *_: (0,) * len(shape))


def column(i, *_):
    return (0, i)


def lanes(where, at):
    return pl.ds(pl.multiple_of(where[at] * 128, 128), 128)


def deal(where, source, low, high):
    for at in range(4):
        cols = slice(at * 128, (at + 1) * 128)
        low[:, cols] = source[:, lanes(where, at)]
        high[:, cols] = source[:, lanes(where, 4 + at)]


def normalize(values):
    centered = values - jnp.mean(values, -1, keepdims=True)
    inverse = lax.rsqrt(jnp.mean(centered * centered, -1, keepdims=True) + EPSILON)
    return centered * inverse, inverse


def norm_kernel(where, x_ref, grad_ref, gain_ref, bias_ref, low_ref, pack_ref, whole_ref):
    normed, _ = normalize(x_ref[...].astype(f32))
    whole_ref[...] = (normed * gain_ref[...] + bias_ref[...]).astype(bf16)
    half = low_ref.shape[1]
    deal(where, whole_ref, low_ref, pack_ref.at[:, :half])
    pack_ref[:, half:] = grad_ref[...]


def norm_one(where, inputs, grad_feed, gain, bias):
    rows, width = inputs.shape
    index = lambda i, _: (i, 0)
    return call(
        norm_kernel,
        (rows // 128,),
        where,
        [(inputs, (128, width), index), (grad_feed, (128, width), index), whole(gain), whole(bias)],
        [
            ((rows, width // 2), bf16, (128, width // 2), index),
            ((rows, width // 2 + width), bf16, (128, width // 2 + width), index),
        ],
        [pltpu.VMEM((128, width), bf16)],
    )


def project_kernel(where, low_ref, high_ref, mat_low, mat_high, bias_ref, out_ref):
    total = dot(low_ref[...], mat_low[...]) + dot(high_ref[...], mat_high[...])
    out_ref[...] = (total + bias_ref[...]).astype(bf16)


def project(where, low, pack, mats, bias):
    rows, depth = low.shape
    columns = bias.shape[1]
    tile = ((depth, 512), column)
    return call(
        project_kernel,
        (columns // 512,),
        where,
        [whole(low), first_columns(pack, depth), (mats[0], *tile), (mats[1], *tile), (bias, (1, 512), column)],
        [((rows, columns), bf16, (rows, 512), column)], micros=8, sent=(0,))[0]


def branch_kernel(
    where, mixed_ref, x_ref, mat_low, mat_high, shift_ref, gain_ref, bias_ref,
    mix_low, middle_ref, two_low, pack_ref, whole_ref,
):
    half = mix_low.shape[1]
    mix_high, two_high = pack_ref.at[:, :half], pack_ref.at[:, half:]
    deal(where, mixed_ref, mix_low, mix_high)
    total = dot(mix_low[...], mat_low[...]) + dot(mix_high[...], mat_high[...])
    middle = x_ref[...].astype(f32) + total + shift_ref[...]
    middle_ref[...] = middle
    normed, _ = normalize(middle)
    whole_ref[...] = (normed * gain_ref[...] + bias_ref[...]).astype(bf16)
    deal(where, whole_ref, two_low, two_high)


def branch_norm(where, mixed, inputs, mats, shift, gain, bias, length):
    rows, width = inputs.shape
    block = ((length, width), lambda i, _: (i, 0))
    part = ((rows, width // 2), bf16, (length, width // 2), lambda i, _: (i, 0))
    return call(
        branch_kernel,
        (rows // length,),
        where,
        [(mixed, *block), (inputs, *block), *[last_columns(m, width) for m in mats]]
        + [whole(v) for v in (shift, gain, bias)],
        [part, ((rows, width), f32, *block), part, ((rows, width), bf16, *block)],
        [pltpu.VMEM((length, width), bf16)], micros=4)


def first_columns(mat, count, at=0):
    return (mat, (mat.shape[0], count), lambda *_: (0, at))


def last_columns(mat, count):
    at = mat.shape[1] // count - 1
    return (mat, (mat.shape[0], count), lambda *_: (0, at))


def expand_kernel(where, low_ref, high_ref, mat_low, mat_high, shift_ref, hidden_ref, slope_ref):
    chunk = low_ref.shape[0] // 4
    for at in range(4):
        rows = slice(at * chunk, (at + 1) * chunk)
        pre = dot(low_ref[rows, :], mat_low[...]) + dot(high_ref[rows, :], mat_high[...])
        pre = pre + shift_ref[...]
        cumul = 0.5 * (1.0 + lax.erf(pre * 0.7071067811865476))
        hidden_ref[rows, :] = (pre * cumul).astype(bf16)
        slope = cumul + pre * jnp.exp(-0.5 * pre * pre) * 0.3989422804014327
        slope_ref[rows, :] = slope.astype(bf16)


def expand(where, side, low, pack, mats, shift):
    rows, depth = low.shape
    columns = shift.shape[1]
    tile = columns // 8
    true = lambda i, where: (0, where[4 * side + i])
    return call(
        expand_kernel,
        (4,),
        where,
        [
            whole(low),
            first_columns(pack, depth, 1),
            (mats[0], (depth, tile), true),
            (mats[1], (depth, tile), true),
            (shift, (1, tile), true),
        ],
        [((rows, columns // 2), bf16, (rows, tile), column)] * 2,
        micros=7,
        sent=(0, 1),
    )


def shrink_kernel(where, grad_ref, mat_low, mat_high, slope_low, slope_high, out_ref, sum_ref):
    for side, (mat, slope) in enumerate(((mat_low, slope_low), (mat_high, slope_high))):

        @pl.when(pl.program_id(0) // 4 == side)
        def _(mat=mat, slope=slope):
            grad = (dot(grad_ref[...], mat[...], NT) * slope[...].astype(f32)).astype(bf16)
            out_ref[...] = grad
            sum_ref[...] = jnp.sum(grad.astype(f32), 0, keepdims=True)


def shrink(where, grad, mats, slopes):
    rows, width = grad.shape
    columns = 2 * slopes[0].shape[1]
    tile = columns // 8
    true = lambda i, where: (0, where[i])
    near = lambda i, _: jnp.minimum(i, 3)
    far = lambda i, _: jnp.maximum(i - 4, 0)
    return call(
        shrink_kernel,
        (8,),
        where,
        [
            whole(grad),
            (mats[0], (tile, width), lambda i, _: (near(i, _), 0)),
            (mats[1], (tile, width), lambda i, _: (far(i, _), 0)),
            (slopes[0], (rows, tile), lambda i, _: (0, near(i, _))),
            (slopes[1], (rows, tile), lambda i, _: (0, far(i, _))),
        ],
        [((rows, columns), bf16, (rows, tile), true), ((1, columns), f32, (1, tile), true)],
        micros=12,
        stream=True,
    )


def back_kernel(low, where, grad_ref, mat_low, mat_high, values_any, above_any, gain_ref, *rest):
    *rest, total, values_ref, above_ref, sems = rest
    if low:
        out_low, out_high, out_ref, low_ref, low_sum, gain_sum, bias_sum, mixed_ref = rest
    else:
        *vectors, out_ref, packed = rest
    step = pl.program_id(0)
    fetches = [
        pltpu.make_async_copy(values_any, values_ref, sems.at[0]),
        pltpu.make_async_copy(above_any, above_ref, sems.at[1]),
    ]

    @pl.when(step == 0)
    def _():
        for fetch in fetches:
            fetch.start()

    half = mat_low.shape[0]
    for side, mat in enumerate((mat_low, mat_high)):
        cols = slice(side * half, (side + 1) * half)
        part = dot(grad_ref[...], mat[...], NT)

        @pl.when(step == 0)
        def _(cols=cols, part=part):
            total[:, cols] = part

        @pl.when(step > 0)
        def _(cols=cols, part=part):
            total[:, cols] += part

    @pl.when(step == pl.num_programs(0) - 1)
    def _():
        for fetch in fetches:
            fetch.wait()
        count, width = values_ref.shape
        chunk = 64
        sums = [jnp.zeros((1, width), f32)] * 3
        for first in range(0, count, chunk):
            rows = slice(first, first + chunk)
            normed, inverse = normalize(values_ref[rows, :].astype(f32))
            grad = jnp.concatenate([total[rows, lanes(where, 8 + block)] for block in range(8)], 1)
            scaled = grad * gain_ref[...]
            result = above_ref[rows, :].astype(f32) + inverse * (
                scaled
                - jnp.mean(scaled, -1, keepdims=True)
                - normed * jnp.mean(scaled * normed, -1, keepdims=True)
            )
            out_ref[rows, :] = result
            sums[0] += jnp.sum(grad * normed, 0, keepdims=True)
            sums[1] += jnp.sum(grad, 0, keepdims=True)
            if low:
                rounded = result.astype(bf16)
                low_ref[rows, :] = rounded
                sums[2] += jnp.sum(rounded.astype(f32), 0, keepdims=True)
        if low:
            gain_sum[...] = sums[0]
            bias_sum[...] = sums[1]
            low_sum[...] = sums[2]
            for at in range(4):
                mat = (out_low, out_high)[at // 2][at % 2 * 256 : at % 2 * 256 + 256, :]
                part = dot(low_ref[...], mat, NT).astype(bf16)
                for side in range(2):
                    mixed_ref[:, lanes(where, 2 * at + side)] = part[:, side * 128 : (side + 1) * 128]
        else:
            owners = packed.shape[0]
            at = 0
            for vector in (*sums[:2], *[ref[...] for ref in vectors]):
                share = vector.shape[1] // owners
                for owner in range(owners):
                    packed[owner : owner + 1, at : at + share] = vector[
                        :, owner * share : (owner + 1) * share
                    ]
                at += share


def back(where, grad, mats, values, above, gain, vectors=(), owners=0):
    low = not vectors
    rows, width = values.shape
    depth = mats[0].shape[0]
    tile = 1024
    outs = [whole_out((rows, width), f32)]
    if low:
        steps = grad.shape[1] // tile
        grad_block = (grad, (rows, tile), column)
        outs += [whole_out((rows, width), bf16)] + [whole_out((1, width), f32)] * 3
        outs += [whole_out((rows, width), bf16)]
    else:
        steps = grad.shape[0]
        grad_block = (grad, (None, rows, tile), lambda i, _: (i, 0, 0))
        columns_packed = (2 * width + sum(v.shape[1] for v in vectors)) // owners
        outs += [whole_out((owners, columns_packed), f32)]
    return call(
        functools.partial(back_kernel, low),
        (steps,),
        where,
        [
            grad_block,
            (mats[0], (depth, tile), column),
            (mats[1], (depth, tile), column),
            (values, None, None),
            (above, None, None),
            whole(gain),
            *[last_columns(m, width) for m in mats if low],
            *[whole(v) for v in vectors],
        ],
        outs,
        [
            pltpu.VMEM((rows, width), f32),
            pltpu.VMEM((rows, width), values.dtype),
            pltpu.VMEM((rows, width), above.dtype),
            pltpu.SemaphoreType.DMA((2,)),
        ],
        micros=13 if low else 0.005,
        stream=not low,
        sent=(0, 1) if low else (),
    )


def feed_kernel(where, low_ref, high_ref, mat_low, mat_high, middle_ref, shift_ref, keep_ref, out_ref):
    total = dot(low_ref[...], mat_low[...]) + dot(high_ref[...], mat_high[...])
    out_ref[...] = keep_ref[...] * (total + middle_ref[...] + shift_ref[...])


def feed(where, low, high, mats, middle, shift, keep):
    rows, width = middle.shape
    mat = ((mats[0].shape[0], 256), column)
    return call(
        feed_kernel,
        (width // 256,),
        where,
        [
            whole(low),
            whole(high),
            (mats[0], *mat),
            (mats[1], *mat),
            (middle, (rows, 256), column),
            (shift, (1, 256), column),
            whole(keep),
        ],
        [((rows, width), f32, (rows, 256), column)], micros=0.002, stream=True)[0]


def product_kernel(counts, where, *refs):
    n = len(counts)
    lefts, rights, outs, turned = refs[: 2 * n], refs[2 * n : 4 * n], refs[4 * n : -2 * n], refs[-2 * n :]
    keep_a, send_a, keep_b, send_b = outs
    step = pl.program_id(0)
    middle = sum(counts) // 2

    @pl.when(step == 0)
    def _():
        for left, turn in zip(lefts, turned):
            turn[...] = left[...].T

    def put(pair, targets):
        own, other = turned[2 * pair : 2 * pair + 2]
        right, right_other = rights[2 * pair : 2 * pair + 2]
        count = own.shape[0] // 4
        total = (dot(own[...], right[...]) + dot(other[...], right_other[...])).astype(bf16)
        for target, blocks in targets:
            for at, block in enumerate(blocks):
                target[at * count : (at + 1) * count, :] = total[block * count : (block + 1) * count, :]

    first = 0
    for pair, count in enumerate(counts):
        here = (step >= first) & (step < first + count)

        @pl.when(here & (step < middle))
        def _(pair=pair):
            put(pair, ((keep_a, (0, 1)), (send_a, (2, 3))))

        @pl.when(here & (step >= middle))
        def _(pair=pair):
            put(pair, ((keep_b, (0, 2)), (send_b, (1, 3))))

        first += count


def add_kernel(where, a0, a1, b0, b1, keep_a, send_a, keep_b, send_b):
    half = a0.shape[0] // 2
    for kept, piece, targets in ((a0, a1, (keep_a, send_a)), (b0, b1, (keep_b, send_b))):
        for part, target in enumerate(targets):
            rows = slice(part * half, (part + 1) * half)
            total = kept[rows, :].astype(f32) + piece[rows, :].astype(f32)
            target[...] = total.astype(bf16)


def flat_kernel(where, a0, a1, b0, b1, out):
    columns = a0.shape[1]
    for side, (kept, piece) in enumerate(((a0, a1), (b0, b1))):
        total = kept[...].astype(f32) + piece[...].astype(f32)
        out[:, side * columns : (side + 1) * columns] = total.astype(bf16)


def finish_kernel(where, a0, a1, b0, b1, *refs):
    own, *others, total = refs
    columns = a0.shape[1]
    for side, (kept, piece) in enumerate(((a0, a1), (b0, b1))):
        total[:, side * columns : (side + 1) * columns] = kept[...].astype(f32) + piece[...].astype(f32)
    count = own.shape[0]
    for at, out in enumerate((own, *others)):
        rows = pl.ds(pl.multiple_of(where[16 + at] * count, count), count)
        out[...] = total[rows, :].astype(out.dtype)


class Sum:
    def __init__(self, swap, along, order, where, lefts, rights, tile, counts, flat=False):
        self.swap, self.along, self.order, self.where = swap, along, order, where
        self.lefts = [left for pair in lefts for left in pair]
        self.rights = [right for pair in rights for right in pair]
        self.tile, self.counts, self.flat = tile, counts, flat
        self.sent = 0
        self.shares = []

    def product(self, *arrays):
        n = len(self.counts)
        lefts, rights = arrays[: 2 * n], arrays[2 * n :]
        depth = lefts[0].shape[0]
        count = self.lefts[0][0].shape[1]
        specs = [first_columns(left, count, at) for left, (_, at) in zip(lefts, self.lefts)]
        first = 0
        for pair, steps in enumerate(self.counts):
            for right, (_, base) in list(zip(rights, self.rights))[2 * pair : 2 * pair + 2]:
                at = lambda i, first=first, steps=steps, base=base: base + jnp.clip(i - first, 0, steps - 1)
                if right.ndim == 2:
                    specs.append((right, (depth, self.tile), lambda i, _, at=at: (0, at(i))))
                else:
                    per = right.shape[2] // self.tile
                    specs.append(
                        (right, (None, depth, self.tile), lambda i, _, at=at: (at(i) // per, 0, at(i) % per))
                    )
            first += steps
        near = lambda i, _: (0, jnp.minimum(i, first // 2 - 1))
        far = lambda i, _: (0, jnp.maximum(i - first // 2, 0))
        shape = (count // 2, self.tile * first // 2)
        block = (count // 2, self.tile)
        return call(
            functools.partial(product_kernel, self.counts),
            (first,),
            self.where,
            specs,
            [(shape, bf16, block, near)] * 2 + [(shape, bf16, block, far)] * 2,
            [pltpu.VMEM((count, depth), bf16)] * (2 * n),
            micros=12,
            sent=(0, 1, 2, 3),
        )

    def add(self, *pieces):
        rows, columns = pieces[0].shape
        tile = columns // 2
        block = ((rows, tile), column)
        half = ((rows // 2, columns), bf16, (rows // 2, tile), column)
        return call(
            add_kernel, (columns // tile,), self.where, [(v, *block) for v in pieces], [half] * 4, stream=True,
            micros=3 if self.flat else 0.005,
        )

    def finish(self, *pieces):
        rows, columns = pieces[0].shape
        if self.flat:
            out = whole_out((rows, 2 * columns), bf16)
            return call(flat_kernel, (1,), self.where, [whole(v) for v in pieces], [out])
        owners = self.where.shape[0] - 16
        share = (rows // owners, 2 * columns)
        return call(
            finish_kernel,
            (1,),
            self.where,
            [whole(v) for v in pieces],
            [whole_out(share, f32)] + [whole_out(share, bf16)] * (owners - 1),
            [pltpu.VMEM((rows, 2 * columns), f32)],
            micros=0.002,
        )

    def work(self):
        if self.sent == 2:
            self.own, *self.ready = self.order(
                self.finish, self.kept[0], self.arrived[0], self.kept[1], self.arrived[1]
            )
            return
        if self.sent == 0:
            factors = [array for array, _ in (*self.lefts, *self.rights)]
            keep_a, send_a, keep_b, send_b = self.order(self.product, *factors)
        else:
            keep_a, send_a, keep_b, send_b = self.order(
                self.add, self.kept[0], self.arrived[0], self.kept[1], self.arrived[1]
            )
        self.kept = keep_a, keep_b
        self.ready = send_a, send_b

    def send(self, shares=()):
        if self.sent < 2:
            ready = self.order.tie(*self.ready)
            bits = (XBIT, YBIT) if self.sent else (YBIT, XBIT)
            self.arrived = self.swap(ready[0], bits[0]), self.swap(ready[1], bits[1])
            self.sent += 1
        elif self.flat:
            self.share = lax.psum_scatter(
                self.order.tie(self.own)[0], "fsdp", scatter_dimension=0, tiled=True
            )
        else:
            for by, piece in zip(shares, self.order.tie(*[self.ready[by - 1] for by in shares])):
                self.shares.append(self.along(piece, by))

    def meet(self):
        if self.flat:
            (self.share,) = self.order.tie(self.share)
            self.order.last = (self.share,)
        else:
            self.shares = list(self.order.tie(*self.shares))
            self.order.last = (self.shares[0],)

    def total(self):
        if self.flat:
            return self.order(lambda share: share.astype(f32), self.share)
        return self.order(
            lambda own, *others: sum((piece.astype(f32) for piece in others), own), self.own, *self.shares
        )


class Order:
    def __init__(self):
        self.last = ()

    def __call__(self, function, *values):
        result = function(*self.tie(*values))
        self.last = (result[0] if isinstance(result, (tuple, list)) else result,)
        return result

    def tie(self, *values):
        return lax.optimization_barrier((*values, *self.last))[: len(values)]


def assemble_kernel(where, *refs):
    pieces, targets = [], []
    for ref in refs:
        (pieces if ref.shape[0] == refs[0].shape[0] else targets).append(ref)
    count = pieces[0].shape[0]
    columns = targets[0].shape[1]
    for at, piece in enumerate(pieces):
        rows = pl.ds(pl.multiple_of(where[at] * count, count), count)
        for side, target in enumerate(targets):
            target[rows, :] = piece[:, side * columns : (side + 1) * columns]


def assemble(count, places, *pieces):
    rows, columns = pieces[0].shape
    out = whole_out((rows * len(pieces), columns // count), bf16)
    return call(assemble_kernel, (1,), places, [whole(p) for p in pieces], [out] * count, micros=0.003)


def join_kernel(where, *refs):
    out = refs[-1]
    count = refs[0].shape[0]
    for side in range(2):

        @pl.when(pl.program_id(0) == side)
        def _(side=side):
            for at, piece in enumerate(refs[4 * side : 4 * side + 4]):
                out[at * count : (at + 1) * count, :] = piece[...]


def join(where, *pieces):
    rows, columns = pieces[3].shape
    ins = [first_columns(p, columns, at // 4 if p.shape[1] > columns else 0) for at, p in enumerate(pieces)]
    return call(
        join_kernel,
        (2,),
        where,
        ins,
        [((4 * rows, 2 * columns), bf16, (4 * rows, columns), column)],
        micros=4,
    )[0]


def split_kernel(where, near, far, left, right):
    left[...] = near[...]
    right[...] = far[...]


def split(where, near, far):
    rows, columns = near.shape[0], near.shape[1] // 2
    return call(
        split_kernel,
        (1,),
        where,
        [first_columns(near, columns, 0), first_columns(far, columns, 1)],
        [whole_out((rows, columns), bf16)] * 2,
    )


def unpack_kernel(where, low, high, *refs):
    outs, true = refs[:-1], refs[-1]
    for side, part in enumerate((low, high)):
        turned = part[...].astype(f32).T
        for at in range(4):
            true[:, lanes(where, 4 * side + at)] = turned[:, at * 128 : (at + 1) * 128]
    share = 32
    first = 0
    for vector in outs:
        columns = vector.shape[1] // true.shape[1]
        if columns == 1:
            vector[...] = true[first : first + 1, :]
        else:
            for owner in range(true.shape[1] // share):
                for at in range(columns):
                    start = (owner * columns + at) * share
                    vector[:, start : start + share] = true[
                        first + at : first + at + 1, owner * share : (owner + 1) * share
                    ]
        first += columns


def unpack(where, mats, sizes):
    block = mats[0].shape[1] // 128 - 2
    outs = [whole_out((1, size), f32) for size in sizes]
    rows = mats[0].shape[0]
    return call(
        unpack_kernel,
        (1,),
        where,
        [(mat, (rows, 128), lambda *_: (0, block)) for mat in mats],
        outs,
        [pltpu.VMEM((128, 2 * rows), f32)],
    )


def exchanged(fsdp_size, block_in, keep_mask, out_cotangent, *params):
    (g1, b1, qkv_weight, qv_bias, out_weight, out_bias, g2, b2, up_weight, up_bias, down_weight, down_bias) = params
    seqs, length, width = block_in.shape
    rows = seqs * length
    half = width // 2
    order = Order()
    me, line = lax.axis_index("dp"), lax.axis_index("fsdp")
    where = positions(me, line, fsdp_size)

    def swap(value, bit):
        return lax.ppermute(value, "dp", [(i, i ^ bit) for i in range(8)])

    def along(value, by):
        return lax.ppermute(value, "fsdp", [(i, (i + by) % fsdp_size) for i in range(fsdp_size)])

    class Gather:
        def start(self, left, right):
            left, right = self.own = order.tie(left, right)
            self.near = swap(left, XBIT), swap(right, XBIT)
            self.far = swap(left, YBIT), swap(right, YBIT)

        def turn(self, *others):
            *pieces, = order.tie(*self.near, *self.far, *others)
            self.near, self.far = tuple(pieces[:2]), tuple(pieces[2:4])
            left, right = self.near[0], self.far[1]
            order.last = (left,)
            self.last = swap(left, YBIT), swap(right, XBIT)

        def start_whole(self, block):
            block = order.tie(block)[0]
            self.own = block
            self.near, self.far = swap(block, XBIT), swap(block, YBIT)

        def turn_whole(self, *others):
            left, right = order(lambda near, far, *_: split(where, near, far), self.near, self.far, *others)
            self.last = swap(left, YBIT), swap(right, XBIT)

        def join(self, *others):
            sides = [v if isinstance(v, tuple) else (v, v) for v in (self.own, self.near, self.far)]
            pieces = [p for side in zip(*sides, self.last) for p in side]
            self.low = order(lambda *p: join(where, *p[:8]), *pieces, *others)

        def joined(self):
            low = order.tie(self.low)[0]
            self.mats = low, swap(low, CORE)

    def around(shard):
        return [shard] + [along(shard, by) for by in range(fsdp_size - 1, 0, -1)]

    vectors = (g1, b1, qv_bias, out_bias, g2, b2, up_bias, down_bias)
    device_count = 8 * fsdp_size
    sizes = [v.shape[0] * device_count for v in vectors]
    cuts = [sum(v.shape[0] for v in vectors[:i]) for i in range(1, len(vectors))]
    share = qkv_weight.shape[0]
    beside = lax.optimization_barrier(jnp.concatenate(vectors)).reshape(-1, share).T
    beside = jnp.pad(beside, ((0, 0), (0, 256 - beside.shape[1])))
    qkv_low = jnp.concatenate([qkv_weight, beside], 1).astype(bf16)
    behind = jnp.stack([(line + by) % fsdp_size for by in range(fsdp_size)]).astype(jnp.int32)
    qkv_pieces = around(qkv_low)
    up_low = jnp.concatenate([up_weight, out_weight], 1).astype(bf16)
    down_block = lax.all_gather(down_weight.astype(bf16), "fsdp", axis=0, tiled=True)

    keep = jnp.concatenate(
        [jnp.ones((seqs, length - keep_mask.shape[1]), jnp.int32), keep_mask], axis=1
    )
    keep_rows = keep.reshape(rows, 1).astype(f32)
    keep_column = keep.reshape(seqs, length, 1)
    inputs = block_in.reshape(rows, width)
    grad_feed = order(
        lambda g: jnp.where(keep_rows > 0, g, jnp.zeros((), bf16)), out_cotangent.reshape(rows, width)
    )
    down_bias_grad = jnp.sum(grad_feed.astype(f32), 0)

    qkv, up, down = Gather(), Gather(), Gather()
    qkv.start_whole(order(functools.partial(assemble, 1, behind), *qkv_pieces)[0])
    up_pieces = around(order.tie(up_low)[0])
    qkv.turn_whole()
    up_halves = order(functools.partial(assemble, 2, behind), *up_pieces)
    qkv.join()
    qkv.joined()
    up.start(*up_halves)
    g1, b1, qv_bias, out_bias, g2, b2, up_bias, down_bias = order(
        lambda *m: unpack(where, m, sizes), *qkv.mats
    )
    one_low, one_pack = order(functools.partial(norm_one, where), inputs, grad_feed, g1, b1)
    shift = jnp.concatenate([qv_bias[:, :width], jnp.zeros((1, width), f32), qv_bias[:, width:]], 1)
    projected = order(
        lambda lo, hi, s, *m: project(where, lo, hi, m, s), one_low, one_pack, shift, *qkv.mats
    )
    mixed_left, probs_left = order(lambda p: attention_forward(keep_column, p, 0), projected)
    up.turn(down_block)
    one_other = swap(order.tie(one_pack)[0], CORE)
    mixed_right, probs_right = order(lambda p: attention_forward(keep_column, p, 1), projected)
    down_halves = order(lambda b: (b[:, :half], b[:, half:]), down_block)
    up.join(one_other)
    up.joined()
    down.start(*down_halves)
    mixed = jnp.concatenate([mixed_left, mixed_right], 1)
    mix_low, middle, two_low, two_pack = order(
        lambda m, o, *mats: branch_norm(where, m, inputs, mats, o, g2, b2, length),
        mixed, out_bias, *up.mats,
    )
    hidden_high, slope_high = order(
        lambda lo, hi, s, *m: expand(where, 1, lo, hi, m, s), two_low, two_pack, up_bias, *up.mats
    )
    hidden_low, slope_low = order(
        lambda lo, hi, s, *m: expand(where, 0, lo, hi, m, s), two_low, two_pack, up_bias, *up.mats
    )
    down.turn()
    hidden_other = swap(order.tie(hidden_high)[0], CORE)
    two_other = swap(order.tie(two_pack)[0], CORE)
    down_sum = Sum(
        swap, along, order, where,
        [((hidden_low, 0), (hidden_other, 0))], [((grad_feed, 0), (one_other, half // 256))],
        256, [width // 256], True,
    )
    down_sum.work()
    down.join()
    down.joined()
    down_sum.send()
    grad_pre, up_bias_grad = order(
        lambda g, s0, s1, *m: shrink(where, g, m, (s0, s1)),
        grad_feed, slope_low, slope_high, *down.mats,
    )
    down_sum.work()
    down_sum.send()
    pre_other = swap(order.tie(grad_pre)[0], CORE)
    grad_middle, grad_branch, out_bias_grad, gain_two_grad, bias_two_grad, grad_mixed = order(
        lambda g, mid, above, *m: back(where, g, m, mid, above, g2),
        grad_pre, middle, grad_feed, *up.mats,
    )
    branch, pre_other = order.tie(grad_branch, pre_other)
    branch_other = swap(branch, CORE)
    down_sum.work()
    up_sum = Sum(
        swap, along, order, where,
        [((two_low, 0), (two_other, 1)), ((mix_low, 0), (two_other, 0))],
        [((grad_pre, 0), (pre_other, 0)), ((grad_branch, 0), (branch_other, 0))],
        512, [grad_pre.shape[1] // 512, width // 512], True,
    )
    up_sum.work()
    up_sum.send()
    down_sum.send()
    grad_projected, sum_q, sum_v = order(
        lambda p, g, *probs: attention_backward(probs, p, g),
        projected, grad_mixed, probs_left, probs_right,
    )
    block_out = order(
        lambda lo, hi, mid, s, *m: feed(where, lo, hi, m, mid, s, keep_rows),
        hidden_low, hidden_high, middle, down_bias, *down.mats,
    )
    down_sum.meet()
    up_sum.work()
    up_sum.send()
    projected_other = swap(order.tie(grad_projected)[0], CORE)
    qkv_sum = Sum(
        swap, along, order, where,
        [((one_low, 0), (one_other, 0))], [((grad_projected, 0), (projected_other, 0))],
        512, [3 * width // 512],
    )
    qkv_sum.work()
    qkv_sum.send()
    up_sum.work()
    up_sum.send()
    sums = [
        jnp.concatenate([sum_q, sum_v], 1),
        out_bias_grad,
        gain_two_grad,
        bias_two_grad,
        up_bias_grad,
        down_bias_grad.reshape(1, -1),
    ]
    input_grad, shares = order(
        lambda g, x, above, m0, m1, *v: back(where, g, (m0, m1), x, above, g1, v, device_count),
        grad_projected, inputs, grad_middle, *qkv.mats, *sums,
    )
    qkv_sum.work()
    qkv_sum.send()
    shares = order.tie(shares.reshape(2, 2, 2, fsdp_size, -1))[0]

    def halve(shares, axis, bit):
        low, high = (lax.index_in_dim(shares, side, axis, keepdims=False) for side in range(2))
        upper = me & bit > 0
        return jnp.where(upper, high, low), jnp.where(upper, low, high)

    mine, other = halve(shares, 2, CORE)
    mine, other = halve(mine + swap(other, CORE), 1, XBIT)
    up_sum.meet()
    mine, other = order.tie(mine, other)
    order.last = (mine,)
    qkv_sum.work()
    qkv_sum.send((1, 2, 3))
    shares = mine + swap(order.tie(other)[0], XBIT)
    qkv_sum.shares[0], shares = order.tie(qkv_sum.shares[0], shares)
    order.last = (qkv_sum.shares[0],)
    mine, other = halve(shares, 0, YBIT)
    shares = mine + swap(other, YBIT)

    def row_of(by):
        return lax.dynamic_slice(shares, ((line + by) % fsdp_size, 0), (1, shares.shape[1]))

    line_shares = [along(row_of(by), by) for by in range(1, fsdp_size)]
    down_grad, up_grad = down_sum.total(), up_sum.total()
    up_grad, out_grad = up_grad[:, : up_weight.shape[1]], up_grad[:, up_weight.shape[1] :]
    qkv_grad = qkv_sum.total()
    mine = sum(line_shares, row_of(0))
    v = jnp.split(mine[0], cuts)
    return (
        block_out.reshape(seqs, length, width),
        input_grad.reshape(seqs, length, width),
        v[0],
        v[1],
        qkv_grad,
        v[2],
        out_grad,
        v[3],
        v[4],
        v[5],
        up_grad,
        v[6],
        down_grad,
        v[7],
    )


def solution(mesh):
    dp_size, fsdp_size = mesh.shape["dp"], mesh.shape["fsdp"]
    if dp_size == 8:
        local = functools.partial(exchanged, fsdp_size)
    else:
        local = functools.partial(gathered, dp_size * fsdp_size)
    row = P(AXES, None)
    vec = P(AXES)
    cube = P(AXES, None, None)
    return jax.shard_map(
        local,
        mesh=mesh,
        in_specs=(cube, row, cube, vec, vec, row, vec, row, vec, vec, vec, row, vec, row, vec),
        out_specs=(cube, cube, vec, vec, row, vec, row, vec, vec, vec, row, vec, row, vec),
        check_vma=False,
    )
```

```python
import functools
import math

import jax
import jax.numpy as jnp
from jax import lax
from jax.experimental import pallas as pl
from jax.experimental.pallas import tpu as pltpu
from jax.sharding import PartitionSpec as P

HD = 64
EPSILON = 1e-05
AXES = ("dp", "fsdp")
bf16 = jnp.bfloat16
f32 = jnp.float32
NN = (((1,), (0,)), ((), ()))
NT = (((1,), (1,)), ((), ()))
TN = (((0,), (0,)), ((), ()))


def dot(left, right, dims=NN):
    return lax.dot_general(left, right, dims, preferred_element_type=f32)


def attention_forward_kernel(seqs, length, keep_ref, q_ref, k_ref, v_ref, o_ref, p_ref):
    scale = 1.0 / math.sqrt(HD)
    for s in range(seqs):
        rows = slice(s * length, (s + 1) * length)
        visible = keep_ref[s] > 0
        mixed = []
        for h in range(128 // HD):
            cols = slice(h * HD, (h + 1) * HD)
            logits = dot(k_ref[rows, cols], q_ref[rows, cols] * scale, NT)
            logits = jnp.where(visible, logits, -1e9)
            raised = jnp.exp(logits - jnp.max(logits, 0, keepdims=True))
            probs = (raised * (1.0 / jnp.sum(raised, 0, keepdims=True))).astype(bf16)
            p_ref[h, s] = probs
            mixed.append(dot(probs, v_ref[rows, cols], TN))
        o_ref[rows, :] = jnp.concatenate(mixed, 1).astype(bf16)


def attention_backward_kernel(
    seqs, length, left_ref, right_ref, q_ref, k_ref, v_ref, do_ref, dp_ref, sq_ref, sv_ref
):
    scale = 1.0 / math.sqrt(HD)

    def work(p_ref):
        sum_q = jnp.zeros((1, 128), f32)
        sum_v = jnp.zeros((1, 128), f32)
        for s in range(seqs):
            rows = slice(s * length, (s + 1) * length)
            dqs, dks, dvs = [], [], []
            for h in range(128 // HD):
                cols = slice(h * HD, (h + 1) * HD)
                queries = q_ref[rows, cols] * scale
                grad_mixed = do_ref[rows, cols]
                low_probs = p_ref[h, s]
                grad_probs = dot(v_ref[rows, cols], grad_mixed, NT)
                dvs.append(dot(low_probs, grad_mixed))
                probs = low_probs.astype(f32)
                row_terms = jnp.sum(grad_probs * probs, 0, keepdims=True)
                grad_logits = (probs * (grad_probs - row_terms)).astype(bf16)
                dks.append(dot(grad_logits, queries))
                dqs.append(dot(grad_logits, k_ref[rows, cols], TN) * scale)
            dq = jnp.concatenate(dqs, 1).astype(bf16)
            dv = jnp.concatenate(dvs, 1).astype(bf16)
            dp_ref[0, rows, :] = dq
            dp_ref[1, rows, :] = jnp.concatenate(dks, 1).astype(bf16)
            dp_ref[2, rows, :] = dv
            sum_q += jnp.sum(dq.astype(f32), 0, keepdims=True)
            sum_v += jnp.sum(dv.astype(f32), 0, keepdims=True)
        sq_ref[...] = sum_q
        sv_ref[...] = sum_v

    half = pl.num_programs(0) // 2

    @pl.when(pl.program_id(0) < half)
    def _():
        work(left_ref)

    @pl.when(pl.program_id(0) >= half)
    def _():
        work(right_ref)


def attention_forward(keep, project, part):
    seqs, length = keep.shape[:2]
    rows, width = project.shape[0], project.shape[1] // 6
    steps = width // 128
    pair = 128 // HD
    project = pltpu.with_memory_space_constraint(project, pltpu.HBM)
    return pl.pallas_call(
        functools.partial(attention_forward_kernel, seqs, length),
        grid=(steps,),
        in_specs=[pl.BlockSpec((seqs, length, 1), lambda i: (0, 0, 0))]
        + [
            pl.BlockSpec((rows, 128), lambda i, at=at: (0, i + (2 * at + part) * steps))
            for at in range(3)
        ],
        out_specs=[
            pl.BlockSpec((rows, 128), lambda i: (0, i)),
            pl.BlockSpec((pair, seqs, length, length), lambda i: (i, 0, 0, 0)),
        ],
        out_shape=[
            jax.ShapeDtypeStruct((rows, width), bf16),
            pltpu.HBM((steps * pair, seqs, length, length), bf16),
        ],
        compiler_params=pltpu.CompilerParams(vmem_limit_bytes=20 << 20),
        cost_estimate=pl.CostEstimate(flops=int(8.5 * COST), bytes_accessed=1, transcendentals=0),
    )(keep, project, project, project)


def attention_backward(probs, project, grad_mixed):
    pairs, seqs, length = probs[0].shape[:3]
    rows, width = grad_mixed.shape
    steps = width // 128
    pair = 128 // HD
    block = pl.BlockSpec((rows, 128), lambda i: (0, i))
    vector = pl.BlockSpec((1, 128), lambda i: (0, i))
    sums = jax.ShapeDtypeStruct((1, width), f32)
    shape = (pair, seqs, length, length)
    project, grad_mixed, left, right = (
        pltpu.with_memory_space_constraint(v, pltpu.HBM) for v in (project, grad_mixed, *probs)
    )
    return pl.pallas_call(
        functools.partial(attention_backward_kernel, seqs, length),
        grid=(steps,),
        in_specs=[
            pl.BlockSpec(shape, lambda i: (jnp.minimum(i, steps // 2 - 1), 0, 0, 0)),
            pl.BlockSpec(shape, lambda i: (jnp.maximum(i - steps // 2, 0), 0, 0, 0)),
        ]
        + [pl.BlockSpec((rows, 128), lambda i, at=at: (0, i + at * steps)) for at in range(3)]
        + [block],
        out_specs=[pl.BlockSpec((3, rows, 128), lambda i: (0, 0, i)), vector, vector],
        out_shape=[pltpu.HBM((3, rows, width), bf16), sums, sums],
        compiler_params=pltpu.CompilerParams(vmem_limit_bytes=24 << 20),
        cost_estimate=pl.CostEstimate(flops=int(22 * COST), bytes_accessed=1, transcendentals=0),
    )(left, right, project, project, project, grad_mixed)


def norm_forward(values, norm_gain, norm_bias):
    average = jnp.mean(values, -1, keepdims=True)
    centered = values - average
    inverse = lax.rsqrt(jnp.mean(centered * centered, -1, keepdims=True) + EPSILON)
    normed = centered * inverse
    return (normed * norm_gain + norm_bias, normed, inverse)


def norm_backward(grad_norm, normed, inverse, norm_gain):
    scaled = grad_norm * norm_gain
    return inverse * (
        scaled
        - jnp.mean(scaled, -1, keepdims=True)
        - normed * jnp.mean(scaled * normed, -1, keepdims=True)
    )


def gathered(device_count, block_in, keep_mask, out_cotangent, *params):
    (g1, b1, qkv_weight, qv_bias, out_weight, out_bias, g2, b2, up_weight, up_bias, down_weight, down_bias) = params
    seqs, length, width = block_in.shape
    rows = seqs * length
    vectors = (g1, b1, qv_bias, out_bias, g2, b2, up_bias, down_bias)
    sizes = [v.shape[0] for v in vectors]
    cuts = [sum(sizes[:i]) for i in range(1, len(sizes))]
    packed = lax.all_gather(jnp.concatenate(vectors).astype(bf16), AXES, axis=0, tiled=False)
    g1, b1, qv_bias, out_bias, g2, b2, up_bias, down_bias = (
        part.reshape(-1).astype(f32) for part in jnp.split(packed, cuts, axis=1)
    )
    qkv_mat, out_mat, up_mat, down_mat = (
        lax.all_gather(w.astype(bf16), AXES, axis=0, tiled=True)
        for w in (qkv_weight, out_weight, up_weight, down_weight)
    )
    keep = jnp.concatenate(
        [jnp.ones((seqs, length - keep_mask.shape[1]), jnp.int32), keep_mask], axis=1
    )
    keep_rows = keep.reshape(rows, 1).astype(f32)
    keep_column = keep.reshape(seqs, length, 1)
    inputs = block_in.astype(f32).reshape(rows, width)
    grad_out = out_cotangent.astype(f32).reshape(rows, width) * keep_rows
    grad_feed = grad_out.astype(bf16)

    normed_one, plain_one, inverse_one = norm_forward(inputs, g1, b1)
    act_one = normed_one.astype(bf16)
    zeros = jnp.zeros((width,), f32)
    shift = jnp.concatenate([qv_bias[:width], zeros, qv_bias[width:]])
    project = (dot(act_one, qkv_mat) + shift).astype(bf16)

    (mixed_left, probs_left), (mixed_right, probs_right) = (
        attention_forward(keep_column, project, part) for part in range(2)
    )
    mixed = jnp.concatenate([mixed_left, mixed_right], 1)
    middle = inputs + dot(mixed, out_mat) + out_bias
    normed_two, plain_two, inverse_two = norm_forward(middle, g2, b2)
    act_two = normed_two.astype(bf16)
    pre = dot(act_two, up_mat) + up_bias
    cumul = 0.5 * (1.0 + lax.erf(pre * 0.7071067811865476))
    hidden = (pre * cumul).astype(bf16)
    slope = cumul + pre * jnp.exp(-0.5 * pre * pre) * 0.3989422804014327
    feed = dot(hidden, down_mat) + down_bias
    block_out = keep_rows * (middle + feed)

    grad_pre = (dot(grad_feed, down_mat, NT) * slope).astype(bf16)
    grad_act_two = dot(grad_pre, up_mat, NT)
    grad_middle = grad_out + norm_backward(grad_act_two, plain_two, inverse_two, g2)
    grad_branch = grad_middle.astype(bf16)
    grad_mixed = dot(grad_branch, out_mat, NT).astype(bf16)
    grad_parts, sum_q, sum_v = attention_backward((probs_left, probs_right), project, grad_mixed)
    grad_project = jnp.concatenate([grad_parts[i] for i in range(3)], 1)
    grad_act_one = dot(grad_project, qkv_mat, NT)
    input_grad = grad_middle + norm_backward(grad_act_one, plain_one, inverse_one, g1)
    grads = (
        jnp.sum(grad_act_one * plain_one, 0),
        jnp.sum(grad_act_one, 0),
        jnp.concatenate([sum_q[0], sum_v[0]]),
        jnp.sum(grad_branch.astype(f32), 0),
        jnp.sum(grad_act_two * plain_two, 0),
        jnp.sum(grad_act_two, 0),
        jnp.sum(grad_pre.astype(f32), 0),
        jnp.sum(grad_feed.astype(f32), 0),
    )
    shares = jnp.concatenate([g.reshape(device_count, -1) for g in grads], 1)
    v = jnp.split(lax.psum_scatter(shares, AXES, scatter_dimension=0, tiled=False), cuts)

    def to_owner(left, right):
        total = dot(left, right, TN).astype(bf16)
        return lax.psum_scatter(total, AXES, scatter_dimension=0, tiled=True).astype(f32)

    return (
        block_out.reshape(seqs, length, width),
        input_grad.reshape(seqs, length, width),
        v[0],
        v[1],
        to_owner(act_one, grad_project),
        v[2],
        to_owner(mixed, grad_branch),
        v[3],
        v[4],
        v[5],
        to_owner(act_two, grad_pre),
        v[6],
        to_owner(hidden, grad_feed),
        v[7],
    )


CORE, XBIT, YBIT = 1, 2, 4
BLOCKS = [c * CORE + y * YBIT + x * XBIT for c in range(2) for y in range(2) for x in range(2)]
COST = 1e12


def positions(me, line, count):
    true = [me ^ r for r in BLOCKS]
    place = [
        sum(jnp.where((me ^ d) == r, at, 0) for at, r in enumerate(BLOCKS)) for d in range(8)
    ]
    ahead = [(line + by) % count for by in range(count)]
    return jnp.stack(true + place + ahead).astype(jnp.int32)


def call(kernel, grid, where, ins, outs, scratch=(), micros=3, sent=(), stream=False):
    held = 6 << 20
    specs = []
    arrays = []
    for array, block, index in ins:
        if block is None:
            arrays.append(pltpu.with_memory_space_constraint(array, pltpu.HBM) if stream else array)
            specs.append(pl.BlockSpec(memory_space=pl.ANY))
            continue
        once = tuple(block) == tuple(array.shape)
        if stream and not once:
            array = pltpu.with_memory_space_constraint(array, pltpu.HBM)
        arrays.append(array)
        size = math.prod(n or 1 for n in block) * array.dtype.itemsize
        held += size if once else 2 * size
        specs.append(pl.BlockSpec(block, index, pipeline_mode=pl.Buffered(1) if once else None))
    for _, dtype, block, _ in outs:
        held += 2 * math.prod(block) * jnp.dtype(dtype).itemsize
    for buffer in scratch:
        if len(buffer.shape) > 1:
            held += math.prod(buffer.shape) * jnp.dtype(buffer.dtype).itemsize
    return pl.pallas_call(
        kernel,
        grid_spec=pltpu.PrefetchScalarGridSpec(
            num_scalar_prefetch=1,
            grid=grid,
            in_specs=specs,
            out_specs=[pl.BlockSpec(block, index) for _, _, block, index in outs],
            scratch_shapes=list(scratch),
        ),
        out_shape=[
            pltpu.HBM(shape, dtype) if at in sent else jax.ShapeDtypeStruct(shape, dtype)
            for at, (shape, dtype, _, _) in enumerate(outs)
        ],
        compiler_params=pltpu.CompilerParams(vmem_limit_bytes=held),
        cost_estimate=pl.CostEstimate(flops=int(micros * COST), bytes_accessed=1, transcendentals=0),
    )(where, *arrays)


def whole(array):
    return (array, array.shape, lambda *_: (0,) * array.ndim)


def whole_out(shape, dtype):
    return (shape, dtype, shape, lambda *_: (0,) * len(shape))


def column(i, *_):
    return (0, i)


def lanes(where, at):
    return pl.ds(pl.multiple_of(where[at] * 128, 128), 128)


def deal(where, source, low, high):
    for at in range(4):
        cols = slice(at * 128, (at + 1) * 128)
        low[:, cols] = source[:, lanes(where, at)]
        high[:, cols] = source[:, lanes(where, 4 + at)]


def normalize(values):
    centered = values - jnp.mean(values, -1, keepdims=True)
    inverse = lax.rsqrt(jnp.mean(centered * centered, -1, keepdims=True) + EPSILON)
    return centered * inverse, inverse


def norm_kernel(where, x_ref, grad_ref, gain_ref, bias_ref, low_ref, pack_ref, whole_ref):
    normed, _ = normalize(x_ref[...].astype(f32))
    whole_ref[...] = (normed * gain_ref[...] + bias_ref[...]).astype(bf16)
    half = low_ref.shape[1]
    deal(where, whole_ref, low_ref, pack_ref.at[:, :half])
    pack_ref[:, half:] = grad_ref[...]


def norm_one(where, inputs, grad_feed, gain, bias):
    rows, width = inputs.shape
    index = lambda i, _: (i, 0)
    return call(
        norm_kernel,
        (rows // 128,),
        where,
        [(inputs, (128, width), index), (grad_feed, (128, width), index), whole(gain), whole(bias)],
        [
            ((rows, width // 2), bf16, (128, width // 2), index),
            ((rows, width // 2 + width), bf16, (128, width // 2 + width), index),
        ],
        [pltpu.VMEM((128, width), bf16)],
        sent=(1,),
    )


def project_kernel(where, low_ref, high_ref, mat_low, mat_high, bias_ref, out_ref):
    total = dot(low_ref[...], mat_low[...]) + dot(high_ref[...], mat_high[...])
    out_ref[...] = (total + bias_ref[...]).astype(bf16)


def project(where, low, pack, mats, bias):
    rows, depth = low.shape
    columns = bias.shape[1]
    tile = ((depth, 512), column)
    return call(
        project_kernel,
        (columns // 512,),
        where,
        [whole(low), first_columns(pack, depth), (mats[0], *tile), (mats[1], *tile), (bias, (1, 512), column)],
        [((rows, columns), bf16, (rows, 512), column)], micros=8, sent=(0,))[0]


def branch_kernel(
    where, mixed_ref, x_ref, mat_low, mat_high, shift_ref, gain_ref, bias_ref,
    mix_low, middle_ref, two_low, pack_ref, whole_ref,
):
    half = mix_low.shape[1]
    mix_high, two_high = pack_ref.at[:, :half], pack_ref.at[:, half:]
    deal(where, mixed_ref, mix_low, mix_high)
    total = dot(mix_low[...], mat_low[...]) + dot(mix_high[...], mat_high[...])
    middle = x_ref[...].astype(f32) + total + shift_ref[...]
    middle_ref[...] = middle
    normed, _ = normalize(middle)
    whole_ref[...] = (normed * gain_ref[...] + bias_ref[...]).astype(bf16)
    deal(where, whole_ref, two_low, two_high)


def branch_norm(where, mixed, inputs, mats, shift, gain, bias, length):
    rows, width = inputs.shape
    block = ((length, width), lambda i, _: (i, 0))
    part = ((rows, width // 2), bf16, (length, width // 2), lambda i, _: (i, 0))
    return call(
        branch_kernel,
        (rows // length,),
        where,
        [(mixed, *block), (inputs, *block), *[last_columns(m, width) for m in mats]]
        + [whole(v) for v in (shift, gain, bias)],
        [part, ((rows, width), f32, *block), part, ((rows, width), bf16, *block)],
        [pltpu.VMEM((length, width), bf16)],
        micros=4,
        sent=(3,),
    )


def first_columns(mat, count, at=0):
    return (mat, (mat.shape[0], count), lambda *_: (0, at))


def last_columns(mat, count):
    at = mat.shape[1] // count - 1
    return (mat, (mat.shape[0], count), lambda *_: (0, at))


def expand_kernel(where, low_ref, high_ref, mat_low, mat_high, shift_ref, hidden_ref, slope_ref):
    chunk = low_ref.shape[0] // 4
    for at in range(4):
        rows = slice(at * chunk, (at + 1) * chunk)
        pre = dot(low_ref[rows, :], mat_low[...]) + dot(high_ref[rows, :], mat_high[...])
        pre = pre + shift_ref[...]
        cumul = 0.5 * (1.0 + lax.erf(pre * 0.7071067811865476))
        hidden_ref[rows, :] = (pre * cumul).astype(bf16)
        slope = cumul + pre * jnp.exp(-0.5 * pre * pre) * 0.3989422804014327
        slope_ref[rows, :] = slope.astype(bf16)


def expand(where, side, low, pack, mats, shift):
    rows, depth = low.shape
    columns = shift.shape[1]
    tile = columns // 8
    true = lambda i, where: (0, where[4 * side + i])
    return call(
        expand_kernel,
        (4,),
        where,
        [
            whole(low),
            first_columns(pack, depth, 1),
            (mats[0], (depth, tile), true),
            (mats[1], (depth, tile), true),
            (shift, (1, tile), true),
        ],
        [((rows, columns // 2), bf16, (rows, tile), column)] * 2,
        micros=7,
        sent=(0, 1),
    )


def shrink_kernel(where, grad_ref, mat_low, mat_high, slope_low, slope_high, out_ref, sum_ref):
    for side, (mat, slope) in enumerate(((mat_low, slope_low), (mat_high, slope_high))):

        @pl.when(pl.program_id(0) // 4 == side)
        def _(mat=mat, slope=slope):
            grad = (dot(grad_ref[...], mat[...], NT) * slope[...].astype(f32)).astype(bf16)
            out_ref[...] = grad
            sum_ref[...] = jnp.sum(grad.astype(f32), 0, keepdims=True)


def shrink(where, grad, mats, slopes):
    rows, width = grad.shape
    columns = 2 * slopes[0].shape[1]
    tile = columns // 8
    true = lambda i, where: (0, where[i])
    near = lambda i, _: jnp.minimum(i, 3)
    far = lambda i, _: jnp.maximum(i - 4, 0)
    return call(
        shrink_kernel,
        (8,),
        where,
        [
            whole(grad),
            (mats[0], (tile, width), lambda i, _: (near(i, _), 0)),
            (mats[1], (tile, width), lambda i, _: (far(i, _), 0)),
            (slopes[0], (rows, tile), lambda i, _: (0, near(i, _))),
            (slopes[1], (rows, tile), lambda i, _: (0, far(i, _))),
        ],
        [((rows, columns), bf16, (rows, tile), true), ((1, columns), f32, (1, tile), true)],
        micros=12,
        stream=True,
    )


def back_kernel(low, where, grad_ref, mat_low, mat_high, values_any, above_any, gain_ref, *rest):
    *rest, total, values_ref, above_ref, sems = rest
    if low:
        out_low, out_high, out_ref, low_ref, low_sum, gain_sum, bias_sum, mixed_ref = rest
    else:
        *vectors, out_ref, packed = rest
    step = pl.program_id(0)
    fetches = [
        pltpu.make_async_copy(values_any, values_ref, sems.at[0]),
        pltpu.make_async_copy(above_any, above_ref, sems.at[1]),
    ]

    @pl.when(step == 0)
    def _():
        for fetch in fetches:
            fetch.start()

    half = mat_low.shape[0]
    for side, mat in enumerate((mat_low, mat_high)):
        cols = slice(side * half, (side + 1) * half)
        part = dot(grad_ref[...], mat[...], NT)

        @pl.when(step == 0)
        def _(cols=cols, part=part):
            total[:, cols] = part

        @pl.when(step > 0)
        def _(cols=cols, part=part):
            total[:, cols] += part

    @pl.when(step == pl.num_programs(0) - 1)
    def _():
        for fetch in fetches:
            fetch.wait()
        count, width = values_ref.shape
        chunk = 64
        sums = [jnp.zeros((1, width), f32)] * 3
        for first in range(0, count, chunk):
            rows = slice(first, first + chunk)
            normed, inverse = normalize(values_ref[rows, :].astype(f32))
            grad = jnp.concatenate([total[rows, lanes(where, 8 + block)] for block in range(8)], 1)
            scaled = grad * gain_ref[...]
            result = above_ref[rows, :].astype(f32) + inverse * (
                scaled
                - jnp.mean(scaled, -1, keepdims=True)
                - normed * jnp.mean(scaled * normed, -1, keepdims=True)
            )
            out_ref[rows, :] = result
            sums[0] += jnp.sum(grad * normed, 0, keepdims=True)
            sums[1] += jnp.sum(grad, 0, keepdims=True)
            if low:
                rounded = result.astype(bf16)
                low_ref[rows, :] = rounded
                sums[2] += jnp.sum(rounded.astype(f32), 0, keepdims=True)
        if low:
            gain_sum[...] = sums[0]
            bias_sum[...] = sums[1]
            low_sum[...] = sums[2]
            for at in range(4):
                mat = (out_low, out_high)[at // 2][at % 2 * 256 : at % 2 * 256 + 256, :]
                part = dot(low_ref[...], mat, NT).astype(bf16)
                for side in range(2):
                    mixed_ref[:, lanes(where, 2 * at + side)] = part[:, side * 128 : (side + 1) * 128]
        else:
            owners = packed.shape[0]
            at = 0
            for vector in (*sums[:2], *[ref[...] for ref in vectors]):
                share = vector.shape[1] // owners
                for owner in range(owners):
                    packed[owner : owner + 1, at : at + share] = vector[
                        :, owner * share : (owner + 1) * share
                    ]
                at += share


def back(where, grad, mats, values, above, gain, vectors=(), owners=0):
    low = not vectors
    rows, width = values.shape
    depth = mats[0].shape[0]
    tile = 1024
    outs = [whole_out((rows, width), f32)]
    if low:
        steps = grad.shape[1] // tile
        grad_block = (grad, (rows, tile), column)
        outs += [whole_out((rows, width), bf16)] + [whole_out((1, width), f32)] * 3
        outs += [whole_out((rows, width), bf16)]
    else:
        steps = grad.shape[0]
        grad_block = (grad, (None, rows, tile), lambda i, _: (i, 0, 0))
        columns_packed = (2 * width + sum(v.shape[1] for v in vectors)) // owners
        outs += [whole_out((owners, columns_packed), f32)]
    return call(
        functools.partial(back_kernel, low),
        (steps,),
        where,
        [
            grad_block,
            (mats[0], (depth, tile), column),
            (mats[1], (depth, tile), column),
            (values, None, None),
            (above, None, None),
            whole(gain),
            *[last_columns(m, width) for m in mats if low],
            *[whole(v) for v in vectors],
        ],
        outs,
        [
            pltpu.VMEM((rows, width), f32),
            pltpu.VMEM((rows, width), values.dtype),
            pltpu.VMEM((rows, width), above.dtype),
            pltpu.SemaphoreType.DMA((2,)),
        ],
        micros=13 if low else 0.005,
        stream=not low,
        sent=(0, 1, 5) if low else (),
    )


def feed_kernel(where, low_ref, high_ref, mat_low, mat_high, middle_ref, shift_ref, keep_ref, out_ref):
    total = dot(low_ref[...], mat_low[...]) + dot(high_ref[...], mat_high[...])
    out_ref[...] = keep_ref[...] * (total + middle_ref[...] + shift_ref[...])


def feed(where, low, high, mats, middle, shift, keep):
    rows, width = middle.shape
    mat = ((mats[0].shape[0], 256), column)
    return call(
        feed_kernel,
        (width // 256,),
        where,
        [
            whole(low),
            whole(high),
            (mats[0], *mat),
            (mats[1], *mat),
            (middle, (rows, 256), column),
            (shift, (1, 256), column),
            whole(keep),
        ],
        [((rows, width), f32, (rows, 256), column)], micros=0.002, stream=True)[0]


def product_kernel(counts, where, *refs):
    n = len(counts)
    lefts, rights, outs, turned = refs[: 2 * n], refs[2 * n : 4 * n], refs[4 * n : -2 * n], refs[-2 * n :]
    keep_a, send_a, keep_b, send_b = outs
    step = pl.program_id(0)
    middle = sum(counts) // 2

    @pl.when(step == 0)
    def _():
        for left, turn in zip(lefts, turned):
            turn[...] = left[...].T

    def put(pair, targets):
        own, other = turned[2 * pair : 2 * pair + 2]
        right, right_other = rights[2 * pair : 2 * pair + 2]
        count = own.shape[0] // 4
        total = (dot(own[...], right[...]) + dot(other[...], right_other[...])).astype(bf16)
        for target, blocks in targets:
            for at, block in enumerate(blocks):
                target[at * count : (at + 1) * count, :] = total[block * count : (block + 1) * count, :]

    first = 0
    for pair, count in enumerate(counts):
        here = (step >= first) & (step < first + count)

        @pl.when(here & (step < middle))
        def _(pair=pair):
            put(pair, ((keep_a, (0, 1)), (send_a, (2, 3))))

        @pl.when(here & (step >= middle))
        def _(pair=pair):
            put(pair, ((keep_b, (0, 2)), (send_b, (1, 3))))

        first += count


def add_kernel(where, a0, a1, b0, b1, keep_a, send_a, keep_b, send_b):
    half = a0.shape[0] // 2
    for kept, piece, targets in ((a0, a1, (keep_a, send_a)), (b0, b1, (keep_b, send_b))):
        for part, target in enumerate(targets):
            rows = slice(part * half, (part + 1) * half)
            total = kept[rows, :].astype(f32) + piece[rows, :].astype(f32)
            target[...] = total.astype(bf16)


def flat_kernel(where, a0, a1, b0, b1, out):
    columns = a0.shape[1]
    for side, (kept, piece) in enumerate(((a0, a1), (b0, b1))):
        total = kept[...].astype(f32) + piece[...].astype(f32)
        out[:, side * columns : (side + 1) * columns] = total.astype(bf16)


def finish_kernel(where, a0, a1, b0, b1, *refs):
    own, *others, total = refs
    columns = a0.shape[1]
    for side, (kept, piece) in enumerate(((a0, a1), (b0, b1))):
        total[:, side * columns : (side + 1) * columns] = kept[...].astype(f32) + piece[...].astype(f32)
    count = own.shape[0]
    for at, out in enumerate((own, *others)):
        rows = pl.ds(pl.multiple_of(where[16 + at] * count, count), count)
        out[...] = total[rows, :].astype(out.dtype)


class Sum:
    def __init__(self, swap, along, order, where, lefts, rights, tile, counts, flat=False):
        self.swap, self.along, self.order, self.where = swap, along, order, where
        self.lefts = [left for pair in lefts for left in pair]
        self.rights = [right for pair in rights for right in pair]
        self.tile, self.counts, self.flat = tile, counts, flat
        self.sent = 0
        self.shares = []

    def product(self, *arrays):
        n = len(self.counts)
        lefts, rights = arrays[: 2 * n], arrays[2 * n :]
        depth = lefts[0].shape[0]
        count = self.lefts[0][0].shape[1]
        specs = [first_columns(left, count, at) for left, (_, at) in zip(lefts, self.lefts)]
        first = 0
        for pair, steps in enumerate(self.counts):
            for right, (_, base) in list(zip(rights, self.rights))[2 * pair : 2 * pair + 2]:
                at = lambda i, first=first, steps=steps, base=base: base + jnp.clip(i - first, 0, steps - 1)
                if right.ndim == 2:
                    specs.append((right, (depth, self.tile), lambda i, _, at=at: (0, at(i))))
                else:
                    per = right.shape[2] // self.tile
                    specs.append(
                        (right, (None, depth, self.tile), lambda i, _, at=at: (at(i) // per, 0, at(i) % per))
                    )
            first += steps
        near = lambda i, _: (0, jnp.minimum(i, first // 2 - 1))
        far = lambda i, _: (0, jnp.maximum(i - first // 2, 0))
        shape = (count // 2, self.tile * first // 2)
        block = (count // 2, self.tile)
        return call(
            functools.partial(product_kernel, self.counts),
            (first,),
            self.where,
            specs,
            [(shape, bf16, block, near)] * 2 + [(shape, bf16, block, far)] * 2,
            [pltpu.VMEM((count, depth), bf16)] * (2 * n),
            micros=12,
            sent=(0, 1, 2, 3),
        )

    def add(self, *pieces):
        rows, columns = pieces[0].shape
        tile = columns // 2
        block = ((rows, tile), column)
        half = ((rows // 2, columns), bf16, (rows // 2, tile), column)
        return call(
            add_kernel, (columns // tile,), self.where, [(v, *block) for v in pieces], [half] * 4, stream=True,
            micros=3 if self.flat else 0.005,
        )

    def finish(self, *pieces):
        rows, columns = pieces[0].shape
        if self.flat:
            out = whole_out((rows, 2 * columns), bf16)
            return call(flat_kernel, (1,), self.where, [whole(v) for v in pieces], [out])
        owners = self.where.shape[0] - 16
        share = (rows // owners, 2 * columns)
        return call(
            finish_kernel,
            (1,),
            self.where,
            [whole(v) for v in pieces],
            [whole_out(share, f32)] + [whole_out(share, bf16)] * (owners - 1),
            [pltpu.VMEM((rows, 2 * columns), f32)],
            micros=0.002,
        )

    def work(self):
        if self.sent == 2:
            self.own, *self.ready = self.order(
                self.finish, self.kept[0], self.arrived[0], self.kept[1], self.arrived[1]
            )
            return
        if self.sent == 0:
            factors = [array for array, _ in (*self.lefts, *self.rights)]
            keep_a, send_a, keep_b, send_b = self.order(self.product, *factors)
        else:
            keep_a, send_a, keep_b, send_b = self.order(
                self.add, self.kept[0], self.arrived[0], self.kept[1], self.arrived[1]
            )
        self.kept = keep_a, keep_b
        self.ready = send_a, send_b

    def send(self, shares=()):
        if self.sent < 2:
            ready = self.order.tie(*self.ready)
            bits = (XBIT, YBIT) if self.sent else (YBIT, XBIT)
            self.arrived = self.swap(ready[0], bits[0]), self.swap(ready[1], bits[1])
            self.sent += 1
        elif self.flat:
            self.share = lax.psum_scatter(
                self.order.tie(self.own)[0], "fsdp", scatter_dimension=0, tiled=True
            )
        else:
            for by, piece in zip(shares, self.order.tie(*[self.ready[by - 1] for by in shares])):
                self.shares.append(self.along(piece, by))

    def meet(self):
        if self.flat:
            (self.share,) = self.order.tie(self.share)
            self.order.last = (self.share,)
        else:
            self.shares = list(self.order.tie(*self.shares))
            self.order.last = (self.shares[0],)

    def total(self):
        if self.flat:
            return self.share.astype(f32)
        return self.order(
            lambda own, *others: sum((piece.astype(f32) for piece in others), own), self.own, *self.shares
        )


class Order:
    def __init__(self):
        self.last = ()

    def __call__(self, function, *values):
        result = function(*self.tie(*values))
        self.last = (result[0] if isinstance(result, (tuple, list)) else result,)
        return result

    def tie(self, *values):
        return lax.optimization_barrier((*values, *self.last))[: len(values)]


def assemble_kernel(where, *refs):
    pieces, targets = [], []
    for ref in refs:
        (pieces if ref.shape[0] == refs[0].shape[0] else targets).append(ref)
    count = pieces[0].shape[0]
    columns = targets[0].shape[1]
    for at, piece in enumerate(pieces):
        rows = pl.ds(pl.multiple_of(where[at] * count, count), count)
        for side, target in enumerate(targets):
            target[rows, :] = piece[:, side * columns : (side + 1) * columns]


def assemble(count, places, *pieces):
    rows, columns = pieces[0].shape
    out = whole_out((rows * len(pieces), columns // count), bf16)
    return call(assemble_kernel, (1,), places, [whole(p) for p in pieces], [out] * count, micros=0.003)


def join_kernel(where, *refs):
    out = refs[-1]
    count = refs[0].shape[0]
    for side in range(2):

        @pl.when(pl.program_id(0) == side)
        def _(side=side):
            for at, piece in enumerate(refs[4 * side : 4 * side + 4]):
                out[at * count : (at + 1) * count, :] = piece[...]


def join(where, *pieces):
    rows, columns = pieces[3].shape
    ins = [first_columns(p, columns, at // 4 if p.shape[1] > columns else 0) for at, p in enumerate(pieces)]
    return call(
        join_kernel,
        (2,),
        where,
        ins,
        [((4 * rows, 2 * columns), bf16, (4 * rows, columns), column)],
        micros=4,
    )[0]


def split_kernel(where, near, far, left, right):
    left[...] = near[...]
    right[...] = far[...]


def split(where, near, far):
    rows, columns = near.shape[0], near.shape[1] // 2
    return call(
        split_kernel,
        (1,),
        where,
        [first_columns(near, columns, 0), first_columns(far, columns, 1)],
        [whole_out((rows, columns), bf16)] * 2,
    )


def unpack_kernel(where, low, high, *refs):
    outs, true = refs[:-1], refs[-1]
    for side, part in enumerate((low, high)):
        turned = part[...].astype(f32).T
        for at in range(4):
            true[:, lanes(where, 4 * side + at)] = turned[:, at * 128 : (at + 1) * 128]
    share = 32
    first = 0
    for vector in outs:
        columns = vector.shape[1] // true.shape[1]
        if columns == 1:
            vector[...] = true[first : first + 1, :]
        else:
            for owner in range(true.shape[1] // share):
                for at in range(columns):
                    start = (owner * columns + at) * share
                    vector[:, start : start + share] = true[
                        first + at : first + at + 1, owner * share : (owner + 1) * share
                    ]
        first += columns


def unpack(where, mats, sizes):
    block = mats[0].shape[1] // 128 - 2
    outs = [whole_out((1, size), f32) for size in sizes]
    rows = mats[0].shape[0]
    return call(
        unpack_kernel,
        (1,),
        where,
        [(mat, (rows, 128), lambda *_: (0, block)) for mat in mats],
        outs,
        [pltpu.VMEM((128, 2 * rows), f32)],
    )


def exchanged(fsdp_size, block_in, keep_mask, out_cotangent, *params):
    (g1, b1, qkv_weight, qv_bias, out_weight, out_bias, g2, b2, up_weight, up_bias, down_weight, down_bias) = params
    seqs, length, width = block_in.shape
    rows = seqs * length
    half = width // 2
    order = Order()
    me, line = lax.axis_index("dp"), lax.axis_index("fsdp")
    where = positions(me, line, fsdp_size)

    def swap(value, bit):
        return lax.ppermute(value, "dp", [(i, i ^ bit) for i in range(8)])

    def along(value, by):
        return lax.ppermute(value, "fsdp", [(i, (i + by) % fsdp_size) for i in range(fsdp_size)])

    class Gather:
        def start(self, left, right):
            left, right = self.own = order.tie(left, right)
            self.near = swap(left, XBIT), swap(right, XBIT)
            self.far = swap(left, YBIT), swap(right, YBIT)

        def turn(self, *others):
            *pieces, = order.tie(*self.near, *self.far, *others)
            self.near, self.far = tuple(pieces[:2]), tuple(pieces[2:4])
            left, right = self.near[0], self.far[1]
            order.last = (left,)
            self.last = swap(left, YBIT), swap(right, XBIT)

        def start_whole(self, block):
            block = order.tie(block)[0]
            self.own = block
            self.near, self.far = swap(block, XBIT), swap(block, YBIT)

        def turn_whole(self, *others):
            left, right = order(lambda near, far, *_: split(where, near, far), self.near, self.far, *others)
            self.last = swap(left, YBIT), swap(right, XBIT)

        def join(self, *others):
            sides = [v if isinstance(v, tuple) else (v, v) for v in (self.own, self.near, self.far)]
            pieces = [p for side in zip(*sides, self.last) for p in side]
            self.low = order(lambda *p: join(where, *p[:8]), *pieces, *others)

        def joined(self):
            low = order.tie(self.low)[0]
            self.mats = low, swap(low, CORE)

    def around(shard):
        return [shard] + [along(shard, by) for by in range(fsdp_size - 1, 0, -1)]

    vectors = (g1, b1, qv_bias, out_bias, g2, b2, up_bias, down_bias)
    device_count = 8 * fsdp_size
    sizes = [v.shape[0] * device_count for v in vectors]
    cuts = [sum(v.shape[0] for v in vectors[:i]) for i in range(1, len(vectors))]
    share = qkv_weight.shape[0]
    beside = lax.optimization_barrier(jnp.concatenate(vectors)).reshape(-1, share).T
    beside = jnp.pad(beside, ((0, 0), (0, 256 - beside.shape[1])))
    qkv_low = jnp.concatenate([qkv_weight, beside], 1).astype(bf16)
    behind = jnp.stack([(line + by) % fsdp_size for by in range(fsdp_size)]).astype(jnp.int32)
    qkv_pieces = around(qkv_low)
    up_low = jnp.concatenate([up_weight, out_weight], 1).astype(bf16)
    down_block = lax.all_gather(down_weight.astype(bf16), "fsdp", axis=0, tiled=True)

    keep = jnp.concatenate(
        [jnp.ones((seqs, length - keep_mask.shape[1]), jnp.int32), keep_mask], axis=1
    )
    keep_rows = keep.reshape(rows, 1).astype(f32)
    keep_column = keep.reshape(seqs, length, 1)
    inputs = block_in.reshape(rows, width)
    grad_feed = order(
        lambda g: jnp.where(keep_rows > 0, g, jnp.zeros((), bf16)), out_cotangent.reshape(rows, width)
    )
    down_bias_grad = jnp.sum(grad_feed.astype(f32), 0)

    qkv, up, down = Gather(), Gather(), Gather()
    qkv.start_whole(order(functools.partial(assemble, 1, behind), *qkv_pieces)[0])
    up_pieces = around(order.tie(up_low)[0])
    qkv.turn_whole()
    up_halves = order(functools.partial(assemble, 2, behind), *up_pieces)
    qkv.join()
    qkv.joined()
    up.start(*up_halves)
    g1, b1, qv_bias, out_bias, g2, b2, up_bias, down_bias = order(
        lambda *m: unpack(where, m, sizes), *qkv.mats
    )
    one_low, one_pack = order(functools.partial(norm_one, where), inputs, grad_feed, g1, b1)
    shift = jnp.concatenate([qv_bias[:, :width], jnp.zeros((1, width), f32), qv_bias[:, width:]], 1)
    projected = order(
        lambda lo, hi, s, *m: project(where, lo, hi, m, s), one_low, one_pack, shift, *qkv.mats
    )
    mixed_left, probs_left = order(lambda p: attention_forward(keep_column, p, 0), projected)
    up.turn(down_block)
    one_other = swap(order.tie(one_pack)[0], CORE)
    mixed_right, probs_right = order(lambda p: attention_forward(keep_column, p, 1), projected)
    down_halves = order(lambda b: (b[:, :half], b[:, half:]), down_block)
    up.join(one_other)
    up.joined()
    down.start(*down_halves)
    mixed = jnp.concatenate([mixed_left, mixed_right], 1)
    mix_low, middle, two_low, two_pack = order(
        lambda m, o, *mats: branch_norm(where, m, inputs, mats, o, g2, b2, length),
        mixed, out_bias, *up.mats,
    )
    hidden_high, slope_high = order(
        lambda lo, hi, s, *m: expand(where, 1, lo, hi, m, s), two_low, two_pack, up_bias, *up.mats
    )
    hidden_low, slope_low = order(
        lambda lo, hi, s, *m: expand(where, 0, lo, hi, m, s), two_low, two_pack, up_bias, *up.mats
    )
    down.turn()
    hidden_other = swap(order.tie(hidden_high)[0], CORE)
    two_other = swap(order.tie(two_pack)[0], CORE)
    down_sum = Sum(
        swap, along, order, where,
        [((hidden_low, 0), (hidden_other, 0))], [((grad_feed, 0), (one_other, half // 256))],
        256, [width // 256], True,
    )
    down_sum.work()
    down.join()
    down.joined()
    down_sum.send()
    grad_pre, up_bias_grad = order(
        lambda g, s0, s1, *m: shrink(where, g, m, (s0, s1)),
        grad_feed, slope_low, slope_high, *down.mats,
    )
    down_sum.work()
    down_sum.send()
    pre_other = swap(order.tie(grad_pre)[0], CORE)
    grad_middle, grad_branch, out_bias_grad, gain_two_grad, bias_two_grad, grad_mixed = order(
        lambda g, mid, above, *m: back(where, g, m, mid, above, g2),
        grad_pre, middle, grad_feed, *up.mats,
    )
    branch, pre_other = order.tie(grad_branch, pre_other)
    branch_other = swap(branch, CORE)
    down_sum.work()
    up_sum = Sum(
        swap, along, order, where,
        [((two_low, 0), (two_other, 1)), ((mix_low, 0), (two_other, 0))],
        [((grad_pre, 0), (pre_other, 0)), ((grad_branch, 0), (branch_other, 0))],
        512, [grad_pre.shape[1] // 512, width // 512], True,
    )
    up_sum.work()
    up_sum.send()
    down_sum.send()
    grad_projected, sum_q, sum_v = order(
        lambda p, g, *probs: attention_backward(probs, p, g),
        projected, grad_mixed, probs_left, probs_right,
    )
    block_out = order(
        lambda lo, hi, mid, s, *m: feed(where, lo, hi, m, mid, s, keep_rows),
        hidden_low, hidden_high, middle, down_bias, *down.mats,
    )
    down_sum.meet()
    up_sum.work()
    up_sum.send()
    projected_other = swap(order.tie(grad_projected)[0], CORE)
    qkv_sum = Sum(
        swap, along, order, where,
        [((one_low, 0), (one_other, 0))], [((grad_projected, 0), (projected_other, 0))],
        512, [3 * width // 512],
    )
    qkv_sum.work()
    qkv_sum.send()
    up_sum.work()
    up_sum.send()
    sums = [
        jnp.concatenate([sum_q, sum_v], 1),
        out_bias_grad,
        gain_two_grad,
        bias_two_grad,
        up_bias_grad,
        down_bias_grad.reshape(1, -1),
    ]
    input_grad, shares = order(
        lambda g, x, above, m0, m1, *v: back(where, g, (m0, m1), x, above, g1, v, device_count),
        grad_projected, inputs, grad_middle, *qkv.mats, *sums,
    )
    qkv_sum.work()
    qkv_sum.send()
    shares = order.tie(shares.reshape(2, 2, 2, fsdp_size, -1))[0]

    def halve(shares, axis, bit):
        low, high = (lax.index_in_dim(shares, side, axis, keepdims=False) for side in range(2))
        upper = me & bit > 0
        return jnp.where(upper, high, low), jnp.where(upper, low, high)

    mine, other = halve(shares, 2, CORE)
    mine, other = halve(mine + swap(other, CORE), 1, XBIT)
    up_sum.meet()
    mine, other = order.tie(mine, other)
    order.last = (mine,)
    qkv_sum.work()
    qkv_sum.send((1, 2, 3))
    shares = mine + swap(order.tie(other)[0], XBIT)
    qkv_sum.shares[0], shares = order.tie(qkv_sum.shares[0], shares)
    order.last = (qkv_sum.shares[0],)
    mine, other = halve(shares, 0, YBIT)
    shares = mine + swap(other, YBIT)

    def row_of(by):
        return lax.dynamic_slice(shares, ((line + by) % fsdp_size, 0), (1, shares.shape[1]))

    line_shares = [along(row_of(by), by) for by in range(1, fsdp_size)]
    down_grad, up_grad = down_sum.total(), up_sum.total()
    up_grad, out_grad = up_grad[:, : up_weight.shape[1]], up_grad[:, up_weight.shape[1] :]
    qkv_grad = qkv_sum.total()
    mine = sum(line_shares, row_of(0))
    v = jnp.split(mine[0], cuts)
    return (
        block_out.reshape(seqs, length, width),
        input_grad.reshape(seqs, length, width),
        v[0],
        v[1],
        qkv_grad,
        v[2],
        out_grad,
        v[3],
        v[4],
        v[5],
        up_grad,
        v[6],
        down_grad,
        v[7],
    )


def solution(mesh):
    dp_size, fsdp_size = mesh.shape["dp"], mesh.shape["fsdp"]
    if dp_size == 8:
        local = functools.partial(exchanged, fsdp_size)
    else:
        local = functools.partial(gathered, dp_size * fsdp_size)
    row = P(AXES, None)
    vec = P(AXES)
    cube = P(AXES, None, None)
    return jax.shard_map(
        local,
        mesh=mesh,
        in_specs=(cube, row, cube, vec, vec, row, vec, row, vec, vec, vec, row, vec, row, vec),
        out_specs=(cube, cube, vec, vec, row, vec, row, vec, vec, vec, row, vec, row, vec),
        check_vma=False,
    )
```

```python
import functools
import math

import jax
import jax.numpy as jnp
from jax import lax
from jax.experimental import pallas as pl
from jax.experimental.pallas import tpu as pltpu
from jax.sharding import PartitionSpec as P

HD = 64
EPSILON = 1e-05
AXES = ("dp", "fsdp")
bf16 = jnp.bfloat16
f32 = jnp.float32
NN = (((1,), (0,)), ((), ()))
NT = (((1,), (1,)), ((), ()))
TN = (((0,), (0,)), ((), ()))


def dot(left, right, dims=NN):
    return lax.dot_general(left, right, dims, preferred_element_type=f32)


def attention_forward_kernel(seqs, length, keep_ref, q_ref, k_ref, v_ref, o_ref, p_ref):
    scale = 1.0 / math.sqrt(HD)
    for s in range(seqs):
        rows = slice(s * length, (s + 1) * length)
        visible = keep_ref[s] > 0
        mixed = []
        for h in range(128 // HD):
            cols = slice(h * HD, (h + 1) * HD)
            logits = dot(k_ref[rows, cols], q_ref[rows, cols] * scale, NT)
            logits = jnp.where(visible, logits, -1e9)
            raised = jnp.exp(logits - jnp.max(logits, 0, keepdims=True))
            probs = (raised * (1.0 / jnp.sum(raised, 0, keepdims=True))).astype(bf16)
            p_ref[h, s] = probs
            mixed.append(dot(probs, v_ref[rows, cols], TN))
        o_ref[rows, :] = jnp.concatenate(mixed, 1).astype(bf16)


def attention_backward_kernel(
    seqs, length, left_ref, right_ref, q_ref, k_ref, v_ref, do_ref, dp_ref, sq_ref, sv_ref
):
    scale = 1.0 / math.sqrt(HD)

    def work(p_ref):
        sum_q = jnp.zeros((1, 128), f32)
        sum_v = jnp.zeros((1, 128), f32)
        for s in range(seqs):
            rows = slice(s * length, (s + 1) * length)
            dqs, dks, dvs = [], [], []
            for h in range(128 // HD):
                cols = slice(h * HD, (h + 1) * HD)
                queries = q_ref[rows, cols] * scale
                grad_mixed = do_ref[rows, cols]
                low_probs = p_ref[h, s]
                grad_probs = dot(v_ref[rows, cols], grad_mixed, NT)
                dvs.append(dot(low_probs, grad_mixed))
                probs = low_probs.astype(f32)
                row_terms = jnp.sum(grad_probs * probs, 0, keepdims=True)
                grad_logits = (probs * (grad_probs - row_terms)).astype(bf16)
                dks.append(dot(grad_logits, queries))
                dqs.append(dot(grad_logits, k_ref[rows, cols], TN) * scale)
            dq = jnp.concatenate(dqs, 1).astype(bf16)
            dv = jnp.concatenate(dvs, 1).astype(bf16)
            dp_ref[0, rows, :] = dq
            dp_ref[1, rows, :] = jnp.concatenate(dks, 1).astype(bf16)
            dp_ref[2, rows, :] = dv
            sum_q += jnp.sum(dq.astype(f32), 0, keepdims=True)
            sum_v += jnp.sum(dv.astype(f32), 0, keepdims=True)
        sq_ref[...] = sum_q
        sv_ref[...] = sum_v

    half = pl.num_programs(0) // 2

    @pl.when(pl.program_id(0) < half)
    def _():
        work(left_ref)

    @pl.when(pl.program_id(0) >= half)
    def _():
        work(right_ref)


def attention_forward(keep, project, part):
    seqs, length = keep.shape[:2]
    rows, width = project.shape[0], project.shape[1] // 6
    steps = width // 128
    pair = 128 // HD
    project = pltpu.with_memory_space_constraint(project, pltpu.HBM)
    return pl.pallas_call(
        functools.partial(attention_forward_kernel, seqs, length),
        grid=(steps,),
        in_specs=[pl.BlockSpec((seqs, length, 1), lambda i: (0, 0, 0))]
        + [
            pl.BlockSpec((rows, 128), lambda i, at=at: (0, i + (2 * at + part) * steps))
            for at in range(3)
        ],
        out_specs=[
            pl.BlockSpec((rows, 128), lambda i: (0, i)),
            pl.BlockSpec((pair, seqs, length, length), lambda i: (i, 0, 0, 0)),
        ],
        out_shape=[
            jax.ShapeDtypeStruct((rows, width), bf16),
            pltpu.HBM((steps * pair, seqs, length, length), bf16),
        ],
        compiler_params=pltpu.CompilerParams(vmem_limit_bytes=20 << 20),
        cost_estimate=pl.CostEstimate(flops=int(8.5 * COST), bytes_accessed=1, transcendentals=0),
    )(keep, project, project, project)


def attention_backward(probs, project, grad_mixed):
    pairs, seqs, length = probs[0].shape[:3]
    rows, width = grad_mixed.shape
    steps = width // 128
    pair = 128 // HD
    block = pl.BlockSpec((rows, 128), lambda i: (0, i))
    vector = pl.BlockSpec((1, 128), lambda i: (0, i))
    sums = jax.ShapeDtypeStruct((1, width), f32)
    shape = (pair, seqs, length, length)
    project, grad_mixed, left, right = (
        pltpu.with_memory_space_constraint(v, pltpu.HBM) for v in (project, grad_mixed, *probs)
    )
    return pl.pallas_call(
        functools.partial(attention_backward_kernel, seqs, length),
        grid=(steps,),
        in_specs=[
            pl.BlockSpec(shape, lambda i: (jnp.minimum(i, steps // 2 - 1), 0, 0, 0)),
            pl.BlockSpec(shape, lambda i: (jnp.maximum(i - steps // 2, 0), 0, 0, 0)),
        ]
        + [pl.BlockSpec((rows, 128), lambda i, at=at: (0, i + at * steps)) for at in range(3)]
        + [block],
        out_specs=[pl.BlockSpec((3, rows, 128), lambda i: (0, 0, i)), vector, vector],
        out_shape=[pltpu.HBM((3, rows, width), bf16), sums, sums],
        compiler_params=pltpu.CompilerParams(vmem_limit_bytes=24 << 20),
        cost_estimate=pl.CostEstimate(flops=int(22 * COST), bytes_accessed=1, transcendentals=0),
    )(left, right, project, project, project, grad_mixed)


def norm_forward(values, norm_gain, norm_bias):
    average = jnp.mean(values, -1, keepdims=True)
    centered = values - average
    inverse = lax.rsqrt(jnp.mean(centered * centered, -1, keepdims=True) + EPSILON)
    normed = centered * inverse
    return (normed * norm_gain + norm_bias, normed, inverse)


def norm_backward(grad_norm, normed, inverse, norm_gain):
    scaled = grad_norm * norm_gain
    return inverse * (
        scaled
        - jnp.mean(scaled, -1, keepdims=True)
        - normed * jnp.mean(scaled * normed, -1, keepdims=True)
    )


def gathered(device_count, block_in, keep_mask, out_cotangent, *params):
    (g1, b1, qkv_weight, qv_bias, out_weight, out_bias, g2, b2, up_weight, up_bias, down_weight, down_bias) = params
    seqs, length, width = block_in.shape
    rows = seqs * length
    vectors = (g1, b1, qv_bias, out_bias, g2, b2, up_bias, down_bias)
    sizes = [v.shape[0] for v in vectors]
    cuts = [sum(sizes[:i]) for i in range(1, len(sizes))]
    packed = lax.all_gather(jnp.concatenate(vectors).astype(bf16), AXES, axis=0, tiled=False)
    g1, b1, qv_bias, out_bias, g2, b2, up_bias, down_bias = (
        part.reshape(-1).astype(f32) for part in jnp.split(packed, cuts, axis=1)
    )
    qkv_mat, out_mat, up_mat, down_mat = (
        lax.all_gather(w.astype(bf16), AXES, axis=0, tiled=True)
        for w in (qkv_weight, out_weight, up_weight, down_weight)
    )
    keep = jnp.concatenate(
        [jnp.ones((seqs, length - keep_mask.shape[1]), jnp.int32), keep_mask], axis=1
    )
    keep_rows = keep.reshape(rows, 1).astype(f32)
    keep_column = keep.reshape(seqs, length, 1)
    inputs = block_in.astype(f32).reshape(rows, width)
    grad_out = out_cotangent.astype(f32).reshape(rows, width) * keep_rows
    grad_feed = grad_out.astype(bf16)

    normed_one, plain_one, inverse_one = norm_forward(inputs, g1, b1)
    act_one = normed_one.astype(bf16)
    zeros = jnp.zeros((width,), f32)
    shift = jnp.concatenate([qv_bias[:width], zeros, qv_bias[width:]])
    project = (dot(act_one, qkv_mat) + shift).astype(bf16)

    (mixed_left, probs_left), (mixed_right, probs_right) = (
        attention_forward(keep_column, project, part) for part in range(2)
    )
    mixed = jnp.concatenate([mixed_left, mixed_right], 1)
    middle = inputs + dot(mixed, out_mat) + out_bias
    normed_two, plain_two, inverse_two = norm_forward(middle, g2, b2)
    act_two = normed_two.astype(bf16)
    pre = dot(act_two, up_mat) + up_bias
    cumul = 0.5 * (1.0 + lax.erf(pre * 0.7071067811865476))
    hidden = (pre * cumul).astype(bf16)
    slope = cumul + pre * jnp.exp(-0.5 * pre * pre) * 0.3989422804014327
    feed = dot(hidden, down_mat) + down_bias
    block_out = keep_rows * (middle + feed)

    grad_pre = (dot(grad_feed, down_mat, NT) * slope).astype(bf16)
    grad_act_two = dot(grad_pre, up_mat, NT)
    grad_middle = grad_out + norm_backward(grad_act_two, plain_two, inverse_two, g2)
    grad_branch = grad_middle.astype(bf16)
    grad_mixed = dot(grad_branch, out_mat, NT).astype(bf16)
    grad_parts, sum_q, sum_v = attention_backward((probs_left, probs_right), project, grad_mixed)
    grad_project = jnp.concatenate([grad_parts[i] for i in range(3)], 1)
    grad_act_one = dot(grad_project, qkv_mat, NT)
    input_grad = grad_middle + norm_backward(grad_act_one, plain_one, inverse_one, g1)
    grads = (
        jnp.sum(grad_act_one * plain_one, 0),
        jnp.sum(grad_act_one, 0),
        jnp.concatenate([sum_q[0], sum_v[0]]),
        jnp.sum(grad_branch.astype(f32), 0),
        jnp.sum(grad_act_two * plain_two, 0),
        jnp.sum(grad_act_two, 0),
        jnp.sum(grad_pre.astype(f32), 0),
        jnp.sum(grad_feed.astype(f32), 0),
    )
    shares = jnp.concatenate([g.reshape(device_count, -1) for g in grads], 1)
    v = jnp.split(lax.psum_scatter(shares, AXES, scatter_dimension=0, tiled=False), cuts)

    def to_owner(left, right):
        total = dot(left, right, TN).astype(bf16)
        return lax.psum_scatter(total, AXES, scatter_dimension=0, tiled=True).astype(f32)

    return (
        block_out.reshape(seqs, length, width),
        input_grad.reshape(seqs, length, width),
        v[0],
        v[1],
        to_owner(act_one, grad_project),
        v[2],
        to_owner(mixed, grad_branch),
        v[3],
        v[4],
        v[5],
        to_owner(act_two, grad_pre),
        v[6],
        to_owner(hidden, grad_feed),
        v[7],
    )


CORE, XBIT, YBIT = 1, 2, 4
BLOCKS = [c * CORE + y * YBIT + x * XBIT for c in range(2) for y in range(2) for x in range(2)]
COST = 1e12


def positions(me, line, count):
    true = [me ^ r for r in BLOCKS]
    place = [
        sum(jnp.where((me ^ d) == r, at, 0) for at, r in enumerate(BLOCKS)) for d in range(8)
    ]
    ahead = [(line + by) % count for by in range(count)]
    return jnp.stack(true + place + ahead).astype(jnp.int32)


def call(kernel, grid, where, ins, outs, scratch=(), micros=3, sent=(), stream=False):
    held = 6 << 20
    specs = []
    arrays = []
    for array, block, index in ins:
        if block is None:
            arrays.append(pltpu.with_memory_space_constraint(array, pltpu.HBM) if stream else array)
            specs.append(pl.BlockSpec(memory_space=pl.ANY))
            continue
        once = tuple(block) == tuple(array.shape)
        if stream and not once:
            array = pltpu.with_memory_space_constraint(array, pltpu.HBM)
        arrays.append(array)
        size = math.prod(n or 1 for n in block) * array.dtype.itemsize
        held += size if once else 2 * size
        specs.append(pl.BlockSpec(block, index, pipeline_mode=pl.Buffered(1) if once else None))
    for _, dtype, block, _ in outs:
        held += 2 * math.prod(block) * jnp.dtype(dtype).itemsize
    for buffer in scratch:
        if len(buffer.shape) > 1:
            held += math.prod(buffer.shape) * jnp.dtype(buffer.dtype).itemsize
    return pl.pallas_call(
        kernel,
        grid_spec=pltpu.PrefetchScalarGridSpec(
            num_scalar_prefetch=1,
            grid=grid,
            in_specs=specs,
            out_specs=[pl.BlockSpec(block, index) for _, _, block, index in outs],
            scratch_shapes=list(scratch),
        ),
        out_shape=[
            pltpu.HBM(shape, dtype) if at in sent else jax.ShapeDtypeStruct(shape, dtype)
            for at, (shape, dtype, _, _) in enumerate(outs)
        ],
        compiler_params=pltpu.CompilerParams(vmem_limit_bytes=held),
        cost_estimate=pl.CostEstimate(flops=int(micros * COST), bytes_accessed=1, transcendentals=0),
    )(where, *arrays)


def whole(array):
    return (array, array.shape, lambda *_: (0,) * array.ndim)


def whole_out(shape, dtype):
    return (shape, dtype, shape, lambda *_: (0,) * len(shape))


def column(i, *_):
    return (0, i)


def lanes(where, at):
    return pl.ds(pl.multiple_of(where[at] * 128, 128), 128)


def deal(where, source, low, high):
    for at in range(4):
        cols = slice(at * 128, (at + 1) * 128)
        low[:, cols] = source[:, lanes(where, at)]
        high[:, cols] = source[:, lanes(where, 4 + at)]


def normalize(values):
    centered = values - jnp.mean(values, -1, keepdims=True)
    inverse = lax.rsqrt(jnp.mean(centered * centered, -1, keepdims=True) + EPSILON)
    return centered * inverse, inverse


def norm_kernel(where, x_ref, grad_ref, gain_ref, bias_ref, low_ref, pack_ref, whole_ref):
    normed, _ = normalize(x_ref[...].astype(f32))
    whole_ref[...] = (normed * gain_ref[...] + bias_ref[...]).astype(bf16)
    half = low_ref.shape[1]
    deal(where, whole_ref, low_ref, pack_ref.at[:, :half])
    pack_ref[:, half:] = grad_ref[...]


def norm_one(where, inputs, grad_feed, gain, bias):
    rows, width = inputs.shape
    index = lambda i, _: (i, 0)
    return call(
        norm_kernel,
        (rows // 128,),
        where,
        [(inputs, (128, width), index), (grad_feed, (128, width), index), whole(gain), whole(bias)],
        [
            ((rows, width // 2), bf16, (128, width // 2), index),
            ((rows, width // 2 + width), bf16, (128, width // 2 + width), index),
        ],
        [pltpu.VMEM((128, width), bf16)],
    )


def project_kernel(where, low_ref, high_ref, mat_low, mat_high, bias_ref, out_ref):
    total = dot(low_ref[...], mat_low[...]) + dot(high_ref[...], mat_high[...])
    out_ref[...] = (total + bias_ref[...]).astype(bf16)


def project(where, low, pack, mats, bias):
    rows, depth = low.shape
    columns = bias.shape[1]
    tile = ((depth, 512), column)
    return call(
        project_kernel,
        (columns // 512,),
        where,
        [whole(low), first_columns(pack, depth), (mats[0], *tile), (mats[1], *tile), (bias, (1, 512), column)],
        [((rows, columns), bf16, (rows, 512), column)], micros=8, sent=(0,))[0]


def branch_kernel(
    where, mixed_ref, x_ref, mat_low, mat_high, shift_ref, gain_ref, bias_ref,
    mix_low, middle_ref, two_low, pack_ref, whole_ref,
):
    half = mix_low.shape[1]
    mix_high, two_high = pack_ref.at[:, :half], pack_ref.at[:, half:]
    deal(where, mixed_ref, mix_low, mix_high)
    total = dot(mix_low[...], mat_low[...]) + dot(mix_high[...], mat_high[...])
    middle = x_ref[...].astype(f32) + total + shift_ref[...]
    middle_ref[...] = middle
    normed, _ = normalize(middle)
    whole_ref[...] = (normed * gain_ref[...] + bias_ref[...]).astype(bf16)
    deal(where, whole_ref, two_low, two_high)


def branch_norm(where, mixed, inputs, mats, shift, gain, bias, length):
    rows, width = inputs.shape
    block = ((length, width), lambda i, _: (i, 0))
    part = ((rows, width // 2), bf16, (length, width // 2), lambda i, _: (i, 0))
    return call(
        branch_kernel,
        (rows // length,),
        where,
        [(mixed, *block), (inputs, *block), *[last_columns(m, width) for m in mats]]
        + [whole(v) for v in (shift, gain, bias)],
        [part, ((rows, width), f32, *block), part, ((rows, width), bf16, *block)],
        [pltpu.VMEM((length, width), bf16)],
        micros=4,
    )


def first_columns(mat, count, at=0):
    return (mat, (mat.shape[0], count), lambda *_: (0, at))


def last_columns(mat, count):
    at = mat.shape[1] // count - 1
    return (mat, (mat.shape[0], count), lambda *_: (0, at))


def expand_kernel(where, low_ref, high_ref, mat_low, mat_high, shift_ref, hidden_ref, slope_ref):
    chunk = low_ref.shape[0] // 4
    for at in range(4):
        rows = slice(at * chunk, (at + 1) * chunk)
        pre = dot(low_ref[rows, :], mat_low[...]) + dot(high_ref[rows, :], mat_high[...])
        pre = pre + shift_ref[...]
        cumul = 0.5 * (1.0 + lax.erf(pre * 0.7071067811865476))
        hidden_ref[rows, :] = (pre * cumul).astype(bf16)
        slope = cumul + pre * jnp.exp(-0.5 * pre * pre) * 0.3989422804014327
        slope_ref[rows, :] = slope.astype(bf16)


def expand(where, side, low, pack, mats, shift):
    rows, depth = low.shape
    columns = shift.shape[1]
    tile = columns // 8
    true = lambda i, where: (0, where[4 * side + i])
    return call(
        expand_kernel,
        (4,),
        where,
        [
            whole(low),
            first_columns(pack, depth, 1),
            (mats[0], (depth, tile), true),
            (mats[1], (depth, tile), true),
            (shift, (1, tile), true),
        ],
        [((rows, columns // 2), bf16, (rows, tile), column)] * 2,
        micros=7,
        sent=(0, 1),
    )


def shrink_kernel(where, grad_ref, mat_low, mat_high, slope_low, slope_high, out_ref, sum_ref):
    for side, (mat, slope) in enumerate(((mat_low, slope_low), (mat_high, slope_high))):

        @pl.when(pl.program_id(0) // 4 == side)
        def _(mat=mat, slope=slope):
            grad = (dot(grad_ref[...], mat[...], NT) * slope[...].astype(f32)).astype(bf16)
            out_ref[...] = grad
            sum_ref[...] = jnp.sum(grad.astype(f32), 0, keepdims=True)


def shrink(where, grad, mats, slopes):
    rows, width = grad.shape
    columns = 2 * slopes[0].shape[1]
    tile = columns // 8
    true = lambda i, where: (0, where[i])
    near = lambda i, _: jnp.minimum(i, 3)
    far = lambda i, _: jnp.maximum(i - 4, 0)
    return call(
        shrink_kernel,
        (8,),
        where,
        [
            whole(grad),
            (mats[0], (tile, width), lambda i, _: (near(i, _), 0)),
            (mats[1], (tile, width), lambda i, _: (far(i, _), 0)),
            (slopes[0], (rows, tile), lambda i, _: (0, near(i, _))),
            (slopes[1], (rows, tile), lambda i, _: (0, far(i, _))),
        ],
        [((rows, columns), bf16, (rows, tile), true), ((1, columns), f32, (1, tile), true)],
        micros=12,
        stream=True,
    )


def back_kernel(low, where, grad_ref, mat_low, mat_high, values_any, above_any, gain_ref, *rest):
    *rest, total, values_ref, above_ref, sems = rest
    if low:
        out_low, out_high, out_ref, low_ref, low_sum, gain_sum, bias_sum, mixed_ref = rest
    else:
        *vectors, out_ref, packed = rest
    step = pl.program_id(0)
    fetches = [
        pltpu.make_async_copy(values_any, values_ref, sems.at[0]),
        pltpu.make_async_copy(above_any, above_ref, sems.at[1]),
    ]

    @pl.when(step == 0)
    def _():
        for fetch in fetches:
            fetch.start()

    half = mat_low.shape[0]
    for side, mat in enumerate((mat_low, mat_high)):
        cols = slice(side * half, (side + 1) * half)
        part = dot(grad_ref[...], mat[...], NT)

        @pl.when(step == 0)
        def _(cols=cols, part=part):
            total[:, cols] = part

        @pl.when(step > 0)
        def _(cols=cols, part=part):
            total[:, cols] += part

    @pl.when(step == pl.num_programs(0) - 1)
    def _():
        for fetch in fetches:
            fetch.wait()
        count, width = values_ref.shape
        chunk = 64
        sums = [jnp.zeros((1, width), f32)] * 3
        for first in range(0, count, chunk):
            rows = slice(first, first + chunk)
            normed, inverse = normalize(values_ref[rows, :].astype(f32))
            grad = jnp.concatenate([total[rows, lanes(where, 8 + block)] for block in range(8)], 1)
            scaled = grad * gain_ref[...]
            result = above_ref[rows, :].astype(f32) + inverse * (
                scaled
                - jnp.mean(scaled, -1, keepdims=True)
                - normed * jnp.mean(scaled * normed, -1, keepdims=True)
            )
            out_ref[rows, :] = result
            sums[0] += jnp.sum(grad * normed, 0, keepdims=True)
            sums[1] += jnp.sum(grad, 0, keepdims=True)
            if low:
                rounded = result.astype(bf16)
                low_ref[rows, :] = rounded
                sums[2] += jnp.sum(rounded.astype(f32), 0, keepdims=True)
        if low:
            gain_sum[...] = sums[0]
            bias_sum[...] = sums[1]
            low_sum[...] = sums[2]
            for at in range(4):
                mat = (out_low, out_high)[at // 2][at % 2 * 256 : at % 2 * 256 + 256, :]
                part = dot(low_ref[...], mat, NT).astype(bf16)
                for side in range(2):
                    mixed_ref[:, lanes(where, 2 * at + side)] = part[:, side * 128 : (side + 1) * 128]
        else:
            owners = packed.shape[0]
            at = 0
            for vector in (*sums[:2], *[ref[...] for ref in vectors]):
                share = vector.shape[1] // owners
                for owner in range(owners):
                    packed[owner : owner + 1, at : at + share] = vector[
                        :, owner * share : (owner + 1) * share
                    ]
                at += share


def back(where, grad, mats, values, above, gain, vectors=(), owners=0):
    low = not vectors
    rows, width = values.shape
    depth = mats[0].shape[0]
    tile = 1024
    outs = [whole_out((rows, width), f32)]
    if low:
        steps = grad.shape[1] // tile
        grad_block = (grad, (rows, tile), column)
        outs += [whole_out((rows, width), bf16)] + [whole_out((1, width), f32)] * 3
        outs += [whole_out((rows, width), bf16)]
    else:
        steps = grad.shape[0]
        grad_block = (grad, (None, rows, tile), lambda i, _: (i, 0, 0))
        columns_packed = (2 * width + sum(v.shape[1] for v in vectors)) // owners
        outs += [whole_out((owners, columns_packed), f32)]
    return call(
        functools.partial(back_kernel, low),
        (steps,),
        where,
        [
            grad_block,
            (mats[0], (depth, tile), column),
            (mats[1], (depth, tile), column),
            (values, None, None),
            (above, None, None),
            whole(gain),
            *[last_columns(m, width) for m in mats if low],
            *[whole(v) for v in vectors],
        ],
        outs,
        [
            pltpu.VMEM((rows, width), f32),
            pltpu.VMEM((rows, width), values.dtype),
            pltpu.VMEM((rows, width), above.dtype),
            pltpu.SemaphoreType.DMA((2,)),
        ],
        micros=13 if low else 0.005,
        stream=not low,
        sent=(0, 1, 5) if low else (),
    )


def feed_kernel(where, low_ref, high_ref, mat_low, mat_high, middle_ref, shift_ref, keep_ref, out_ref):
    total = dot(low_ref[...], mat_low[...]) + dot(high_ref[...], mat_high[...])
    out_ref[...] = keep_ref[...] * (total + middle_ref[...] + shift_ref[...])


def feed(where, low, high, mats, middle, shift, keep):
    rows, width = middle.shape
    mat = ((mats[0].shape[0], 256), column)
    return call(
        feed_kernel,
        (width // 256,),
        where,
        [
            whole(low),
            whole(high),
            (mats[0], *mat),
            (mats[1], *mat),
            (middle, (rows, 256), column),
            (shift, (1, 256), column),
            whole(keep),
        ],
        [((rows, width), f32, (rows, 256), column)], micros=0.002, stream=True)[0]


def product_kernel(counts, where, *refs):
    n = len(counts)
    lefts, rights, outs, turned = refs[: 2 * n], refs[2 * n : 4 * n], refs[4 * n : -2 * n], refs[-2 * n :]
    keep_a, send_a, keep_b, send_b = outs
    step = pl.program_id(0)
    middle = sum(counts) // 2

    @pl.when(step == 0)
    def _():
        for left, turn in zip(lefts, turned):
            turn[...] = left[...].T

    def put(pair, targets):
        own, other = turned[2 * pair : 2 * pair + 2]
        right, right_other = rights[2 * pair : 2 * pair + 2]
        count = own.shape[0] // 4
        total = (dot(own[...], right[...]) + dot(other[...], right_other[...])).astype(bf16)
        for target, blocks in targets:
            for at, block in enumerate(blocks):
                target[at * count : (at + 1) * count, :] = total[block * count : (block + 1) * count, :]

    first = 0
    for pair, count in enumerate(counts):
        here = (step >= first) & (step < first + count)

        @pl.when(here & (step < middle))
        def _(pair=pair):
            put(pair, ((keep_a, (0, 1)), (send_a, (2, 3))))

        @pl.when(here & (step >= middle))
        def _(pair=pair):
            put(pair, ((keep_b, (0, 2)), (send_b, (1, 3))))

        first += count


def add_kernel(where, a0, a1, b0, b1, keep_a, send_a, keep_b, send_b):
    half = a0.shape[0] // 2
    for kept, piece, targets in ((a0, a1, (keep_a, send_a)), (b0, b1, (keep_b, send_b))):
        for part, target in enumerate(targets):
            rows = slice(part * half, (part + 1) * half)
            total = kept[rows, :].astype(f32) + piece[rows, :].astype(f32)
            target[...] = total.astype(bf16)


def flat_kernel(where, a0, a1, b0, b1, out):
    columns = a0.shape[1]
    for side, (kept, piece) in enumerate(((a0, a1), (b0, b1))):
        total = kept[...].astype(f32) + piece[...].astype(f32)
        out[:, side * columns : (side + 1) * columns] = total.astype(bf16)


def finish_kernel(where, a0, a1, b0, b1, *refs):
    own, *others, total = refs
    columns = a0.shape[1]
    for side, (kept, piece) in enumerate(((a0, a1), (b0, b1))):
        total[:, side * columns : (side + 1) * columns] = kept[...].astype(f32) + piece[...].astype(f32)
    count = own.shape[0]
    for at, out in enumerate((own, *others)):
        rows = pl.ds(pl.multiple_of(where[16 + at] * count, count), count)
        out[...] = total[rows, :].astype(out.dtype)


class Sum:
    def __init__(self, swap, along, order, where, lefts, rights, tile, counts, flat=False):
        self.swap, self.along, self.order, self.where = swap, along, order, where
        self.lefts = [left for pair in lefts for left in pair]
        self.rights = [right for pair in rights for right in pair]
        self.tile, self.counts, self.flat = tile, counts, flat
        self.sent = 0
        self.shares = []

    def product(self, *arrays):
        n = len(self.counts)
        lefts, rights = arrays[: 2 * n], arrays[2 * n :]
        depth = lefts[0].shape[0]
        count = self.lefts[0][0].shape[1]
        specs = [first_columns(left, count, at) for left, (_, at) in zip(lefts, self.lefts)]
        first = 0
        for pair, steps in enumerate(self.counts):
            for right, (_, base) in list(zip(rights, self.rights))[2 * pair : 2 * pair + 2]:
                at = lambda i, first=first, steps=steps, base=base: base + jnp.clip(i - first, 0, steps - 1)
                if right.ndim == 2:
                    specs.append((right, (depth, self.tile), lambda i, _, at=at: (0, at(i))))
                else:
                    per = right.shape[2] // self.tile
                    specs.append(
                        (right, (None, depth, self.tile), lambda i, _, at=at: (at(i) // per, 0, at(i) % per))
                    )
            first += steps
        near = lambda i, _: (0, jnp.minimum(i, first // 2 - 1))
        far = lambda i, _: (0, jnp.maximum(i - first // 2, 0))
        shape = (count // 2, self.tile * first // 2)
        block = (count // 2, self.tile)
        return call(
            functools.partial(product_kernel, self.counts),
            (first,),
            self.where,
            specs,
            [(shape, bf16, block, near)] * 2 + [(shape, bf16, block, far)] * 2,
            [pltpu.VMEM((count, depth), bf16)] * (2 * n),
            micros=12,
            sent=(0, 1, 2, 3),
        )

    def add(self, *pieces):
        rows, columns = pieces[0].shape
        tile = columns // 2
        block = ((rows, tile), column)
        half = ((rows // 2, columns), bf16, (rows // 2, tile), column)
        return call(
            add_kernel, (columns // tile,), self.where, [(v, *block) for v in pieces], [half] * 4, stream=True,
            micros=3 if self.flat else 0.005,
        )

    def finish(self, *pieces):
        rows, columns = pieces[0].shape
        if self.flat:
            out = whole_out((rows, 2 * columns), bf16)
            return call(flat_kernel, (1,), self.where, [whole(v) for v in pieces], [out])
        owners = self.where.shape[0] - 16
        share = (rows // owners, 2 * columns)
        return call(
            finish_kernel,
            (1,),
            self.where,
            [whole(v) for v in pieces],
            [whole_out(share, f32)] + [whole_out(share, bf16)] * (owners - 1),
            [pltpu.VMEM((rows, 2 * columns), f32)],
            micros=0.002,
        )

    def work(self):
        if self.sent == 2:
            self.own, *self.ready = self.order(
                self.finish, self.kept[0], self.arrived[0], self.kept[1], self.arrived[1]
            )
            return
        if self.sent == 0:
            factors = [array for array, _ in (*self.lefts, *self.rights)]
            keep_a, send_a, keep_b, send_b = self.order(self.product, *factors)
        else:
            keep_a, send_a, keep_b, send_b = self.order(
                self.add, self.kept[0], self.arrived[0], self.kept[1], self.arrived[1]
            )
        self.kept = keep_a, keep_b
        self.ready = send_a, send_b

    def send(self, shares=()):
        if self.sent < 2:
            ready = self.order.tie(*self.ready)
            bits = (XBIT, YBIT) if self.sent else (YBIT, XBIT)
            self.arrived = self.swap(ready[0], bits[0]), self.swap(ready[1], bits[1])
            self.sent += 1
        elif self.flat:
            self.share = lax.psum_scatter(
                self.order.tie(self.own)[0], "fsdp", scatter_dimension=0, tiled=True
            )
        else:
            for by, piece in zip(shares, self.order.tie(*[self.ready[by - 1] for by in shares])):
                self.shares.append(self.along(piece, by))

    def meet(self):
        if self.flat:
            (self.share,) = self.order.tie(self.share)
            self.order.last = (self.share,)
        else:
            self.shares = list(self.order.tie(*self.shares))
            self.order.last = (self.shares[0],)

    def total(self):
        if self.flat:
            return self.share.astype(f32)
        return self.order(
            lambda own, *others: sum((piece.astype(f32) for piece in others), own), self.own, *self.shares
        )


class Order:
    def __init__(self):
        self.last = ()

    def __call__(self, function, *values):
        result = function(*self.tie(*values))
        self.last = (result[0] if isinstance(result, (tuple, list)) else result,)
        return result

    def tie(self, *values):
        return lax.optimization_barrier((*values, *self.last))[: len(values)]


def assemble_kernel(where, *refs):
    pieces, targets = [], []
    for ref in refs:
        (pieces if ref.shape[0] == refs[0].shape[0] else targets).append(ref)
    count = pieces[0].shape[0]
    columns = targets[0].shape[1]
    for at, piece in enumerate(pieces):
        rows = pl.ds(pl.multiple_of(where[at] * count, count), count)
        for side, target in enumerate(targets):
            target[rows, :] = piece[:, side * columns : (side + 1) * columns]


def assemble(count, places, *pieces):
    rows, columns = pieces[0].shape
    out = whole_out((rows * len(pieces), columns // count), bf16)
    return call(assemble_kernel, (1,), places, [whole(p) for p in pieces], [out] * count, micros=0.003)


def join_kernel(where, *refs):
    out = refs[-1]
    count = refs[0].shape[0]
    for side in range(2):

        @pl.when(pl.program_id(0) == side)
        def _(side=side):
            for at, piece in enumerate(refs[4 * side : 4 * side + 4]):
                out[at * count : (at + 1) * count, :] = piece[...]


def join(where, *pieces):
    rows, columns = pieces[3].shape
    ins = [first_columns(p, columns, at // 4 if p.shape[1] > columns else 0) for at, p in enumerate(pieces)]
    return call(
        join_kernel,
        (2,),
        where,
        ins,
        [((4 * rows, 2 * columns), bf16, (4 * rows, columns), column)],
        micros=4,
    )[0]


def split_kernel(where, near, far, left, right):
    left[...] = near[...]
    right[...] = far[...]


def split(where, near, far):
    rows, columns = near.shape[0], near.shape[1] // 2
    return call(
        split_kernel,
        (1,),
        where,
        [first_columns(near, columns, 0), first_columns(far, columns, 1)],
        [whole_out((rows, columns), bf16)] * 2,
    )


def unpack_kernel(where, low, high, *refs):
    outs, true = refs[:-1], refs[-1]
    for side, part in enumerate((low, high)):
        turned = part[...].astype(f32).T
        for at in range(4):
            true[:, lanes(where, 4 * side + at)] = turned[:, at * 128 : (at + 1) * 128]
    share = 32
    first = 0
    for vector in outs:
        columns = vector.shape[1] // true.shape[1]
        if columns == 1:
            vector[...] = true[first : first + 1, :]
        else:
            for owner in range(true.shape[1] // share):
                for at in range(columns):
                    start = (owner * columns + at) * share
                    vector[:, start : start + share] = true[
                        first + at : first + at + 1, owner * share : (owner + 1) * share
                    ]
        first += columns


def unpack(where, mats, sizes):
    block = mats[0].shape[1] // 128 - 2
    outs = [whole_out((1, size), f32) for size in sizes]
    rows = mats[0].shape[0]
    return call(
        unpack_kernel,
        (1,),
        where,
        [(mat, (rows, 128), lambda *_: (0, block)) for mat in mats],
        outs,
        [pltpu.VMEM((128, 2 * rows), f32)],
    )


def exchanged(fsdp_size, block_in, keep_mask, out_cotangent, *params):
    (g1, b1, qkv_weight, qv_bias, out_weight, out_bias, g2, b2, up_weight, up_bias, down_weight, down_bias) = params
    seqs, length, width = block_in.shape
    rows = seqs * length
    half = width // 2
    order = Order()
    me, line = lax.axis_index("dp"), lax.axis_index("fsdp")
    where = positions(me, line, fsdp_size)

    def swap(value, bit):
        return lax.ppermute(value, "dp", [(i, i ^ bit) for i in range(8)])

    def along(value, by):
        return lax.ppermute(value, "fsdp", [(i, (i + by) % fsdp_size) for i in range(fsdp_size)])

    class Gather:
        def start(self, left, right):
            left, right = self.own = order.tie(left, right)
            self.near = swap(left, XBIT), swap(right, XBIT)
            self.far = swap(left, YBIT), swap(right, YBIT)

        def turn(self, *others):
            *pieces, = order.tie(*self.near, *self.far, *others)
            self.near, self.far = tuple(pieces[:2]), tuple(pieces[2:4])
            left, right = self.near[0], self.far[1]
            order.last = (left,)
            self.last = swap(left, YBIT), swap(right, XBIT)

        def start_whole(self, block):
            block = order.tie(block)[0]
            self.own = block
            self.near, self.far = swap(block, XBIT), swap(block, YBIT)

        def turn_whole(self, *others):
            left, right = order(lambda near, far, *_: split(where, near, far), self.near, self.far, *others)
            self.last = swap(left, YBIT), swap(right, XBIT)

        def join(self, *others):
            sides = [v if isinstance(v, tuple) else (v, v) for v in (self.own, self.near, self.far)]
            pieces = [p for side in zip(*sides, self.last) for p in side]
            self.low = order(lambda *p: join(where, *p[:8]), *pieces, *others)

        def joined(self):
            low = order.tie(self.low)[0]
            self.mats = low, swap(low, CORE)

    def around(shard):
        return [shard] + [along(shard, by) for by in range(fsdp_size - 1, 0, -1)]

    vectors = (g1, b1, qv_bias, out_bias, g2, b2, up_bias, down_bias)
    device_count = 8 * fsdp_size
    sizes = [v.shape[0] * device_count for v in vectors]
    cuts = [sum(v.shape[0] for v in vectors[:i]) for i in range(1, len(vectors))]
    share = qkv_weight.shape[0]
    beside = lax.optimization_barrier(jnp.concatenate(vectors)).reshape(-1, share).T
    beside = jnp.pad(beside, ((0, 0), (0, 256 - beside.shape[1])))
    qkv_low = jnp.concatenate([qkv_weight, beside], 1).astype(bf16)
    behind = jnp.stack([(line + by) % fsdp_size for by in range(fsdp_size)]).astype(jnp.int32)
    qkv_pieces = around(qkv_low)
    up_low = jnp.concatenate([up_weight, out_weight], 1).astype(bf16)
    down_block = lax.all_gather(down_weight.astype(bf16), "fsdp", axis=0, tiled=True)

    keep = jnp.concatenate(
        [jnp.ones((seqs, length - keep_mask.shape[1]), jnp.int32), keep_mask], axis=1
    )
    keep_rows = keep.reshape(rows, 1).astype(f32)
    keep_column = keep.reshape(seqs, length, 1)
    inputs = block_in.reshape(rows, width)
    grad_feed = order(
        lambda g: jnp.where(keep_rows > 0, g, jnp.zeros((), bf16)), out_cotangent.reshape(rows, width)
    )
    down_bias_grad = jnp.sum(grad_feed.astype(f32), 0)

    qkv, up, down = Gather(), Gather(), Gather()
    qkv.start_whole(order(functools.partial(assemble, 1, behind), *qkv_pieces)[0])
    up_pieces = around(order.tie(up_low)[0])
    qkv.turn_whole()
    up_halves = order(functools.partial(assemble, 2, behind), *up_pieces)
    qkv.join()
    qkv.joined()
    up.start(*up_halves)
    g1, b1, qv_bias, out_bias, g2, b2, up_bias, down_bias = order(
        lambda *m: unpack(where, m, sizes), *qkv.mats
    )
    one_low, one_pack = order(functools.partial(norm_one, where), inputs, grad_feed, g1, b1)
    shift = jnp.concatenate([qv_bias[:, :width], jnp.zeros((1, width), f32), qv_bias[:, width:]], 1)
    projected = order(
        lambda lo, hi, s, *m: project(where, lo, hi, m, s), one_low, one_pack, shift, *qkv.mats
    )
    mixed_left, probs_left = order(lambda p: attention_forward(keep_column, p, 0), projected)
    up.turn(down_block)
    one_other = swap(order.tie(one_pack)[0], CORE)
    mixed_right, probs_right = order(lambda p: attention_forward(keep_column, p, 1), projected)
    down_halves = order(lambda b: (b[:, :half], b[:, half:]), down_block)
    up.join(one_other)
    up.joined()
    down.start(*down_halves)
    mixed = jnp.concatenate([mixed_left, mixed_right], 1)
    mix_low, middle, two_low, two_pack = order(
        lambda m, o, *mats: branch_norm(where, m, inputs, mats, o, g2, b2, length),
        mixed, out_bias, *up.mats,
    )
    hidden_high, slope_high = order(
        lambda lo, hi, s, *m: expand(where, 1, lo, hi, m, s), two_low, two_pack, up_bias, *up.mats
    )
    hidden_low, slope_low = order(
        lambda lo, hi, s, *m: expand(where, 0, lo, hi, m, s), two_low, two_pack, up_bias, *up.mats
    )
    down.turn()
    hidden_other = swap(order.tie(hidden_high)[0], CORE)
    two_other = swap(order.tie(two_pack)[0], CORE)
    down_sum = Sum(
        swap, along, order, where,
        [((hidden_low, 0), (hidden_other, 0))], [((grad_feed, 0), (one_other, half // 256))],
        256, [width // 256], True,
    )
    down_sum.work()
    down.join()
    down.joined()
    down_sum.send()
    grad_pre, up_bias_grad = order(
        lambda g, s0, s1, *m: shrink(where, g, m, (s0, s1)),
        grad_feed, slope_low, slope_high, *down.mats,
    )
    down_sum.work()
    down_sum.send()
    pre_other = swap(order.tie(grad_pre)[0], CORE)
    grad_middle, grad_branch, out_bias_grad, gain_two_grad, bias_two_grad, grad_mixed = order(
        lambda g, mid, above, *m: back(where, g, m, mid, above, g2),
        grad_pre, middle, grad_feed, *up.mats,
    )
    branch, pre_other = order.tie(grad_branch, pre_other)
    branch_other = swap(branch, CORE)
    down_sum.work()
    up_sum = Sum(
        swap, along, order, where,
        [((two_low, 0), (two_other, 1)), ((mix_low, 0), (two_other, 0))],
        [((grad_pre, 0), (pre_other, 0)), ((grad_branch, 0), (branch_other, 0))],
        512, [grad_pre.shape[1] // 512, width // 512], True,
    )
    up_sum.work()
    up_sum.send()
    down_sum.send()
    grad_projected, sum_q, sum_v = order(
        lambda p, g, *probs: attention_backward(probs, p, g),
        projected, grad_mixed, probs_left, probs_right,
    )
    block_out = order(
        lambda lo, hi, mid, s, *m: feed(where, lo, hi, m, mid, s, keep_rows),
        hidden_low, hidden_high, middle, down_bias, *down.mats,
    )
    down_sum.meet()
    up_sum.work()
    up_sum.send()
    projected_other = swap(order.tie(grad_projected)[0], CORE)
    qkv_sum = Sum(
        swap, along, order, where,
        [((one_low, 0), (one_other, 0))], [((grad_projected, 0), (projected_other, 0))],
        512, [3 * width // 512],
    )
    qkv_sum.work()
    qkv_sum.send()
    up_sum.work()
    up_sum.send()
    sums = [
        jnp.concatenate([sum_q, sum_v], 1),
        out_bias_grad,
        gain_two_grad,
        bias_two_grad,
        up_bias_grad,
        down_bias_grad.reshape(1, -1),
    ]
    input_grad, shares = order(
        lambda g, x, above, m0, m1, *v: back(where, g, (m0, m1), x, above, g1, v, device_count),
        grad_projected, inputs, grad_middle, *qkv.mats, *sums,
    )
    qkv_sum.work()
    qkv_sum.send()
    shares = order.tie(shares.reshape(2, 2, 2, fsdp_size, -1))[0]

    def halve(shares, axis, bit):
        low, high = (lax.index_in_dim(shares, side, axis, keepdims=False) for side in range(2))
        upper = me & bit > 0
        return jnp.where(upper, high, low), jnp.where(upper, low, high)

    mine, other = halve(shares, 2, CORE)
    mine, other = halve(mine + swap(other, CORE), 1, XBIT)
    up_sum.meet()
    mine, other = order.tie(mine, other)
    order.last = (mine,)
    qkv_sum.work()
    qkv_sum.send((1, 2, 3))
    shares = mine + swap(order.tie(other)[0], XBIT)
    qkv_sum.shares[0], shares = order.tie(qkv_sum.shares[0], shares)
    order.last = (qkv_sum.shares[0],)
    mine, other = halve(shares, 0, YBIT)
    shares = mine + swap(other, YBIT)

    def row_of(by):
        return lax.dynamic_slice(shares, ((line + by) % fsdp_size, 0), (1, shares.shape[1]))

    line_shares = [along(row_of(by), by) for by in range(1, fsdp_size)]
    down_grad, up_grad = down_sum.total(), up_sum.total()
    up_grad, out_grad = up_grad[:, : up_weight.shape[1]], up_grad[:, up_weight.shape[1] :]
    qkv_grad = qkv_sum.total()
    mine = sum(line_shares, row_of(0))
    v = jnp.split(mine[0], cuts)
    return (
        block_out.reshape(seqs, length, width),
        input_grad.reshape(seqs, length, width),
        v[0],
        v[1],
        qkv_grad,
        v[2],
        out_grad,
        v[3],
        v[4],
        v[5],
        up_grad,
        v[6],
        down_grad,
        v[7],
    )


def solution(mesh):
    dp_size, fsdp_size = mesh.shape["dp"], mesh.shape["fsdp"]
    if dp_size == 8:
        local = functools.partial(exchanged, fsdp_size)
    else:
        local = functools.partial(gathered, dp_size * fsdp_size)
    row = P(AXES, None)
    vec = P(AXES)
    cube = P(AXES, None, None)
    return jax.shard_map(
        local,
        mesh=mesh,
        in_specs=(cube, row, cube, vec, vec, row, vec, row, vec, vec, vec, row, vec, row, vec),
        out_specs=(cube, cube, vec, vec, row, vec, row, vec, vec, vec, row, vec, row, vec),
        check_vma=False,
    )
```
